256 devices in a mesh: lat: 16 (over x, z_lo), wave: 8 (over y, core), lev: 2 (over z_hi).
Axes of the slice: x: 4, y: 4, z: 8 (z_hi: 2, z_lo: 4; z = z_hi * 4 + z_lo), core: 2. Of those that a mesh axis runs over, the one named last changes fastest.
Arguments:
- out_grad: bfloat16 [64, 1280, 2560], P('lev', 'lat', 'wave'), may hold values from -6 to 6
- grid_state: bfloat16 [64, 1280, 2560], P('lev', 'lat', 'wave'), may hold values from -4 to 4
- tend_rate: float32 [64], P('lev'), may hold values from 0.5 to 2
- legendre_basis: bfloat16 [1280, 640, 640], P('lat', 'wave'), may hold values from -0.15625 to 0.15625
- wave_slot: int32 [640], replicated, may hold values from 0 to 639, each once
Outputs:
- spectral_grad: float32 [640, 2, 64, 640], P('lat', None, 'lev', 'wave')
The draws below stay inside these ranges and needn't reach their ends.
Inputs may be any that keep to these rules, and one draw needn't show every extreme that they name: `wave_slot`: each wavenumber 0 to 639 occupies exactly one slot.
All inputs are finite; a program needn't handle non-finite values.
Results may differ from the reference program's by a relative error of at most 0.0051.
Values may be sent and summed in bfloat16 or wider, within the bound.
No kernel may reach another device: no remote copies, remote signals or barrier semaphores. Data moves between devices by JAX's collectives and lax.ppermute only.
A program may use at most 128 MiB of HBM per device.

```python
import math
import jax
import jax.numpy as jnp
from jax import lax

NLAT = 1280
NLON = 2560
M = 640
NDEG = 640
CHANNELS = 64


def levels(own_key, dims, shards, least, high):
    gain, own = 1.0, jax.random.fold_in(own_key, 6)
    for position, shards_of in shards:
        heights = jnp.exp(jax.random.uniform(jax.random.fold_in(own, position), (shards_of,), jnp.float32, least / len(shards), high / len(shards)))
        gain = gain * jnp.repeat(heights, dims[position] // shards_of).reshape([-1 if axis == position else 1 for axis in range(len(dims))])
    return gain


def normal_values(key, extent, width, reach, cuts=(), kind=jnp.bfloat16):
    values = width * jax.random.normal(key, extent, jnp.float32)
    if cuts:
        values = values * levels(key, extent, cuts, -0.22, 0.18)
    return jnp.clip(values, -reach, reach).astype(kind)


def setup_inputs(seed: int = 0) -> dict:
    key_list = jax.random.split(jax.random.key(seed), 6)
    return {
        "out_grad": normal_values(key_list[0], (CHANNELS, NLAT, NLON), 1.0, 6.0, ((0, 2), (1, 16), (2, 8))),
        "grid_state": normal_values(key_list[1], (CHANNELS, NLAT, NLON), 1.0, 4.0, ((0, 2), (1, 16), (2, 8))),
        "tend_rate": jnp.clip(jnp.exp(math.log(2.0) - 1.3862944 * jax.random.uniform(key_list[2], (CHANNELS,), jnp.float32) ** levels(key_list[2], (CHANNELS,), ((0, 2),), -0.2, 0.2)), 0.5, 2.0),
        "legendre_basis": normal_values(key_list[3], (NLAT, M, NDEG), NLAT ** -0.5, 0.15625, ((0, 16), (1, 8))),
        "wave_slot": jax.random.permutation(key_list[4], M).astype(jnp.int32),
    }


def wave_table(slots, lon_start, count, lon_total):
    lon = lon_start + jnp.arange(count, dtype=jnp.int32)
    index = slots[None, :] * lon[:, None] % lon_total
    angle = index.astype(jnp.float32) * (2.0 * math.pi / lon_total)
    scale = 1.0 / math.sqrt(lon_total)
    return (jnp.concatenate([jnp.cos(angle), -jnp.sin(angle)], 1) * scale).astype(jnp.bfloat16)

def reference(out_grad, grid_state, tend_rate, legendre_basis, wave_slot):
    slope = 1.0 - jnp.tanh(grid_state.astype(jnp.float32)) ** 2
    grid_grad = (out_grad.astype(jnp.float32) * (1.0 + tend_rate[:, None, None] * slope)).astype(jnp.bfloat16)
    table = wave_table(wave_slot, 0, NLON, NLON)
    flat = grid_grad.reshape(CHANNELS * NLAT, NLON)
    fourier = jnp.dot(flat, table, preferred_element_type=jnp.float32).astype(jnp.bfloat16)
    fourier = fourier.reshape(CHANNELS, NLAT, 2, M)

    def one_slot(slot):
        basis_rows = lax.dynamic_index_in_dim(legendre_basis, slot, 1, keepdims=False)
        column = lax.dynamic_index_in_dim(fourier, slot, 3, keepdims=False)
        column = column.transpose(1, 2, 0).reshape(NLAT, 2 * CHANNELS)
        result = jnp.dot(basis_rows.T, column, preferred_element_type=jnp.float32)
        return result.reshape(NDEG, 2, CHANNELS)
    stacked = lax.map(one_slot, jnp.arange(M, dtype=jnp.int32))
    spectral = stacked.transpose(1, 2, 3, 0)
    degree = jnp.arange(NDEG, dtype=jnp.int32)
    keep = (degree[:, None] >= wave_slot[None, :]).astype(jnp.float32)
    return spectral * keep[:, None, None, :]
```

```python
import functools
import math

import jax
import jax.numpy as jnp
from jax import lax
from jax.experimental import pallas as pl
from jax.experimental.pallas import tpu as pltpu
from jax.sharding import Mesh, PartitionSpec as P

VMEM = 48 * 1024 * 1024


def params():
    return pltpu.CompilerParams(vmem_limit_bytes=VMEM)


def cost(flops, moved, trans=0):
    return pl.CostEstimate(flops=flops, bytes_accessed=moved, transcendentals=trans)


def basis_kernel(where_ref, basis_ref, *refs):
    outs, rows = refs[:-1], refs[-1]
    lats, _, degs = basis_ref.shape
    block = basis_ref[...].astype(jnp.float32)
    half = jnp.where(where_ref[8] == 0, block[:, :8], block[:, 8:])
    for t in range(degs // 128):
        lanes = slice(128 * t, 128 * t + 128)
        rows[t] = half[:, :, lanes].reshape(lats * 8, 128)
        for j, out in enumerate(outs):
            out[0, :, lanes] = rows[t, pl.ds(where_ref[j], lats, stride=8), :].astype(jnp.bfloat16)


def basis_blocks(where, basis):
    lats, slots, degs = basis.shape
    steps = slots // 16
    return pl.pallas_call(
        basis_kernel,
        grid_spec=pltpu.PrefetchScalarGridSpec(
            num_scalar_prefetch=1,
            grid=(steps,),
            in_specs=[pl.BlockSpec((lats, 16, degs), lambda b, w: (0, b, 0))],
            out_specs=[pl.BlockSpec((1, lats, degs), lambda b, w: (b, 0, 0))] * 8,
            scratch_shapes=[pltpu.VMEM((degs // 128, lats * 8, 128), jnp.float32)],
        ),
        out_shape=[jax.ShapeDtypeStruct((steps, lats, degs), jnp.bfloat16)] * 8,
        compiler_params=params(),
        cost_estimate=cost(0, 3 * lats * slots * degs),
        name="basis_blocks",
    )(where, basis)


def grad_kernel(rate_ref, grad_ref, state_ref, out_ref):
    w = pl.program_id(0)
    lons = grad_ref.shape[-1]
    for c in range(4):
        slope = 1.0 - jnp.tanh(state_ref[c, 0].astype(jnp.float32)) ** 2
        value = grad_ref[c, 0].astype(jnp.float32) * (1.0 + rate_ref[8 * c + w] * slope)
        out_ref[0, c // 2, :, pl.ds((c % 2) * lons, lons)] = value.astype(jnp.bfloat16)


def gradient(rate, grad, state):
    chans, lats, lons = grad.shape
    four = (4, chans // 4, lats, lons)
    spec = pl.BlockSpec((4, 1, lats, lons), lambda w: (0, w, 0, 0))
    return pl.pallas_call(
        grad_kernel,
        grid=(8,),
        in_specs=[pl.BlockSpec(memory_space=pltpu.SMEM), spec, spec],
        out_specs=pl.BlockSpec((1, 2, lats, 2 * lons), lambda w: (w, 0, 0, 0)),
        out_shape=jax.ShapeDtypeStruct((8, 2, lats, 2 * lons), jnp.bfloat16),
        compiler_params=params(),
        cost_estimate=cost(6 * grad.size, 6 * grad.size, grad.size),
        name="gradient",
    )(rate, grad.reshape(four), state.reshape(four))


def table_kernel(coarse_cos, coarse_sin, fine_cos, fine_sin, out_ref):
    fine = fine_cos.shape[1]
    for j in range(coarse_cos.shape[1]):
        cos, sin = coarse_cos[:, j : j + 1], coarse_sin[:, j : j + 1]
        lanes = slice(j * fine, (j + 1) * fine)
        out_ref[0, :, lanes] = (cos * fine_cos[...] - sin * fine_sin[...]).astype(jnp.bfloat16)
        out_ref[1, :, lanes] = (-sin * fine_cos[...] - cos * fine_sin[...]).astype(jnp.bfloat16)


def wave_table(slots, lon_total, fine):
    def trig(lon):
        index = slots[:, None] * lon[None, :] % lon_total
        angle = index.astype(jnp.float32) * (2.0 * math.pi / lon_total)
        return jnp.cos(angle), jnp.sin(angle)

    coarse_cos, coarse_sin = trig(fine * jnp.arange(lon_total // fine, dtype=jnp.int32))
    fine_cos, fine_sin = trig(jnp.arange(fine, dtype=jnp.int32))
    scale = 1.0 / math.sqrt(lon_total)
    count, block = slots.shape[0], 128
    coarse_spec = pl.BlockSpec((block, lon_total // fine), lambda s: (s, 0))
    fine_spec = pl.BlockSpec((block, fine), lambda s: (s, 0))
    return pl.pallas_call(
        table_kernel,
        grid=(count // block,),
        in_specs=[coarse_spec, coarse_spec, fine_spec, fine_spec],
        out_specs=pl.BlockSpec((2, block, lon_total), lambda s: (0, s, 0)),
        out_shape=jax.ShapeDtypeStruct((2, count, lon_total), jnp.bfloat16),
        compiler_params=params(),
        cost_estimate=cost(6 * count * lon_total, 4 * count * lon_total),
        name="wave_table",
    )(coarse_cos * scale, coarse_sin * scale, fine_cos, fine_sin)


def fourier_kernel(grad_ref, table_ref, out_ref, rows):
    lats, lons = grad_ref.shape[2], grad_ref.shape[3] // 2

    @pl.when(pl.program_id(0) == 0)
    def _():
        for w in range(8):
            for c in range(4):
                rows[pl.ds(c * lats, lats), pl.ds(w * lons, lons)] = grad_ref[
                    w, c // 2, :, pl.ds((c % 2) * lons, lons)
                ]

    width = 4 * lats
    for p in range(2):
        value = lax.dot_general(
            table_ref[p], rows[...], (((1,), (1,)), ((), ())), preferred_element_type=jnp.float32
        )
        out_ref[:, pl.ds(p * width, width)] = value.astype(jnp.bfloat16)


def fourier_rows(grad, table):
    _, _, lats, lons2 = grad.shape
    slots, lon_total = table.shape[1:]
    block = 128
    return pl.pallas_call(
        fourier_kernel,
        grid=(slots // block,),
        in_specs=[
            pl.BlockSpec(grad.shape, lambda s: (0, 0, 0, 0)),
            pl.BlockSpec((2, block, lon_total), lambda s: (0, s, 0)),
        ],
        out_specs=pl.BlockSpec((block, 8 * lats), lambda s: (s, 0)),
        out_shape=jax.ShapeDtypeStruct((slots, 8 * lats), jnp.bfloat16),
        scratch_shapes=[pltpu.VMEM((4 * lats, lon_total), jnp.bfloat16)],
        compiler_params=params(),
        cost_estimate=cost(2 * 2 * slots * lon_total * 4 * lats, 2 * (grad.size + table.size)),
        name="fourier_rows",
    )(grad, table)


def turn_kernel(in_ref, out_ref, rows):
    waves, slots, width = in_ref.shape
    for t in range(width // 128):
        lanes = slice(128 * t, 128 * t + 128)
        rows[t] = in_ref[:, :, lanes].astype(jnp.float32).reshape(waves * slots, 128)
        for s in range(slots):
            b, lev, r = s // 16, s // 8 % 2, s % 8
            out_ref[2 * r + lev, b, :, lanes] = rows[t, pl.ds(s, waves, stride=slots), :].astype(
                jnp.bfloat16
            )


def turn(fourier):
    waves, slots, width = fourier.shape
    return pl.pallas_call(
        turn_kernel,
        out_shape=jax.ShapeDtypeStruct((16, slots // 16, waves, width), jnp.bfloat16),
        scratch_shapes=[pltpu.VMEM((width // 128, waves * slots, 128), jnp.float32)],
        compiler_params=params(),
        cost_estimate=cost(0, 4 * fourier.size),
        name="turn",
    )(fourier)


def spectral_kernel(where_ref, slot_ref, four_ref, *refs):
    bases, out_ref, left, total = refs[:8], refs[8], refs[9], refs[10]
    lats, degs = bases[0].shape[1:]
    deg_dev = degs // 16
    degree = lax.broadcasted_iota(jnp.int32, (128, degs), 1)

    def summed(b):
        for j in range(8):
            source = where_ref[8 + j]
            for lev in range(2):
                block = four_ref[2 * source + lev, b].astype(jnp.float32)
                for seg in range(8):
                    left[pl.ds(64 * lev + 8 * seg, 8), pl.ds(j * lats, lats)] = block[
                        :, seg * lats : (seg + 1) * lats
                    ]
        basis = jnp.concatenate([ref[b] for ref in bases], 0)
        value = jnp.dot(
            left[...].astype(jnp.bfloat16), basis, preferred_element_type=jnp.float32
        )
        return jnp.where(degree >= slot_ref[b], value, 0.0)

    for k in range(2):
        even, odd = summed(2 * k), summed(2 * k + 1)
        for lev in range(2):
            both = jnp.concatenate([even[64 * lev :][:64], odd[64 * lev :][:64]], 0).T
            for a in range(16):
                out_ref[2 * a + lev, pl.ds(k * deg_dev, deg_dev)] = both[
                    a * deg_dev : (a + 1) * deg_dev
                ].astype(jnp.bfloat16)
    total[...] = summed(4).T
    even = total[pl.ds(0, degs // 2, stride=2), :]
    odd = total[pl.ds(1, degs // 2, stride=2), :]
    low = lax.broadcasted_iota(jnp.int32, even.shape, 1) < 64
    for lev in range(2):
        if lev == 0:
            both = jnp.where(low, even, pltpu.roll(odd, 64, 1))
        else:
            both = jnp.where(low, pltpu.roll(even, 64, 1), odd)
        for a in range(16):
            out_ref[2 * a + lev, pl.ds(2 * deg_dev, deg_dev // 2)] = both[
                a * (deg_dev // 2) : (a + 1) * (deg_dev // 2)
            ].astype(jnp.bfloat16)
    rows = 5 * deg_dev // 2
    if out_ref.shape[1] > rows:
        for a in range(32):
            out_ref[a, pl.ds(rows, out_ref.shape[1] - rows)] = jnp.zeros(
                (out_ref.shape[1] - rows, 128), jnp.bfloat16
            )


def spectral_parts(where, slots, fourier, bases):
    _, lats, degs = bases[0].shape
    smem = pl.BlockSpec(memory_space=pltpu.SMEM)
    return pl.pallas_call(
        spectral_kernel,
        in_specs=[smem, smem] + [pl.BlockSpec(memory_space=pltpu.VMEM)] * 9,
        out_shape=jax.ShapeDtypeStruct((32, 104, 128), jnp.bfloat16),
        scratch_shapes=[
            pltpu.VMEM((128, 8 * lats), jnp.float32),
            pltpu.VMEM((degs, 128), jnp.float32),
        ],
        compiler_params=params(),
        cost_estimate=cost(5 * 2 * 128 * 8 * lats * degs, 16 * bases[0].size + 2 * fourier.size),
        name="spectral_parts",
    )(where, slots, fourier, *bases)


def finish_kernel(in_ref, out_ref, rows):
    depth = in_ref.shape[1]
    for x in range(4):
        for zq in range(2):
            for lev in range(2):
                first = in_ref[8 * x + 2 * zq + lev].astype(jnp.float32)
                second = in_ref[8 * x + 4 + 2 * zq + lev].astype(jnp.float32)
                rows[pl.ds((8 * lev + 2 * x + zq) * depth, depth), :] = first + second
    low = lax.broadcasted_iota(jnp.int32, (16, 128), 1) < 64
    for n in range(0, 40, 2):
        parts = []
        for k in range(2):
            one = rows[pl.ds(40 * k + n, 16, stride=depth), :]
            two = rows[pl.ds(40 * k + n + 1, 16, stride=depth), :]
            parts.append(jnp.where(low, one, pltpu.roll(two, 64, 1)))
            parts.append(jnp.where(low, pltpu.roll(one, 64, 1), two))
        parts.append(rows[pl.ds(80 + n // 2, 16, stride=depth), :])
        out_ref[pl.ds(64 * n, 128), :] = jnp.concatenate(parts, 0).T


def finish(received):
    return pl.pallas_call(
        finish_kernel,
        out_shape=jax.ShapeDtypeStruct((40 * 64, 80), jnp.float32),
        scratch_shapes=[pltpu.VMEM((16 * received.shape[1], 128), jnp.float32)],
        compiler_params=params(),
        cost_estimate=cost(received.size, 2 * received.size + 4 * 40 * 64 * 128),
        name="finish",
    )(received)


def local(out_grad, grid_state, tend_rate, legendre_basis, wave_slot):
    lats, lons = out_grad.shape[1:]
    slot_dev, degs = legendre_basis.shape[1:]
    x, zq = lax.axis_index("x"), lax.axis_index("zq")
    wave, lev = lax.axis_index("wave"), lax.axis_index("lev")
    offsets = [(dx, dz) for dx in range(4) for dz in range(2)]
    to = [(x + dx) % 4 * 2 + (zq + dz) % 2 for dx, dz in offsets]
    source = [(x - dx) % 4 * 2 + (zq - dz) % 2 for dx, dz in offsets]
    where = jnp.stack(to + [lev]).astype(jnp.int32)
    sources = jnp.stack(to + source).astype(jnp.int32)

    grad = gradient(tend_rate, out_grad, grid_state)
    grad = lax.all_to_all(grad, "wave", 0, 0)

    blocks = basis_blocks(where, legendre_basis)
    bases = [blocks[0]]
    for (dx, dz), block in list(zip(offsets, blocks))[1:]:
        pairs = [
            (2 * a + b, 2 * ((a + dx) % 4) + (b + dz) % 2) for a in range(4) for b in range(2)
        ]
        bases.append(lax.ppermute(block, ("x", "zq"), pairs))

    table = wave_table(wave_slot, lons * 8, 128)
    fourier = fourier_rows(grad, table)
    fourier = lax.all_to_all(fourier.reshape(8, slot_dev, 8 * lats), "wave", 0, 0)
    fourier = lax.all_to_all(turn(fourier), ("x", "zq", "lev"), 0, 0, tiled=True)

    first = wave * slot_dev + 8 * lev + 2 * x + zq
    slots = jnp.take(wave_slot, first + 16 * jnp.arange(slot_dev // 16, dtype=jnp.int32))
    parts = spectral_parts(sources, slots, fourier, bases)
    parts = lax.all_to_all(parts, ("x", "zp", "zq", "lev"), 0, 0, tiled=True)
    return finish(parts).reshape(degs // 16, 2, 32, slot_dev)


def solution(mesh):
    fine = Mesh(
        mesh.devices.reshape(4, 2, 2, *mesh.devices.shape[1:]), ("x", "zp", "zq", "wave", "lev")
    )
    lat = ("x", "zp", "zq")
    in_specs = (P("lev", lat, "wave"), P("lev", lat, "wave"), P("lev"), P(lat, "wave", None), P())
    out_specs = P(lat, None, "lev", "wave")
    return jax.shard_map(local, mesh=fine, in_specs=in_specs, out_specs=out_specs, check_vma=False)
```

```python
import functools
import math

import jax
import jax.numpy as jnp
from jax import lax
from jax.experimental import pallas as pl
from jax.experimental.pallas import tpu as pltpu
from jax.sharding import Mesh, PartitionSpec as P

VMEM = 48 * 1024 * 1024


def params():
    return pltpu.CompilerParams(vmem_limit_bytes=VMEM)


def cost(flops, moved, trans=0):
    return pl.CostEstimate(flops=flops, bytes_accessed=moved, transcendentals=trans)


def basis_kernel(where_ref, basis_ref, *refs):
    outs, rows = refs[:-1], refs[-1]
    lats, _, degs = basis_ref.shape
    block = basis_ref[...].astype(jnp.float32)
    half = jnp.where(where_ref[8] == 0, block[:, :8], block[:, 8:])
    for t in range(degs // 128):
        lanes = slice(128 * t, 128 * t + 128)
        rows[t] = half[:, :, lanes].reshape(lats * 8, 128)
        for j, out in enumerate(outs):
            out[0, :, lanes] = rows[t, pl.ds(where_ref[j], lats, stride=8), :].astype(jnp.bfloat16)


def basis_blocks(where, basis):
    lats, slots, degs = basis.shape
    steps = slots // 16
    return pl.pallas_call(
        basis_kernel,
        grid_spec=pltpu.PrefetchScalarGridSpec(
            num_scalar_prefetch=1,
            grid=(steps,),
            in_specs=[pl.BlockSpec((lats, 16, degs), lambda b, w: (0, b, 0))],
            out_specs=[pl.BlockSpec((1, lats, degs), lambda b, w: (b, 0, 0))] * 8,
            scratch_shapes=[pltpu.VMEM((degs // 128, lats * 8, 128), jnp.float32)],
        ),
        out_shape=[jax.ShapeDtypeStruct((steps, lats, degs), jnp.bfloat16)] * 8,
        compiler_params=params(),
        cost_estimate=cost(0, 3 * lats * slots * degs),
        name="basis_blocks",
    )(where, basis)


def grad_kernel(rate_ref, grad_ref, state_ref, out_ref):
    lons, waves = grad_ref.shape[-1], grad_ref.shape[1]
    for v in range(waves):
        w = pl.program_id(0) * waves + v
        for c in range(4):
            slope = 1.0 - jnp.tanh(state_ref[c, v].astype(jnp.float32)) ** 2
            value = grad_ref[c, v].astype(jnp.float32) * (1.0 + rate_ref[8 * c + w] * slope)
            out_ref[v, c // 2, :, pl.ds((c % 2) * lons, lons)] = value.astype(jnp.bfloat16)


def gradient(rate, grad, state):
    chans, lats, lons = grad.shape
    four = (4, chans // 4, lats, lons)
    spec = pl.BlockSpec((4, 2, lats, lons), lambda w: (0, w, 0, 0))
    return pl.pallas_call(
        grad_kernel,
        grid=(4,),
        in_specs=[pl.BlockSpec(memory_space=pltpu.SMEM), spec, spec],
        out_specs=pl.BlockSpec((2, 2, lats, 2 * lons), lambda w: (w, 0, 0, 0)),
        out_shape=jax.ShapeDtypeStruct((8, 2, lats, 2 * lons), jnp.bfloat16),
        compiler_params=pltpu.CompilerParams(vmem_limit_bytes=60 * 1024 * 1024),
        cost_estimate=cost(6 * grad.size, 6 * grad.size, grad.size),
        name="gradient",
    )(rate, grad.reshape(four), state.reshape(four))


def table_kernel(coarse_cos, coarse_sin, fine_cos, fine_sin, out_ref):
    fine = fine_cos.shape[0]
    count = fine_cos.shape[1]
    step = out_ref.shape[0] // fine
    for v in range(step):
        j = pl.program_id(0) * step + v
        cos, sin = coarse_cos[pl.ds(j, 1), :], coarse_sin[pl.ds(j, 1), :]
        rows = slice(v * fine, (v + 1) * fine)
        out_ref[rows, :count] = (cos * fine_cos[...] - sin * fine_sin[...]).astype(jnp.bfloat16)
        out_ref[rows, count:] = (-sin * fine_cos[...] - cos * fine_sin[...]).astype(jnp.bfloat16)


def wave_table(slots, lon_total, fine):
    def trig(lon):
        index = slots[None, :] * lon[:, None] % lon_total
        angle = index.astype(jnp.float32) * (2.0 * math.pi / lon_total)
        return jnp.cos(angle), jnp.sin(angle)

    coarse_cos, coarse_sin = trig(fine * jnp.arange(lon_total // fine, dtype=jnp.int32))
    fine_cos, fine_sin = trig(jnp.arange(fine, dtype=jnp.int32))
    scale = 1.0 / math.sqrt(lon_total)
    count, steps = slots.shape[0], 5
    whole = lambda a: pl.BlockSpec(a.shape, lambda j: (0, 0))
    return pl.pallas_call(
        table_kernel,
        grid=(steps,),
        in_specs=[whole(a) for a in (coarse_cos, coarse_sin, fine_cos, fine_sin)],
        out_specs=pl.BlockSpec((lon_total // steps, 2 * count), lambda j: (j, 0)),
        out_shape=jax.ShapeDtypeStruct((lon_total, 2 * count), jnp.bfloat16),
        compiler_params=params(),
        cost_estimate=cost(6 * count * lon_total, 4 * count * lon_total),
        name="wave_table",
    )(coarse_cos * scale, coarse_sin * scale, fine_cos, fine_sin)


def fourier_kernel(grad_ref, table_ref, *refs):
    out_ref, rows = refs[-2:]
    lats, lons = grad_ref.shape[2], grad_ref.shape[3] // 2
    for w in range(8):
        for c in range(4):
            rows[pl.ds(c * lats, lats), pl.ds(w * lons, lons)] = grad_ref[
                w, c // 2, :, pl.ds((c % 2) * lons, lons)
            ]
    width, slots = 4 * lats, out_ref.shape[0]
    for t in range(2 * slots // 256):
        value = jnp.dot(
            rows[...], table_ref[:, 256 * t : 256 * t + 256], preferred_element_type=jnp.float32
        ).T
        for part in range(2):
            p, first = divmod(256 * t + 128 * part, slots)
            out_ref[pl.ds(first, 128), pl.ds(p * width, width)] = value[
                128 * part : 128 * part + 128
            ].astype(jnp.bfloat16)


def fourier_rows(grad, table, early):
    _, _, lats, lons2 = grad.shape
    lon_total, slots = table.shape[0], table.shape[1] // 2
    vmem = pl.BlockSpec(memory_space=pltpu.VMEM)
    return pl.pallas_call(
        fourier_kernel,
        in_specs=[vmem, vmem] + [pl.BlockSpec(memory_space=pl.ANY)] * len(early),
        out_shape=jax.ShapeDtypeStruct((slots, 8 * lats), jnp.bfloat16),
        scratch_shapes=[pltpu.VMEM((4 * lats, lon_total), jnp.bfloat16)],
        compiler_params=params(),
        cost_estimate=cost(2 * 2 * slots * lon_total * 4 * lats, 2 * (grad.size + table.size)),
        name="fourier_rows",
    )(grad, table, *early)


def turn_kernel(in_ref, *refs):
    out_ref, rows = refs[-2:]
    waves, slots, width = in_ref.shape
    for t in range(width // 128):
        lanes = slice(128 * t, 128 * t + 128)
        rows[t] = in_ref[:, :, lanes].astype(jnp.float32).reshape(waves * slots, 128)
        for s in range(slots):
            b, lev, r = s // 16, s // 8 % 2, s % 8
            out_ref[2 * r + lev, b, :, lanes] = rows[t, pl.ds(s, waves, stride=slots), :].astype(
                jnp.bfloat16
            )


def turn(fourier, early):
    waves, slots, width = fourier.shape
    return pl.pallas_call(
        turn_kernel,
        in_specs=[pl.BlockSpec(memory_space=pltpu.VMEM)]
        + [pl.BlockSpec(memory_space=pl.ANY)] * len(early),
        out_shape=jax.ShapeDtypeStruct((16, slots // 16, waves, width), jnp.bfloat16),
        scratch_shapes=[pltpu.VMEM((width // 128, waves * slots, 128), jnp.float32)],
        compiler_params=params(),
        cost_estimate=cost(0, 4 * fourier.size),
        name="turn",
    )(fourier, *early)


def spectral_kernel(where_ref, slot_ref, four_ref, *refs):
    bases, out_ref, left, total = refs[:8], refs[8], refs[9], refs[10]
    lats, degs = bases[0].shape[1:]
    deg_dev = degs // 16
    degree = lax.broadcasted_iota(jnp.int32, (128, degs), 1)

    def summed(b):
        for j in range(8):
            source = where_ref[8 + j]
            for lev in range(2):
                block = four_ref[2 * source + lev, b].astype(jnp.float32)
                for seg in range(8):
                    left[pl.ds(64 * lev + 8 * seg, 8), pl.ds(j * lats, lats)] = block[
                        :, seg * lats : (seg + 1) * lats
                    ]
        basis = jnp.concatenate([ref[b] for ref in bases], 0)
        value = jnp.dot(
            left[...].astype(jnp.bfloat16), basis, preferred_element_type=jnp.float32
        )
        return jnp.where(degree >= slot_ref[b], value, 0.0)

    for k in range(2):
        even, odd = summed(2 * k), summed(2 * k + 1)
        for lev in range(2):
            both = jnp.concatenate([even[64 * lev :][:64], odd[64 * lev :][:64]], 0).T
            for a in range(16):
                out_ref[2 * a + lev, pl.ds(k * deg_dev, deg_dev)] = both[
                    a * deg_dev : (a + 1) * deg_dev
                ].astype(jnp.bfloat16)
    total[...] = summed(4).T
    even = total[pl.ds(0, degs // 2, stride=2), :]
    odd = total[pl.ds(1, degs // 2, stride=2), :]
    low = lax.broadcasted_iota(jnp.int32, even.shape, 1) < 64
    for lev in range(2):
        if lev == 0:
            both = jnp.where(low, even, pltpu.roll(odd, 64, 1))
        else:
            both = jnp.where(low, pltpu.roll(even, 64, 1), odd)
        for a in range(16):
            out_ref[2 * a + lev, pl.ds(2 * deg_dev, deg_dev // 2)] = both[
                a * (deg_dev // 2) : (a + 1) * (deg_dev // 2)
            ].astype(jnp.bfloat16)
    rows = 5 * deg_dev // 2
    if out_ref.shape[1] > rows:
        for a in range(32):
            out_ref[a, pl.ds(rows, out_ref.shape[1] - rows)] = jnp.zeros(
                (out_ref.shape[1] - rows, 128), jnp.bfloat16
            )


def spectral_parts(where, slots, fourier, bases):
    _, lats, degs = bases[0].shape
    smem = pl.BlockSpec(memory_space=pltpu.SMEM)
    return pl.pallas_call(
        spectral_kernel,
        in_specs=[smem, smem] + [pl.BlockSpec(memory_space=pltpu.VMEM)] * 9,
        out_shape=jax.ShapeDtypeStruct((32, 104, 128), jnp.bfloat16),
        scratch_shapes=[
            pltpu.VMEM((128, 8 * lats), jnp.float32),
            pltpu.VMEM((degs, 128), jnp.float32),
        ],
        compiler_params=params(),
        cost_estimate=cost(5 * 2 * 128 * 8 * lats * degs, 16 * bases[0].size + 2 * fourier.size),
        name="spectral_parts",
    )(where, slots, fourier, *bases)


def finish_kernel(in_ref, out_ref, rows):
    depth = in_ref.shape[1]
    for x in range(4):
        for zq in range(2):
            for lev in range(2):
                first = in_ref[8 * x + 2 * zq + lev].astype(jnp.float32)
                second = in_ref[8 * x + 4 + 2 * zq + lev].astype(jnp.float32)
                rows[pl.ds((8 * lev + 2 * x + zq) * depth, depth), :] = first + second
    low = lax.broadcasted_iota(jnp.int32, (16, 128), 1) < 64
    for n in range(0, 40, 2):
        parts = []
        for k in range(2):
            one = rows[pl.ds(40 * k + n, 16, stride=depth), :]
            two = rows[pl.ds(40 * k + n + 1, 16, stride=depth), :]
            parts.append(jnp.where(low, one, pltpu.roll(two, 64, 1)))
            parts.append(jnp.where(low, pltpu.roll(one, 64, 1), two))
        parts.append(rows[pl.ds(80 + n // 2, 16, stride=depth), :])
        out_ref[pl.ds(64 * n, 128), :] = jnp.concatenate(parts, 0).T


def finish(received):
    return pl.pallas_call(
        finish_kernel,
        out_shape=jax.ShapeDtypeStruct((40 * 64, 80), jnp.float32),
        scratch_shapes=[pltpu.VMEM((16 * received.shape[1], 128), jnp.float32)],
        compiler_params=params(),
        cost_estimate=cost(received.size, 2 * received.size + 4 * 40 * 64 * 128),
        name="finish",
    )(received)


def local(out_grad, grid_state, tend_rate, legendre_basis, wave_slot):
    lats, lons = out_grad.shape[1:]
    slot_dev, degs = legendre_basis.shape[1:]
    x, zq = lax.axis_index("x"), lax.axis_index("zq")
    wave, lev = lax.axis_index("wave"), lax.axis_index("lev")
    offsets = [(dx, dz) for dx in range(4) for dz in range(2)]
    to = [(x + dx) % 4 * 2 + (zq + dz) % 2 for dx, dz in offsets]
    source = [(x - dx) % 4 * 2 + (zq - dz) % 2 for dx, dz in offsets]
    where = jnp.stack(to + [lev]).astype(jnp.int32)
    sources = jnp.stack(to + source).astype(jnp.int32)

    grad = gradient(tend_rate, out_grad, grid_state)
    grad = lax.all_to_all(grad, "wave", 0, 0)

    blocks = basis_blocks(where, legendre_basis)
    bases = [blocks[0]]
    for (dx, dz), block in list(zip(offsets, blocks))[1:]:
        pairs = [
            (2 * a + b, 2 * ((a + dx) % 4) + (b + dz) % 2) for a in range(4) for b in range(2)
        ]
        bases.append(lax.ppermute(block, ("x", "zq"), pairs))

    by = dict(zip(offsets, bases))
    table = wave_table(wave_slot, lons * 8, 128)
    fourier = fourier_rows(grad, table, [by[0, 1], by[1, 0], by[3, 0]])
    fourier = lax.all_to_all(fourier.reshape(8, slot_dev, 8 * lats), "wave", 0, 0)
    fourier = lax.all_to_all(turn(fourier, [by[1, 1], by[2, 0], by[3, 1], by[2, 1]]), ("x", "zq", "lev"), 0, 0, tiled=True)

    first = wave * slot_dev + 8 * lev + 2 * x + zq
    slots = jnp.take(wave_slot, first + 16 * jnp.arange(slot_dev // 16, dtype=jnp.int32))
    parts = spectral_parts(sources, slots, fourier, bases)
    parts = lax.all_to_all(parts, ("x", "zp", "zq", "lev"), 0, 0, tiled=True)
    return finish(parts).reshape(degs // 16, 2, 32, slot_dev)


def solution(mesh):
    fine = Mesh(
        mesh.devices.reshape(4, 2, 2, *mesh.devices.shape[1:]), ("x", "zp", "zq", "wave", "lev")
    )
    lat = ("x", "zp", "zq")
    in_specs = (P("lev", lat, "wave"), P("lev", lat, "wave"), P("lev"), P(lat, "wave", None), P())
    out_specs = P(lat, None, "lev", "wave")
    return jax.shard_map(local, mesh=fine, in_specs=in_specs, out_specs=out_specs, check_vma=False)
```

```python
import math

import jax
import jax.numpy as jnp
from jax import lax
from jax.experimental import pallas as pl
from jax.experimental.pallas import tpu as pltpu
from jax.sharding import Mesh, PartitionSpec as P

def params(mib):
    return pltpu.CompilerParams(vmem_limit_bytes=mib * 1024 * 1024)


def cost(flops, moved, trans=0):
    return pl.CostEstimate(flops=flops, bytes_accessed=moved, transcendentals=trans)


def basis_kernel(lev_ref, basis_ref, out_ref):
    lats, _, degs = basis_ref.shape
    row = lax.broadcasted_iota(jnp.int32, (128, 128), 0)
    col = lax.broadcasted_iota(jnp.int32, (128, 128), 1)
    swap = (col == row % 16 * 8 + row // 16).astype(jnp.bfloat16)
    for g in range(lats // 16):
        block = basis_ref[16 * g : 16 * g + 16].astype(jnp.float32).reshape(128, degs)
        turned = jnp.dot(swap, block.astype(jnp.bfloat16), preferred_element_type=jnp.float32)
        out_ref[:, 0, 16 * g : 16 * g + 16, :] = turned.astype(jnp.bfloat16).reshape(8, 16, degs)


def basis_blocks(lev, basis):
    lats, slots, degs = basis.shape
    steps = slots // 16
    return pl.pallas_call(
        basis_kernel,
        grid_spec=pltpu.PrefetchScalarGridSpec(
            num_scalar_prefetch=1,
            grid=(steps,),
            in_specs=[pl.BlockSpec((lats, 8, degs), lambda b, lev: (0, 2 * b + lev[0], 0))],
            out_specs=pl.BlockSpec((8, 1, lats, degs), lambda b, lev: (0, b, 0, 0)),
        ),
        out_shape=jax.ShapeDtypeStruct((8, steps, lats, degs), jnp.bfloat16),
        compiler_params=params(60),
        cost_estimate=cost(0, 2 * lats * slots * degs),
        name="basis_blocks",
    )(lev, basis)


def grad_kernel(wave_ref, rate_ref, grad_hbm, state_hbm, _, *refs):
    outs, (grad_buf, state_buf, sems) = refs[:8], refs[8:]
    lons = grad_hbm.shape[-1]
    copies = []
    for k in range(8):
        to = wave_ref[k]
        copies.append(pltpu.make_async_copy(grad_hbm.at[:, to], grad_buf.at[k], sems.at[0, k]))
        copies.append(pltpu.make_async_copy(state_hbm.at[:, to], state_buf.at[k], sems.at[1, k]))
    for copy in copies:
        copy.start()
    for k in range(8):
        copies[2 * k].wait()
        copies[2 * k + 1].wait()
        for c in range(4):
            slope = 1.0 - jnp.tanh(state_buf[k, c].astype(jnp.float32)) ** 2
            rate = rate_ref[8 * c + wave_ref[k]]
            value = grad_buf[k, c].astype(jnp.float32) * (1.0 + rate * slope)
            outs[k][c // 2, :, pl.ds((c % 2) * lons, lons)] = value.astype(jnp.bfloat16)


def gradient(to, rate, grad, state, after):
    chans, lats, lons = grad.shape
    four = (4, chans // 4, lats, lons)
    smem, hbm = pl.BlockSpec(memory_space=pltpu.SMEM), pl.BlockSpec(memory_space=pltpu.HBM)
    buffer = pltpu.VMEM((8, 4, lats, lons), jnp.bfloat16)
    return pl.pallas_call(
        grad_kernel,
        in_specs=[smem, smem, hbm, hbm, pl.BlockSpec(memory_space=pl.ANY)],
        out_shape=[jax.ShapeDtypeStruct((2, lats, 2 * lons), jnp.bfloat16)] * 8,
        scratch_shapes=[buffer, buffer, pltpu.SemaphoreType.DMA((2, 8))],
        compiler_params=params(12),
        cost_estimate=cost(6 * grad.size, 6 * grad.size, grad.size),
        name="gradient",
    )(to, rate, grad.reshape(four), state.reshape(four), after)


def table_kernel(coarse_cos, coarse_sin, fine_cos, fine_sin, out_ref):
    fine = fine_cos.shape[0]
    for j in range(coarse_cos.shape[0]):
        cos, sin = coarse_cos[j : j + 1, :], coarse_sin[j : j + 1, :]
        out_ref[0, j * fine : (j + 1) * fine, :] = (
            cos * fine_cos[...] - sin * fine_sin[...]
        ).astype(jnp.bfloat16)


def wave_table(slots, blocks, lons, fine):
    lon_total = 8 * lons
    quarter = jnp.array([0, lon_total // 4], jnp.int32)[None, :, None]
    phase = jnp.broadcast_to(quarter, (8, 2, slots.shape[1])).reshape(1, -1)
    slot = jnp.broadcast_to(slots[:, None, :], (8, 2, slots.shape[1])).reshape(1, -1)

    def trig(lon, shift):
        index = (slot * lon[:, None] + shift) % lon_total
        angle = index.astype(jnp.float32) * (2.0 * math.pi / lon_total)
        return jnp.cos(angle), jnp.sin(angle)

    starts = blocks[:, None] * lons + fine * jnp.arange(lons // fine, dtype=jnp.int32)[None, :]
    coarse_cos, coarse_sin = trig(starts.reshape(-1), 0)
    fine_cos, fine_sin = trig(jnp.arange(fine, dtype=jnp.int32), phase)
    scale = 1.0 / math.sqrt(lon_total)
    columns = slot.shape[1]
    part = lambda a: pl.BlockSpec((a.shape[0], 256), lambda j: (0, j))
    return pl.pallas_call(
        table_kernel,
        grid=(columns // 256,),
        in_specs=[part(a) for a in (coarse_cos, coarse_sin, fine_cos, fine_sin)],
        out_specs=pl.BlockSpec((1, lon_total, 256), lambda j: (j, 0, 0)),
        out_shape=jax.ShapeDtypeStruct((columns // 256, lon_total, 256), jnp.bfloat16),
        compiler_params=params(12),
        cost_estimate=cost(3 * columns * lon_total, 2 * columns * lon_total),
        name="wave_table",
    )(coarse_cos * scale, coarse_sin * scale, fine_cos, fine_sin)


def fourier_kernel(table_ref, *refs):
    grads, outs, rows = refs[:8], refs[8:16], refs[16]
    lats, lons = grads[0].shape[1], grads[0].shape[2] // 2
    for k in range(8):
        for c in range(4):
            rows[pl.ds(c * lats, lats), pl.ds(k * lons, lons)] = grads[k][
                c // 2, :, pl.ds((c % 2) * lons, lons)
            ]
    width, slots = 4 * lats, outs[0].shape[0]
    for step in range(16 * slots // 256):
        value = jnp.dot(rows[...], table_ref[step], preferred_element_type=jnp.float32).T
        first, stop = 256 * step, 256 * step + 256
        for kp in range(first // slots, -(-stop // slots)):
            low, high = max(first, kp * slots), min(stop, (kp + 1) * slots)
            outs[kp // 2][low - kp * slots : high - kp * slots, pl.ds(kp % 2 * width, width)] = (
                value[low - first : high - first].astype(jnp.bfloat16)
            )


def fourier_rows(table, grads):
    _, lats, lons2 = grads[0].shape
    steps, lon_total, _ = table.shape
    slots = steps * 256 // 16
    return pl.pallas_call(
        fourier_kernel,
        in_specs=[pl.BlockSpec(memory_space=pltpu.VMEM)] * 9,
        out_shape=[jax.ShapeDtypeStruct((slots, 8 * lats), jnp.bfloat16)] * 8,
        scratch_shapes=[pltpu.VMEM((4 * lats, lon_total), jnp.bfloat16)],
        compiler_params=params(24),
        cost_estimate=cost(2 * steps * 256 * lon_total * 4 * lats, 2 * table.size),
        name="fourier_rows",
    )(table, *grads)


def turn_kernel(wave_ref, _, *refs):
    blocks, (out_ref, rows) = refs[:8], refs[8:]
    slots, width = blocks[0].shape
    for t in range(width // 128):
        lanes = slice(128 * t, 128 * t + 128)
        for k in range(8):
            start = pl.multiple_of(wave_ref[k] * slots, 8)
            rows[t, pl.ds(start, slots), :] = blocks[k][:, lanes].astype(jnp.float32)
        for s in range(slots):
            b, lev, r = s // 16, s // 8 % 2, s % 8
            out_ref[2 * r + lev, b, :, lanes] = rows[t, pl.ds(s, 8, stride=slots), :].astype(
                jnp.bfloat16
            )


def turn(waves, after, blocks):
    slots, width = blocks[0].shape
    vmem = pl.BlockSpec(memory_space=pltpu.VMEM)
    return pl.pallas_call(
        turn_kernel,
        in_specs=[pl.BlockSpec(memory_space=pltpu.SMEM), pl.BlockSpec(memory_space=pl.ANY)]
        + [vmem] * 8,
        out_shape=jax.ShapeDtypeStruct((16, slots // 16, 8, width), jnp.bfloat16),
        scratch_shapes=[pltpu.VMEM((width // 128, 8 * slots, 128), jnp.float32)],
        compiler_params=params(12),
        cost_estimate=cost(0, 32 * blocks[0].size),
        name="turn",
    )(waves, after, *blocks)


def spectral_kernel(slot_ref, four_hbm, basis_hbm, out_ref, four_ref, basis, left, total, sems):
    steps, _, lats, degs = basis.shape
    deg_dev = degs // 16
    copies = [
        pltpu.make_async_copy(basis_hbm.at[:, b], basis.at[b], sems.at[b]) for b in range(steps)
    ]
    fetch = pltpu.make_async_copy(four_hbm, four_ref, sems.at[steps])
    fetch.start()
    for copy in copies:
        copy.start()
    fetch.wait()

    def summed(b):
        for q in range(8):
            for lev in range(2):
                block = four_ref[2 * q + lev, b].astype(jnp.float32)
                for seg in range(8):
                    left[pl.ds(64 * lev + 8 * seg, 8), pl.ds(q * lats, lats)] = block[
                        :, seg * lats : (seg + 1) * lats
                    ]
        copies[b].wait()
        value = jnp.dot(
            left[...].astype(jnp.bfloat16),
            basis[b].reshape(8 * lats, degs),
            preferred_element_type=jnp.float32,
        )
        degree = lax.broadcasted_iota(jnp.int32, value.shape, 1)
        return jnp.where(degree >= slot_ref[b], value, 0.0)

    for k in range(2):
        even, odd = summed(2 * k), summed(2 * k + 1)
        for lev in range(2):
            rows = slice(64 * lev, 64 * lev + 64)
            both = jnp.concatenate([even[rows], odd[rows]], 0).T
            for a in range(16):
                out_ref[2 * a + lev, pl.ds(k * deg_dev, deg_dev)] = both[
                    a * deg_dev : (a + 1) * deg_dev
                ].astype(jnp.bfloat16)
    total[...] = summed(4).T
    half = deg_dev // 2
    even = total[pl.ds(0, degs // 2, stride=2), :]
    odd = total[pl.ds(1, degs // 2, stride=2), :]
    low = lax.broadcasted_iota(jnp.int32, even.shape, 1) < 64
    pair = (
        jnp.where(low, even, pltpu.roll(odd, 64, 1)),
        jnp.where(low, pltpu.roll(even, 64, 1), odd),
    )
    for a in range(16):
        for lev in range(2):
            out_ref[2 * a + lev, pl.ds(2 * deg_dev, half)] = pair[lev][
                a * half : (a + 1) * half
            ].astype(jnp.bfloat16)
    rows = 5 * half
    for a in range(32):
        out_ref[a, pl.ds(rows, out_ref.shape[1] - rows)] = jnp.zeros(
            (out_ref.shape[1] - rows, 128), jnp.bfloat16
        )


def spectral_parts(slots, fourier, basis):
    _, steps, lats, degs = basis.shape
    hbm = pl.BlockSpec(memory_space=pl.ANY)
    return pl.pallas_call(
        spectral_kernel,
        in_specs=[pl.BlockSpec(memory_space=pltpu.SMEM), hbm, hbm],
        out_shape=jax.ShapeDtypeStruct((32, 104, 128), jnp.bfloat16),
        scratch_shapes=[
            pltpu.VMEM(fourier.shape, jnp.bfloat16),
            pltpu.VMEM((steps, 8, lats, degs), jnp.bfloat16),
            pltpu.VMEM((128, 8 * lats), jnp.float32),
            pltpu.VMEM((degs, 128), jnp.float32),
            pltpu.SemaphoreType.DMA((steps + 1,)),
        ],
        compiler_params=params(16),
        cost_estimate=cost(5 * 2 * 128 * 8 * lats * degs, 2 * basis.size + 2 * fourier.size),
        name="spectral_parts",
    )(slots, fourier, basis)


def finish_kernel(in_ref, out_ref, rows):
    depth = in_ref.shape[1]
    for x in range(4):
        for zq in range(2):
            for lev in range(2):
                first = in_ref[8 * x + 2 * zq + lev].astype(jnp.float32)
                second = in_ref[8 * x + 4 + 2 * zq + lev].astype(jnp.float32)
                rows[pl.ds((8 * lev + 2 * x + zq) * depth, depth), :] = first + second
    low = lax.broadcasted_iota(jnp.int32, (16, 128), 1) < 64
    for n in range(0, 40, 2):
        parts = []
        for k in range(2):
            one = rows[pl.ds(40 * k + n, 16, stride=depth), :]
            two = rows[pl.ds(40 * k + n + 1, 16, stride=depth), :]
            parts.append(jnp.where(low, one, pltpu.roll(two, 64, 1)))
            parts.append(jnp.where(low, pltpu.roll(one, 64, 1), two))
        parts.append(rows[pl.ds(80 + n // 2, 16, stride=depth), :])
        out_ref[pl.ds(64 * n, 128), :] = jnp.concatenate(parts, 0).T


def finish(received):
    return pl.pallas_call(
        finish_kernel,
        out_shape=jax.ShapeDtypeStruct((40 * 64, 80), jnp.float32),
        scratch_shapes=[pltpu.VMEM((16 * received.shape[1], 128), jnp.float32)],
        compiler_params=params(12),
        cost_estimate=cost(received.size, 2 * received.size + 4 * 40 * 64 * 128),
        name="finish",
    )(received)


def local(out_grad, grid_state, tend_rate, legendre_basis, wave_slot):
    lats, lons = out_grad.shape[1:]
    slot_dev, degs = legendre_basis.shape[1:]
    x, zq = lax.axis_index("x"), lax.axis_index("zq")
    wave, lev = lax.axis_index("wave"), lax.axis_index("lev")

    partner = wave ^ jnp.arange(8, dtype=jnp.int32)

    def swapped(blocks):
        return [blocks[0]] + [
            lax.ppermute(blocks[k], "wave", [(w, w ^ k) for w in range(8)]) for k in range(1, 8)
        ]

    basis = basis_blocks(lev.astype(jnp.int32)[None], legendre_basis)
    grads = gradient(partner, tend_rate, out_grad, grid_state, basis)
    basis = lax.all_to_all(basis, ("x", "zq"), 0, 0, tiled=True)
    grads = swapped(grads)
    table = wave_table(wave_slot.reshape(8, slot_dev)[partner], partner, lons, 64)
    blocks = swapped(fourier_rows(table, grads))
    fourier = lax.all_to_all(turn(partner, basis, blocks), ("x", "zq", "lev"), 0, 0, tiled=True)

    first = wave * slot_dev + 8 * lev + 2 * x + zq
    slots = jnp.take(wave_slot, first + 16 * jnp.arange(slot_dev // 16, dtype=jnp.int32))
    parts = spectral_parts(slots, fourier, basis)
    parts = lax.all_to_all(parts, ("x", "zp", "zq", "lev"), 0, 0, tiled=True)
    return finish(parts).reshape(degs // 16, 2, 32, slot_dev)


def solution(mesh):
    fine = Mesh(
        mesh.devices.reshape(4, 2, 2, *mesh.devices.shape[1:]), ("x", "zp", "zq", "wave", "lev")
    )
    lat = ("x", "zp", "zq")
    in_specs = (P("lev", lat, "wave"), P("lev", lat, "wave"), P("lev"), P(lat, "wave", None), P())
    out_specs = P(lat, None, "lev", "wave")
    return jax.shard_map(local, mesh=fine, in_specs=in_specs, out_specs=out_specs, check_vma=False)
```

```python
import math

import jax
import jax.numpy as jnp
from jax import lax
from jax.experimental import pallas as pl
from jax.experimental.pallas import tpu as pltpu
from jax.sharding import Mesh, PartitionSpec as P

def params(mib):
    return pltpu.CompilerParams(vmem_limit_bytes=mib * 1024 * 1024)


def cost(flops, moved, trans=0):
    return pl.CostEstimate(flops=flops, bytes_accessed=moved, transcendentals=trans)


def basis_kernel(lev_ref, basis_hbm, out_hbm, token_ref, in_buf, out_buf, in_sems, out_sems):
    steps, lats, _, degs = in_buf.shape
    lev = lev_ref[0]
    reads = [
        pltpu.make_async_copy(basis_hbm.at[:, 2 * b + lev], in_buf.at[b], in_sems.at[b])
        for b in range(steps)
    ]
    for read in reads:
        read.start()
    row = lax.broadcasted_iota(jnp.int32, (128, 128), 0)
    col = lax.broadcasted_iota(jnp.int32, (128, 128), 1)
    swap = (col == row % 16 * 8 + row // 16).astype(jnp.bfloat16)
    token_ref[...] = jnp.zeros_like(token_ref)
    writes = []
    for b in range(steps):
        reads[b].wait()
        for g in range(lats // 16):
            block = in_buf[b, 16 * g : 16 * g + 16].astype(jnp.float32).reshape(128, degs)
            turned = jnp.dot(swap, block.astype(jnp.bfloat16), preferred_element_type=jnp.float32)
            out_buf[b, :, 16 * g : 16 * g + 16, :] = turned.astype(jnp.bfloat16).reshape(
                8, 16, degs
            )
        writes.append(pltpu.make_async_copy(out_buf.at[b], out_hbm.at[:, b], out_sems.at[b]))
        writes[b].start()
    for write in writes:
        write.wait()


def basis_blocks(lev, basis):
    lats, slots, degs = basis.shape
    steps = slots // 16
    hbm = pl.BlockSpec(memory_space=pltpu.HBM)
    return pl.pallas_call(
        basis_kernel,
        in_specs=[pl.BlockSpec(memory_space=pltpu.SMEM), hbm],
        out_specs=[hbm, pl.BlockSpec(memory_space=pltpu.VMEM)],
        out_shape=[
            jax.ShapeDtypeStruct((8, steps, lats, degs), jnp.bfloat16),
            jax.ShapeDtypeStruct((8, 128), jnp.float32),
        ],
        scratch_shapes=[
            pltpu.VMEM((steps, lats, 8, degs), jnp.bfloat16),
            pltpu.VMEM((steps, 8, lats, degs), jnp.bfloat16),
            pltpu.SemaphoreType.DMA((steps,)),
            pltpu.SemaphoreType.DMA((steps,)),
        ],
        compiler_params=params(60),
        cost_estimate=cost(0, 2 * lats * slots * degs),
        name="basis_blocks",
    )(lev, basis.reshape(lats, slots // 8, 8, degs))


def grad_kernel(wave_ref, rate_ref, grad_ref, state_ref, _, *outs):
    lons = grad_ref.shape[-1]
    for k in range(8):
        to = wave_ref[k]
        for c in range(4):
            slope = 1.0 - jnp.tanh(state_ref[c, to].astype(jnp.float32)) ** 2
            value = grad_ref[c, to].astype(jnp.float32) * (1.0 + rate_ref[8 * c + to] * slope)
            outs[k][c // 2, :, pl.ds((c % 2) * lons, lons)] = value.astype(jnp.bfloat16)


def gradient(to, rate, grad, state, after):
    chans, lats, lons = grad.shape
    four = (4, chans // 4, lats, lons)
    smem, vmem = pl.BlockSpec(memory_space=pltpu.SMEM), pl.BlockSpec(memory_space=pltpu.VMEM)
    return pl.pallas_call(
        grad_kernel,
        in_specs=[smem, smem, vmem, vmem, vmem],
        out_shape=[jax.ShapeDtypeStruct((2, lats, 2 * lons), jnp.bfloat16)] * 8,
        compiler_params=params(16),
        cost_estimate=cost(6 * grad.size, 6 * grad.size, grad.size),
        name="gradient",
    )(to, rate, grad.reshape(four), state.reshape(four), after)


def table_kernel(coarse_cos, coarse_sin, fine_cos, fine_sin, out_ref):
    fine = fine_cos.shape[0]
    for j in range(coarse_cos.shape[0]):
        cos, sin = coarse_cos[j : j + 1, :], coarse_sin[j : j + 1, :]
        out_ref[0, j * fine : (j + 1) * fine, :] = (
            cos * fine_cos[...] - sin * fine_sin[...]
        ).astype(jnp.bfloat16)


def wave_table(slots, blocks, lons, fine):
    lon_total = 8 * lons
    quarter = jnp.array([0, lon_total // 4], jnp.int32)[None, :, None]
    phase = jnp.broadcast_to(quarter, (8, 2, slots.shape[1])).reshape(1, -1)
    slot = jnp.broadcast_to(slots[:, None, :], (8, 2, slots.shape[1])).reshape(1, -1)

    def trig(lon, shift):
        index = (slot * lon[:, None] + shift) % lon_total
        angle = index.astype(jnp.float32) * (2.0 * math.pi / lon_total)
        return jnp.cos(angle), jnp.sin(angle)

    starts = blocks[:, None] * lons + fine * jnp.arange(lons // fine, dtype=jnp.int32)[None, :]
    coarse_cos, coarse_sin = trig(starts.reshape(-1), 0)
    fine_cos, fine_sin = trig(jnp.arange(fine, dtype=jnp.int32), phase)
    scale = 1.0 / math.sqrt(lon_total)
    columns = slot.shape[1]
    part = lambda a: pl.BlockSpec((a.shape[0], 256), lambda j: (0, j))
    return pl.pallas_call(
        table_kernel,
        grid=(columns // 256,),
        in_specs=[part(a) for a in (coarse_cos, coarse_sin, fine_cos, fine_sin)],
        out_specs=pl.BlockSpec((1, lon_total, 256), lambda j: (j, 0, 0)),
        out_shape=jax.ShapeDtypeStruct((columns // 256, lon_total, 256), jnp.bfloat16),
        compiler_params=params(12),
        cost_estimate=cost(3 * columns * lon_total, 2 * columns * lon_total),
        name="wave_table",
    )(coarse_cos * scale, coarse_sin * scale, fine_cos, fine_sin)


def fourier_kernel(table_ref, *refs):
    grads, outs, rows = refs[:8], refs[8:16], refs[16]
    lats, lons = grads[0].shape[1], grads[0].shape[2] // 2
    for k in range(8):
        for c in range(4):
            rows[pl.ds(c * lats, lats), pl.ds(k * lons, lons)] = grads[k][
                c // 2, :, pl.ds((c % 2) * lons, lons)
            ]
    width, slots = 4 * lats, outs[0].shape[0]
    for step in range(16 * slots // 256):
        value = jnp.dot(rows[...], table_ref[step], preferred_element_type=jnp.float32).T
        first, stop = 256 * step, 256 * step + 256
        for kp in range(first // slots, -(-stop // slots)):
            low, high = max(first, kp * slots), min(stop, (kp + 1) * slots)
            outs[kp // 2][low - kp * slots : high - kp * slots, pl.ds(kp % 2 * width, width)] = (
                value[low - first : high - first].astype(jnp.bfloat16)
            )


def fourier_rows(table, grads):
    _, lats, lons2 = grads[0].shape
    steps, lon_total, _ = table.shape
    slots = steps * 256 // 16
    return pl.pallas_call(
        fourier_kernel,
        in_specs=[pl.BlockSpec(memory_space=pltpu.VMEM)] * 9,
        out_shape=[jax.ShapeDtypeStruct((slots, 8 * lats), jnp.bfloat16)] * 8,
        scratch_shapes=[pltpu.VMEM((4 * lats, lon_total), jnp.bfloat16)],
        compiler_params=params(24),
        cost_estimate=cost(2 * steps * 256 * lon_total * 4 * lats, 2 * table.size),
        name="fourier_rows",
    )(table, *grads)


def turn_kernel(wave_ref, _, *refs):
    blocks, (out_ref, rows) = refs[:8], refs[8:]
    slots, width = blocks[0].shape
    for t in range(width // 128):
        lanes = slice(128 * t, 128 * t + 128)
        for k in range(8):
            start = pl.multiple_of(wave_ref[k] * slots, 8)
            rows[t, pl.ds(start, slots), :] = blocks[k][:, lanes].astype(jnp.float32)
        for s in range(slots):
            b, lev, r = s // 16, s // 8 % 2, s % 8
            out_ref[2 * r + lev, b, :, lanes] = rows[t, pl.ds(s, 8, stride=slots), :].astype(
                jnp.bfloat16
            )


def turn(waves, after, blocks):
    slots, width = blocks[0].shape
    vmem = pl.BlockSpec(memory_space=pltpu.VMEM)
    return pl.pallas_call(
        turn_kernel,
        in_specs=[pl.BlockSpec(memory_space=pltpu.SMEM), pl.BlockSpec(memory_space=pl.ANY)]
        + [vmem] * 8,
        out_shape=jax.ShapeDtypeStruct((16, slots // 16, 8, width), jnp.bfloat16),
        scratch_shapes=[pltpu.VMEM((width // 128, 8 * slots, 128), jnp.float32)],
        compiler_params=params(12),
        cost_estimate=cost(0, 32 * blocks[0].size),
        name="turn",
    )(waves, after, *blocks)


def spectral_kernel(slot_ref, four_hbm, basis_hbm, out_ref, four_ref, basis, left, total, sems):
    steps, _, lats, degs = basis.shape
    deg_dev = degs // 16
    copies = [
        pltpu.make_async_copy(basis_hbm.at[:, b], basis.at[b], sems.at[b]) for b in range(steps)
    ]
    fetch = pltpu.make_async_copy(four_hbm, four_ref, sems.at[steps])
    fetch.start()
    for copy in copies:
        copy.start()
    fetch.wait()

    def summed(b):
        for q in range(8):
            for lev in range(2):
                block = four_ref[2 * q + lev, b].astype(jnp.float32)
                for seg in range(8):
                    left[pl.ds(64 * lev + 8 * seg, 8), pl.ds(q * lats, lats)] = block[
                        :, seg * lats : (seg + 1) * lats
                    ]
        copies[b].wait()
        value = jnp.dot(
            left[...].astype(jnp.bfloat16),
            basis[b].reshape(8 * lats, degs),
            preferred_element_type=jnp.float32,
        )
        degree = lax.broadcasted_iota(jnp.int32, value.shape, 1)
        return jnp.where(degree >= slot_ref[b], value, 0.0)

    for k in range(2):
        even, odd = summed(2 * k), summed(2 * k + 1)
        for lev in range(2):
            rows = slice(64 * lev, 64 * lev + 64)
            both = jnp.concatenate([even[rows], odd[rows]], 0).T
            for a in range(16):
                out_ref[2 * a + lev, pl.ds(k * deg_dev, deg_dev)] = both[
                    a * deg_dev : (a + 1) * deg_dev
                ].astype(jnp.bfloat16)
    total[...] = summed(4).T
    half = deg_dev // 2
    even = total[pl.ds(0, degs // 2, stride=2), :]
    odd = total[pl.ds(1, degs // 2, stride=2), :]
    low = lax.broadcasted_iota(jnp.int32, even.shape, 1) < 64
    pair = (
        jnp.where(low, even, pltpu.roll(odd, 64, 1)),
        jnp.where(low, pltpu.roll(even, 64, 1), odd),
    )
    for a in range(16):
        for lev in range(2):
            out_ref[2 * a + lev, pl.ds(2 * deg_dev, half)] = pair[lev][
                a * half : (a + 1) * half
            ].astype(jnp.bfloat16)
    rows = 5 * half
    for a in range(32):
        out_ref[a, pl.ds(rows, out_ref.shape[1] - rows)] = jnp.zeros(
            (out_ref.shape[1] - rows, 128), jnp.bfloat16
        )


def spectral_parts(slots, fourier, basis):
    _, steps, lats, degs = basis.shape
    hbm = pl.BlockSpec(memory_space=pl.ANY)
    return pl.pallas_call(
        spectral_kernel,
        in_specs=[pl.BlockSpec(memory_space=pltpu.SMEM), hbm, hbm],
        out_shape=jax.ShapeDtypeStruct((32, 104, 128), jnp.bfloat16),
        scratch_shapes=[
            pltpu.VMEM(fourier.shape, jnp.bfloat16),
            pltpu.VMEM((steps, 8, lats, degs), jnp.bfloat16),
            pltpu.VMEM((128, 8 * lats), jnp.float32),
            pltpu.VMEM((degs, 128), jnp.float32),
            pltpu.SemaphoreType.DMA((steps + 1,)),
        ],
        compiler_params=params(16),
        cost_estimate=cost(5 * 2 * 128 * 8 * lats * degs, 2 * basis.size + 2 * fourier.size),
        name="spectral_parts",
    )(slots, fourier, basis)


def finish_kernel(in_ref, out_ref, rows):
    depth = in_ref.shape[1]
    for x in range(4):
        for zq in range(2):
            for lev in range(2):
                first = in_ref[8 * x + 2 * zq + lev].astype(jnp.float32)
                second = in_ref[8 * x + 4 + 2 * zq + lev].astype(jnp.float32)
                rows[pl.ds((8 * lev + 2 * x + zq) * depth, depth), :] = first + second
    low = lax.broadcasted_iota(jnp.int32, (16, 128), 1) < 64
    for n in range(0, 40, 2):
        parts = []
        for k in range(2):
            one = rows[pl.ds(40 * k + n, 16, stride=depth), :]
            two = rows[pl.ds(40 * k + n + 1, 16, stride=depth), :]
            parts.append(jnp.where(low, one, pltpu.roll(two, 64, 1)))
            parts.append(jnp.where(low, pltpu.roll(one, 64, 1), two))
        parts.append(rows[pl.ds(80 + n // 2, 16, stride=depth), :])
        out_ref[pl.ds(64 * n, 128), :] = jnp.concatenate(parts, 0).T


def finish(received):
    return pl.pallas_call(
        finish_kernel,
        out_shape=jax.ShapeDtypeStruct((40 * 64, 80), jnp.float32),
        scratch_shapes=[pltpu.VMEM((16 * received.shape[1], 128), jnp.float32)],
        compiler_params=params(12),
        cost_estimate=cost(received.size, 2 * received.size + 4 * 40 * 64 * 128),
        name="finish",
    )(received)


def local(out_grad, grid_state, tend_rate, legendre_basis, wave_slot):
    lats, lons = out_grad.shape[1:]
    slot_dev, degs = legendre_basis.shape[1:]
    x, zq = lax.axis_index("x"), lax.axis_index("zq")
    wave, lev = lax.axis_index("wave"), lax.axis_index("lev")

    partner = wave ^ jnp.arange(8, dtype=jnp.int32)

    def swapped(blocks):
        blocks = list(blocks)
        for k in (4, 5, 2, 6, 3, 7, 1):
            blocks[k] = lax.ppermute(blocks[k], "wave", [(w, w ^ k) for w in range(8)])
        return blocks

    basis, token = basis_blocks(lev.astype(jnp.int32)[None], legendre_basis)
    grads = gradient(partner, tend_rate, out_grad, grid_state, token)
    basis = lax.all_to_all(basis, ("x", "zq"), 0, 0, tiled=True)
    grads = swapped(grads)
    table = wave_table(wave_slot.reshape(8, slot_dev)[partner], partner, lons, 64)
    blocks = swapped(fourier_rows(table, grads))
    fourier = lax.all_to_all(turn(partner, basis, blocks), ("x", "zq", "lev"), 0, 0, tiled=True)

    first = wave * slot_dev + 8 * lev + 2 * x + zq
    slots = jnp.take(wave_slot, first + 16 * jnp.arange(slot_dev // 16, dtype=jnp.int32))
    parts = spectral_parts(slots, fourier, basis)
    parts = lax.all_to_all(parts, ("x", "zp", "zq", "lev"), 0, 0, tiled=True)
    return finish(parts).reshape(degs // 16, 2, 32, slot_dev)


def solution(mesh):
    fine = Mesh(
        mesh.devices.reshape(4, 2, 2, *mesh.devices.shape[1:]), ("x", "zp", "zq", "wave", "lev")
    )
    lat = ("x", "zp", "zq")
    in_specs = (P("lev", lat, "wave"), P("lev", lat, "wave"), P("lev"), P(lat, "wave", None), P())
    out_specs = P(lat, None, "lev", "wave")
    return jax.shard_map(local, mesh=fine, in_specs=in_specs, out_specs=out_specs, check_vma=False)
```

```python
import math

import jax
import jax.numpy as jnp
from jax import lax
from jax.experimental import pallas as pl
from jax.experimental.pallas import tpu as pltpu
from jax.sharding import Mesh, PartitionSpec as P

TO = ((0, 1, 2, 6, 4, 3, 7, 5), (0, 1, 6, 2, 4, 7, 3, 5))
FROM = ((0, 1, 2, 6, 4, 7, 3, 5), (0, 1, 6, 2, 4, 3, 7, 5))


def params(mib):
    return pltpu.CompilerParams(vmem_limit_bytes=mib * 1024 * 1024)


def cost(flops, moved, trans=0):
    return pl.CostEstimate(flops=flops, bytes_accessed=moved, transcendentals=trans)


def basis_kernel(lev_ref, basis_hbm, out_hbm, token_ref, in_buf, out_buf, in_sems, out_sems):
    steps, lats, _, degs = in_buf.shape
    lev = lev_ref[0]
    reads = [
        pltpu.make_async_copy(basis_hbm.at[:, 2 * b + lev], in_buf.at[b], in_sems.at[b])
        for b in range(steps)
    ]
    for read in reads:
        read.start()
    row = lax.broadcasted_iota(jnp.int32, (128, 128), 0)
    col = lax.broadcasted_iota(jnp.int32, (128, 128), 1)
    swap = (col == row % 16 * 8 + row // 16).astype(jnp.bfloat16)
    token_ref[...] = jnp.zeros_like(token_ref)
    writes = []
    for b in range(steps):
        reads[b].wait()
        for g in range(lats // 16):
            block = in_buf[b, 16 * g : 16 * g + 16].astype(jnp.float32).reshape(128, degs)
            turned = jnp.dot(swap, block.astype(jnp.bfloat16), preferred_element_type=jnp.float32)
            out_buf[b, :, 16 * g : 16 * g + 16, :] = turned.astype(jnp.bfloat16).reshape(
                8, 16, degs
            )
        writes.append(pltpu.make_async_copy(out_buf.at[b], out_hbm.at[:, b], out_sems.at[b]))
        writes[b].start()
    for write in writes:
        write.wait()


def basis_blocks(lev, basis):
    lats, slots, degs = basis.shape
    steps = slots // 16
    hbm = pl.BlockSpec(memory_space=pltpu.HBM)
    return pl.pallas_call(
        basis_kernel,
        in_specs=[pl.BlockSpec(memory_space=pltpu.SMEM), hbm],
        out_specs=[hbm, pl.BlockSpec(memory_space=pltpu.VMEM)],
        out_shape=[
            jax.ShapeDtypeStruct((8, steps, lats, degs), jnp.bfloat16),
            jax.ShapeDtypeStruct((8, 128), jnp.float32),
        ],
        scratch_shapes=[
            pltpu.VMEM((steps, lats, 8, degs), jnp.bfloat16),
            pltpu.VMEM((steps, 8, lats, degs), jnp.bfloat16),
            pltpu.SemaphoreType.DMA((steps,)),
            pltpu.SemaphoreType.DMA((steps,)),
        ],
        compiler_params=params(60),
        cost_estimate=cost(0, 2 * lats * slots * degs),
        name="basis_blocks",
    )(lev, basis.reshape(lats, slots // 8, 8, degs))


def grad_kernel(wave_ref, rate_ref, grad_ref, state_ref, _, *outs):
    lons = grad_ref.shape[-1]
    for k in range(8):
        to = wave_ref[k]
        for c in range(4):
            slope = 1.0 - jnp.tanh(state_ref[c, to].astype(jnp.float32)) ** 2
            value = grad_ref[c, to].astype(jnp.float32) * (1.0 + rate_ref[8 * c + to] * slope)
            outs[k][c // 2, :, pl.ds((c % 2) * lons, lons)] = value.astype(jnp.bfloat16)


def gradient(to, rate, grad, state, after):
    chans, lats, lons = grad.shape
    four = (4, chans // 4, lats, lons)
    smem, vmem = pl.BlockSpec(memory_space=pltpu.SMEM), pl.BlockSpec(memory_space=pltpu.VMEM)
    return pl.pallas_call(
        grad_kernel,
        in_specs=[smem, smem, vmem, vmem, vmem],
        out_shape=[jax.ShapeDtypeStruct((2, lats, 2 * lons), jnp.bfloat16)] * 8,
        compiler_params=params(16),
        cost_estimate=cost(6 * grad.size, 6 * grad.size, grad.size),
        name="gradient",
    )(to, rate, grad.reshape(four), state.reshape(four), after)


def table_kernel(coarse_cos, coarse_sin, fine_cos, fine_sin, out_ref):
    fine = fine_cos.shape[0]
    for j in range(coarse_cos.shape[0]):
        cos, sin = coarse_cos[j : j + 1, :], coarse_sin[j : j + 1, :]
        out_ref[0, j * fine : (j + 1) * fine, :] = (
            cos * fine_cos[...] - sin * fine_sin[...]
        ).astype(jnp.bfloat16)


def wave_table(slots, blocks, lons, fine):
    lon_total = 8 * lons
    quarter = jnp.array([0, lon_total // 4], jnp.int32)[None, :, None]
    phase = jnp.broadcast_to(quarter, (8, 2, slots.shape[1])).reshape(1, -1)
    slot = jnp.broadcast_to(slots[:, None, :], (8, 2, slots.shape[1])).reshape(1, -1)

    def trig(lon, shift):
        index = (slot * lon[:, None] + shift) % lon_total
        angle = index.astype(jnp.float32) * (2.0 * math.pi / lon_total)
        return jnp.cos(angle), jnp.sin(angle)

    starts = blocks[:, None] * lons + fine * jnp.arange(lons // fine, dtype=jnp.int32)[None, :]
    coarse_cos, coarse_sin = trig(starts.reshape(-1), 0)
    fine_cos, fine_sin = trig(jnp.arange(fine, dtype=jnp.int32), phase)
    scale = 1.0 / math.sqrt(lon_total)
    columns = slot.shape[1]
    part = lambda a: pl.BlockSpec((a.shape[0], 256), lambda j: (0, j))
    return pl.pallas_call(
        table_kernel,
        grid=(columns // 256,),
        in_specs=[part(a) for a in (coarse_cos, coarse_sin, fine_cos, fine_sin)],
        out_specs=pl.BlockSpec((1, lon_total, 256), lambda j: (j, 0, 0)),
        out_shape=jax.ShapeDtypeStruct((columns // 256, lon_total, 256), jnp.bfloat16),
        compiler_params=params(12),
        cost_estimate=cost(3 * columns * lon_total, 2 * columns * lon_total),
        name="wave_table",
    )(coarse_cos * scale, coarse_sin * scale, fine_cos, fine_sin)


def fourier_kernel(table_ref, *refs):
    grads, outs, rows = refs[:8], refs[8:16], refs[16]
    lats, lons = grads[0].shape[1], grads[0].shape[2] // 2
    for k in range(8):
        for c in range(4):
            rows[pl.ds(c * lats, lats), pl.ds(k * lons, lons)] = grads[k][
                c // 2, :, pl.ds((c % 2) * lons, lons)
            ]
    width, slots = 4 * lats, outs[0].shape[0]
    for step in range(16 * slots // 256):
        value = jnp.dot(rows[...], table_ref[step], preferred_element_type=jnp.float32).T
        first, stop = 256 * step, 256 * step + 256
        for kp in range(first // slots, -(-stop // slots)):
            low, high = max(first, kp * slots), min(stop, (kp + 1) * slots)
            outs[kp // 2][low - kp * slots : high - kp * slots, pl.ds(kp % 2 * width, width)] = (
                value[low - first : high - first].astype(jnp.bfloat16)
            )


def fourier_rows(table, grads):
    _, lats, lons2 = grads[0].shape
    steps, lon_total, _ = table.shape
    slots = steps * 256 // 16
    return pl.pallas_call(
        fourier_kernel,
        in_specs=[pl.BlockSpec(memory_space=pltpu.VMEM)] * 9,
        out_shape=[jax.ShapeDtypeStruct((slots, 8 * lats), jnp.bfloat16)] * 8,
        scratch_shapes=[pltpu.VMEM((4 * lats, lon_total), jnp.bfloat16)],
        compiler_params=params(24),
        cost_estimate=cost(2 * steps * 256 * lon_total * 4 * lats, 2 * table.size),
        name="fourier_rows",
    )(table, *grads)


def turn_kernel(wave_ref, _, *refs):
    blocks, (out_ref, rows) = refs[:8], refs[8:]
    slots, width = blocks[0].shape
    for t in range(width // 128):
        lanes = slice(128 * t, 128 * t + 128)
        for k in range(8):
            start = pl.multiple_of(wave_ref[k] * slots, 8)
            rows[t, pl.ds(start, slots), :] = blocks[k][:, lanes].astype(jnp.float32)
        for s in range(slots):
            b, lev, r = s // 16, s // 8 % 2, s % 8
            out_ref[2 * r + lev, b, :, lanes] = rows[t, pl.ds(s, 8, stride=slots), :].astype(
                jnp.bfloat16
            )


def turn(waves, after, blocks):
    slots, width = blocks[0].shape
    vmem = pl.BlockSpec(memory_space=pltpu.VMEM)
    return pl.pallas_call(
        turn_kernel,
        in_specs=[pl.BlockSpec(memory_space=pltpu.SMEM), pl.BlockSpec(memory_space=pl.ANY)]
        + [vmem] * 8,
        out_shape=jax.ShapeDtypeStruct((16, slots // 16, 8, width), jnp.bfloat16),
        scratch_shapes=[pltpu.VMEM((width // 128, 8 * slots, 128), jnp.float32)],
        compiler_params=params(12),
        cost_estimate=cost(0, 32 * blocks[0].size),
        name="turn",
    )(waves, after, *blocks)


def spectral_kernel(slot_ref, four_hbm, basis_hbm, out_ref, four_ref, basis, left, total, sems):
    steps, _, lats, degs = basis.shape
    deg_dev = degs // 16
    fetch = pltpu.make_async_copy(four_hbm, four_ref, sems.at[steps, 0])
    fetch.start()
    copies = [
        [
            pltpu.make_async_copy(basis_hbm.at[q, b], basis.at[b, q], sems.at[b, q])
            for q in range(8)
        ]
        for b in range(steps)
    ]
    for copy in sum(copies, []):
        copy.start()
    fetch.wait()

    def summed(b):
        for q in range(8):
            for lev in range(2):
                block = four_ref[2 * q + lev, b].astype(jnp.float32)
                for seg in range(8):
                    left[pl.ds(64 * lev + 8 * seg, 8), pl.ds(q * lats, lats)] = block[
                        :, seg * lats : (seg + 1) * lats
                    ]
        for copy in copies[b]:
            copy.wait()
        value = jnp.dot(
            left[...].astype(jnp.bfloat16),
            basis[b].reshape(8 * lats, degs),
            preferred_element_type=jnp.float32,
        )
        degree = lax.broadcasted_iota(jnp.int32, value.shape, 1)
        return jnp.where(degree >= slot_ref[b], value, 0.0)

    for k in range(2):
        even, odd = summed(2 * k), summed(2 * k + 1)
        for lev in range(2):
            rows = slice(64 * lev, 64 * lev + 64)
            both = jnp.concatenate([even[rows], odd[rows]], 0).T
            for a in range(16):
                out_ref[2 * a + lev, pl.ds(k * deg_dev, deg_dev)] = both[
                    a * deg_dev : (a + 1) * deg_dev
                ].astype(jnp.bfloat16)
    total[...] = summed(4).T
    half = deg_dev // 2
    even = total[pl.ds(0, degs // 2, stride=2), :]
    odd = total[pl.ds(1, degs // 2, stride=2), :]
    low = lax.broadcasted_iota(jnp.int32, even.shape, 1) < 64
    pair = (
        jnp.where(low, even, pltpu.roll(odd, 64, 1)),
        jnp.where(low, pltpu.roll(even, 64, 1), odd),
    )
    for a in range(16):
        for lev in range(2):
            out_ref[2 * a + lev, pl.ds(2 * deg_dev, half)] = pair[lev][
                a * half : (a + 1) * half
            ].astype(jnp.bfloat16)
    rows = 5 * half
    for a in range(32):
        out_ref[a, pl.ds(rows, out_ref.shape[1] - rows)] = jnp.zeros(
            (out_ref.shape[1] - rows, 128), jnp.bfloat16
        )


def spectral_parts(slots, fourier, basis):
    _, steps, lats, degs = basis.shape
    hbm = pl.BlockSpec(memory_space=pl.ANY)
    return pl.pallas_call(
        spectral_kernel,
        in_specs=[pl.BlockSpec(memory_space=pltpu.SMEM), hbm, hbm],
        out_shape=jax.ShapeDtypeStruct((32, 104, 128), jnp.bfloat16),
        scratch_shapes=[
            pltpu.VMEM(fourier.shape, jnp.bfloat16),
            pltpu.VMEM((steps, 8, lats, degs), jnp.bfloat16),
            pltpu.VMEM((128, 8 * lats), jnp.float32),
            pltpu.VMEM((degs, 128), jnp.float32),
            pltpu.SemaphoreType.DMA((steps + 1, 8)),
        ],
        compiler_params=params(16),
        cost_estimate=cost(5 * 2 * 128 * 8 * lats * degs, 2 * basis.size + 2 * fourier.size),
        name="spectral_parts",
    )(slots, fourier, basis)


def finish_kernel(in_ref, out_ref, rows):
    depth = in_ref.shape[1]
    for x in range(4):
        for zq in range(2):
            for lev in range(2):
                first = in_ref[8 * x + 2 * zq + lev].astype(jnp.float32)
                second = in_ref[8 * x + 4 + 2 * zq + lev].astype(jnp.float32)
                rows[pl.ds((8 * lev + 2 * x + zq) * depth, depth), :] = first + second
    low = lax.broadcasted_iota(jnp.int32, (16, 128), 1) < 64
    for n in range(0, 40, 2):
        parts = []
        for k in range(2):
            one = rows[pl.ds(40 * k + n, 16, stride=depth), :]
            two = rows[pl.ds(40 * k + n + 1, 16, stride=depth), :]
            parts.append(jnp.where(low, one, pltpu.roll(two, 64, 1)))
            parts.append(jnp.where(low, pltpu.roll(one, 64, 1), two))
        parts.append(rows[pl.ds(80 + n // 2, 16, stride=depth), :])
        out_ref[pl.ds(64 * n, 128), :] = jnp.concatenate(parts, 0).T


def finish(received):
    return pl.pallas_call(
        finish_kernel,
        out_shape=jax.ShapeDtypeStruct((40 * 64, 80), jnp.float32),
        scratch_shapes=[pltpu.VMEM((16 * received.shape[1], 128), jnp.float32)],
        compiler_params=params(12),
        cost_estimate=cost(received.size, 2 * received.size + 4 * 40 * 64 * 128),
        name="finish",
    )(received)


def local(out_grad, grid_state, tend_rate, legendre_basis, wave_slot):
    lats, lons = out_grad.shape[1:]
    slot_dev, degs = legendre_basis.shape[1:]
    x, zq = lax.axis_index("x"), lax.axis_index("zq")
    wave, lev = lax.axis_index("wave"), lax.axis_index("lev")

    to, source = (
        wave ^ jnp.where(wave % 2 == 0, *(jnp.array(row, jnp.int32) for row in table))
        for table in (TO, FROM)
    )

    def swapped(blocks):
        return [blocks[0]] + [
            lax.ppermute(blocks[k], "wave", [(w, w ^ TO[w % 2][k]) for w in range(8)])
            for k in range(1, 8)
        ]

    basis, token = basis_blocks(lev.astype(jnp.int32)[None], legendre_basis)
    grads = gradient(to, tend_rate, out_grad, grid_state, token)
    basis = lax.all_to_all(basis, ("x", "zq"), 0, 0, tiled=True)
    grads = swapped(grads)
    table = wave_table(wave_slot.reshape(8, slot_dev)[to], source, lons, 64)
    blocks = swapped(fourier_rows(table, grads))
    fourier = lax.all_to_all(turn(source, basis, blocks), ("x", "zq", "lev"), 0, 0, tiled=True)

    first = wave * slot_dev + 8 * lev + 2 * x + zq
    slots = jnp.take(wave_slot, first + 16 * jnp.arange(slot_dev // 16, dtype=jnp.int32))
    parts = spectral_parts(slots, fourier, basis)
    parts = lax.all_to_all(parts, ("x", "zp", "zq", "lev"), 0, 0, tiled=True)
    return finish(parts).reshape(degs // 16, 2, 32, slot_dev)


def solution(mesh):
    fine = Mesh(
        mesh.devices.reshape(4, 2, 2, *mesh.devices.shape[1:]), ("x", "zp", "zq", "wave", "lev")
    )
    lat = ("x", "zp", "zq")
    in_specs = (P("lev", lat, "wave"), P("lev", lat, "wave"), P("lev"), P(lat, "wave", None), P())
    out_specs = P(lat, None, "lev", "wave")
    return jax.shard_map(local, mesh=fine, in_specs=in_specs, out_specs=out_specs, check_vma=False)
```

```python
import math

import jax
import jax.numpy as jnp
from jax import lax
from jax.experimental import pallas as pl
from jax.experimental.pallas import tpu as pltpu
from jax.sharding import Mesh, PartitionSpec as P

TO = ((0, 1, 2, 6, 4, 3, 7, 5), (0, 1, 6, 2, 4, 7, 3, 5))
FROM = ((0, 1, 2, 6, 4, 7, 3, 5), (0, 1, 6, 2, 4, 3, 7, 5))


AXES = ("x", "zp", "zq", "wave", "lev")
BASIS_AT = ([m for m in range(8)], [m % 2 * 4 + -(m // 2) % 4 for m in range(8)])
FOUR_AT = (
    [m for m in range(16)],
    [m % 2 * 8 + m // 2 % 2 * 4 + -(m // 4) % 4 for m in range(16)],
)
LAST_AT = (
    [m for m in range(32)],
    [-(m % 2 * 4 + m // 2 % 4) % 8 * 4 + -(m // 8) % 4 for m in range(32)],
)


def exchange(blocks, at, axes):
    sizes = dict(x=4, zp=2, zq=2, wave=8, lev=2)
    coordinates = [dict()]
    for axis in AXES:
        coordinates = [{**c, axis: i} for c in coordinates for i in range(sizes[axis])]
    groups = {}
    for index, c in enumerate(coordinates):
        member = 0
        for axis in axes:
            member = member * sizes[axis] + c[axis]
        key = tuple(c[axis] for axis in AXES if axis not in axes)
        groups.setdefault(key, {})[at[c["wave"] % 2][member]] = index
    lists = [[group[i] for i in range(len(group))] for group in groups.values()]
    return lax.all_to_all(blocks, AXES, 0, 0, tiled=True, axis_index_groups=lists)


def params(mib):
    return pltpu.CompilerParams(vmem_limit_bytes=mib * 1024 * 1024)


def cost(flops, moved, trans=0):
    return pl.CostEstimate(flops=flops, bytes_accessed=moved, transcendentals=trans)


def basis_kernel(lev_ref, at_ref, basis_hbm, out_hbm, token_ref, in_buf, out_buf, in_sems, out_sems):
    steps, lats, _, degs = in_buf.shape
    lev = lev_ref[0]
    reads = [
        pltpu.make_async_copy(basis_hbm.at[:, 2 * b + lev], in_buf.at[b], in_sems.at[b])
        for b in range(steps)
    ]
    for read in reads:
        read.start()
    row = lax.broadcasted_iota(jnp.int32, (128, 128), 0)
    col = lax.broadcasted_iota(jnp.int32, (128, 128), 1)
    swap = (col == row % 16 * 8 + row // 16).astype(jnp.bfloat16)
    token_ref[...] = jnp.zeros_like(token_ref)
    writes = []
    for b in range(steps):
        reads[b].wait()
        for g in range(lats // 16):
            block = in_buf[b, 16 * g : 16 * g + 16].astype(jnp.float32).reshape(128, degs)
            turned = jnp.dot(swap, block.astype(jnp.bfloat16), preferred_element_type=jnp.float32)
            out_buf[b, :, 16 * g : 16 * g + 16, :] = turned.astype(jnp.bfloat16).reshape(
                8, 16, degs
            )
        for r in range(8):
            write = pltpu.make_async_copy(
                out_buf.at[b, r], out_hbm.at[at_ref[r], b], out_sems.at[b, r]
            )
            write.start()
            writes.append(write)
    for write in writes:
        write.wait()


def basis_blocks(lev, at, basis):
    lats, slots, degs = basis.shape
    steps = slots // 16
    hbm, smem = pl.BlockSpec(memory_space=pltpu.HBM), pl.BlockSpec(memory_space=pltpu.SMEM)
    return pl.pallas_call(
        basis_kernel,
        in_specs=[smem, smem, hbm],
        out_specs=[hbm, pl.BlockSpec(memory_space=pltpu.VMEM)],
        out_shape=[
            jax.ShapeDtypeStruct((8, steps, lats, degs), jnp.bfloat16),
            jax.ShapeDtypeStruct((8, 128), jnp.float32),
        ],
        scratch_shapes=[
            pltpu.VMEM((steps, lats, 8, degs), jnp.bfloat16),
            pltpu.VMEM((steps, 8, lats, degs), jnp.bfloat16),
            pltpu.SemaphoreType.DMA((steps,)),
            pltpu.SemaphoreType.DMA((steps, 8)),
        ],
        compiler_params=params(60),
        cost_estimate=cost(0, 2 * lats * slots * degs),
        name="basis_blocks",
    )(lev, at, basis.reshape(lats, slots // 8, 8, degs))


def grad_kernel(wave_ref, rate_ref, grad_ref, state_ref, _, *outs):
    lons = grad_ref.shape[-1]
    for k in range(8):
        to = wave_ref[k]
        for c in range(4):
            slope = 1.0 - jnp.tanh(state_ref[c, to].astype(jnp.float32)) ** 2
            value = grad_ref[c, to].astype(jnp.float32) * (1.0 + rate_ref[8 * c + to] * slope)
            outs[k][c // 2, :, pl.ds((c % 2) * lons, lons)] = value.astype(jnp.bfloat16)


def gradient(to, rate, grad, state, after):
    chans, lats, lons = grad.shape
    four = (4, chans // 4, lats, lons)
    smem, vmem = pl.BlockSpec(memory_space=pltpu.SMEM), pl.BlockSpec(memory_space=pltpu.VMEM)
    return pl.pallas_call(
        grad_kernel,
        in_specs=[smem, smem, vmem, vmem, vmem],
        out_shape=[jax.ShapeDtypeStruct((2, lats, 2 * lons), jnp.bfloat16)] * 8,
        compiler_params=params(16),
        cost_estimate=cost(6 * grad.size, 6 * grad.size, grad.size),
        name="gradient",
    )(to, rate, grad.reshape(four), state.reshape(four), after)


def table_kernel(coarse_cos, coarse_sin, fine_cos, fine_sin, out_ref):
    fine = fine_cos.shape[0]
    for j in range(coarse_cos.shape[0]):
        cos, sin = coarse_cos[j : j + 1, :], coarse_sin[j : j + 1, :]
        out_ref[0, j * fine : (j + 1) * fine, :] = (
            cos * fine_cos[...] - sin * fine_sin[...]
        ).astype(jnp.bfloat16)


def wave_table(slots, blocks, lons, fine):
    lon_total = 8 * lons
    quarter = jnp.array([0, lon_total // 4], jnp.int32)[None, :, None]
    phase = jnp.broadcast_to(quarter, (8, 2, slots.shape[1])).reshape(1, -1)
    slot = jnp.broadcast_to(slots[:, None, :], (8, 2, slots.shape[1])).reshape(1, -1)

    def trig(lon, shift):
        index = (slot * lon[:, None] + shift) % lon_total
        angle = index.astype(jnp.float32) * (2.0 * math.pi / lon_total)
        return jnp.cos(angle), jnp.sin(angle)

    starts = blocks[:, None] * lons + fine * jnp.arange(lons // fine, dtype=jnp.int32)[None, :]
    coarse_cos, coarse_sin = trig(starts.reshape(-1), 0)
    fine_cos, fine_sin = trig(jnp.arange(fine, dtype=jnp.int32), phase)
    scale = 1.0 / math.sqrt(lon_total)
    columns = slot.shape[1]
    part = lambda a: pl.BlockSpec((a.shape[0], 256), lambda j: (0, j))
    return pl.pallas_call(
        table_kernel,
        grid=(columns // 256,),
        in_specs=[part(a) for a in (coarse_cos, coarse_sin, fine_cos, fine_sin)],
        out_specs=pl.BlockSpec((1, lon_total, 256), lambda j: (j, 0, 0)),
        out_shape=jax.ShapeDtypeStruct((columns // 256, lon_total, 256), jnp.bfloat16),
        compiler_params=params(12),
        cost_estimate=cost(3 * columns * lon_total, 2 * columns * lon_total),
        name="wave_table",
    )(coarse_cos * scale, coarse_sin * scale, fine_cos, fine_sin)


def fourier_kernel(table_ref, *refs):
    grads, outs, rows = refs[:8], refs[8:16], refs[16]
    lats, lons = grads[0].shape[1], grads[0].shape[2] // 2
    for k in range(8):
        for c in range(4):
            rows[pl.ds(c * lats, lats), pl.ds(k * lons, lons)] = grads[k][
                c // 2, :, pl.ds((c % 2) * lons, lons)
            ]
    width, slots = 4 * lats, outs[0].shape[0]
    for step in range(16 * slots // 256):
        value = jnp.dot(rows[...], table_ref[step], preferred_element_type=jnp.float32).T
        first, stop = 256 * step, 256 * step + 256
        for kp in range(first // slots, -(-stop // slots)):
            low, high = max(first, kp * slots), min(stop, (kp + 1) * slots)
            outs[kp // 2][low - kp * slots : high - kp * slots, pl.ds(kp % 2 * width, width)] = (
                value[low - first : high - first].astype(jnp.bfloat16)
            )


def fourier_rows(table, grads):
    _, lats, lons2 = grads[0].shape
    steps, lon_total, _ = table.shape
    slots = steps * 256 // 16
    return pl.pallas_call(
        fourier_kernel,
        in_specs=[pl.BlockSpec(memory_space=pltpu.VMEM)] * 9,
        out_shape=[jax.ShapeDtypeStruct((slots, 8 * lats), jnp.bfloat16)] * 8,
        scratch_shapes=[pltpu.VMEM((4 * lats, lon_total), jnp.bfloat16)],
        compiler_params=params(24),
        cost_estimate=cost(2 * steps * 256 * lon_total * 4 * lats, 2 * table.size),
        name="fourier_rows",
    )(table, *grads)


def turn_kernel(wave_ref, at_ref, _, *refs):
    blocks, (out_ref, rows) = refs[:8], refs[8:]
    slots, width = blocks[0].shape
    for t in range(width // 128):
        lanes = slice(128 * t, 128 * t + 128)
        for k in range(8):
            start = pl.multiple_of(wave_ref[k] * slots, 8)
            rows[t, pl.ds(start, slots), :] = blocks[k][:, lanes].astype(jnp.float32)
        for s in range(slots):
            b, lev, r = s // 16, s // 8 % 2, s % 8
            out_ref[at_ref[2 * r + lev], b, :, lanes] = rows[t, pl.ds(s, 8, stride=slots), :].astype(
                jnp.bfloat16
            )


def turn(waves, at, after, blocks):
    slots, width = blocks[0].shape
    vmem, smem = pl.BlockSpec(memory_space=pltpu.VMEM), pl.BlockSpec(memory_space=pltpu.SMEM)
    return pl.pallas_call(
        turn_kernel,
        in_specs=[smem, smem, pl.BlockSpec(memory_space=pl.ANY)] + [vmem] * 8,
        out_shape=jax.ShapeDtypeStruct((16, slots // 16, 8, width), jnp.bfloat16),
        scratch_shapes=[pltpu.VMEM((width // 128, 8 * slots, 128), jnp.float32)],
        compiler_params=params(12),
        cost_estimate=cost(0, 32 * blocks[0].size),
        name="turn",
    )(waves, at, after, *blocks)


def spectral_kernel(slot_ref, four_at, last_at, four_ref, basis_hbm, out_ref, *scratch):
    basis, left, total, sems = scratch
    steps, _, lats, degs = basis.shape
    deg_dev = degs // 16
    copies = [
        pltpu.make_async_copy(basis_hbm.at[:, b], basis.at[b], sems.at[b]) for b in range(steps)
    ]
    for copy in copies:
        copy.start()

    def summed(b):
        for j in range(8):
            for lev in range(2):
                block = four_ref[four_at[2 * j + lev], b].astype(jnp.float32)
                for seg in range(8):
                    left[pl.ds(64 * lev + 8 * seg, 8), pl.ds(j * lats, lats)] = block[
                        :, seg * lats : (seg + 1) * lats
                    ]
        copies[b].wait()
        value = jnp.dot(
            left[...].astype(jnp.bfloat16),
            basis[b].reshape(8 * lats, degs),
            preferred_element_type=jnp.float32,
        )
        degree = lax.broadcasted_iota(jnp.int32, value.shape, 1)
        return jnp.where(degree >= slot_ref[b], value, 0.0)

    for k in range(2):
        even, odd = summed(2 * k), summed(2 * k + 1)
        for lev in range(2):
            rows = slice(64 * lev, 64 * lev + 64)
            both = jnp.concatenate([even[rows], odd[rows]], 0).T
            for a in range(16):
                out_ref[last_at[2 * a + lev], pl.ds(k * deg_dev, deg_dev)] = both[
                    a * deg_dev : (a + 1) * deg_dev
                ].astype(jnp.bfloat16)
    total[...] = summed(4).T
    half = deg_dev // 2
    even = total[pl.ds(0, degs // 2, stride=2), :]
    odd = total[pl.ds(1, degs // 2, stride=2), :]
    low = lax.broadcasted_iota(jnp.int32, even.shape, 1) < 64
    pair = (
        jnp.where(low, even, pltpu.roll(odd, 64, 1)),
        jnp.where(low, pltpu.roll(even, 64, 1), odd),
    )
    for a in range(16):
        for lev in range(2):
            out_ref[last_at[2 * a + lev], pl.ds(2 * deg_dev, half)] = pair[lev][
                a * half : (a + 1) * half
            ].astype(jnp.bfloat16)
    rows = 5 * half
    for a in range(32):
        out_ref[a, pl.ds(rows, out_ref.shape[1] - rows)] = jnp.zeros(
            (out_ref.shape[1] - rows, 128), jnp.bfloat16
        )


def spectral_parts(slots, four_at, last_at, fourier, basis):
    _, steps, lats, degs = basis.shape
    vmem, smem = pl.BlockSpec(memory_space=pltpu.VMEM), pl.BlockSpec(memory_space=pltpu.SMEM)
    return pl.pallas_call(
        spectral_kernel,
        in_specs=[smem, smem, smem, vmem, pl.BlockSpec(memory_space=pl.ANY)],
        out_shape=jax.ShapeDtypeStruct((32, 104, 128), jnp.bfloat16),
        scratch_shapes=[
            pltpu.VMEM((steps, 8, lats, degs), jnp.bfloat16),
            pltpu.VMEM((128, 8 * lats), jnp.float32),
            pltpu.VMEM((degs, 128), jnp.float32),
            pltpu.SemaphoreType.DMA((steps,)),
        ],
        compiler_params=params(16),
        cost_estimate=cost(5 * 2 * 128 * 8 * lats * degs, 2 * basis.size + 2 * fourier.size),
        name="spectral_parts",
    )(slots, four_at, last_at, fourier, basis)


def finish_kernel(at_ref, in_ref, out_ref, rows):
    depth = in_ref.shape[1]
    for x in range(4):
        for zq in range(2):
            for lev in range(2):
                first = in_ref[at_ref[8 * x + 2 * zq + lev]].astype(jnp.float32)
                second = in_ref[at_ref[8 * x + 4 + 2 * zq + lev]].astype(jnp.float32)
                rows[pl.ds((8 * lev + 2 * x + zq) * depth, depth), :] = first + second
    low = lax.broadcasted_iota(jnp.int32, (16, 128), 1) < 64
    for n in range(0, 40, 2):
        parts = []
        for k in range(2):
            one = rows[pl.ds(40 * k + n, 16, stride=depth), :]
            two = rows[pl.ds(40 * k + n + 1, 16, stride=depth), :]
            parts.append(jnp.where(low, one, pltpu.roll(two, 64, 1)))
            parts.append(jnp.where(low, pltpu.roll(one, 64, 1), two))
        parts.append(rows[pl.ds(80 + n // 2, 16, stride=depth), :])
        out_ref[pl.ds(64 * n, 128), :] = jnp.concatenate(parts, 0).T


def finish(at, received):
    return pl.pallas_call(
        finish_kernel,
        in_specs=[pl.BlockSpec(memory_space=pltpu.SMEM), pl.BlockSpec(memory_space=pltpu.VMEM)],
        out_shape=jax.ShapeDtypeStruct((40 * 64, 80), jnp.float32),
        scratch_shapes=[pltpu.VMEM((16 * received.shape[1], 128), jnp.float32)],
        compiler_params=params(12),
        cost_estimate=cost(received.size, 2 * received.size + 4 * 40 * 64 * 128),
        name="finish",
    )(at, received)


def local(out_grad, grid_state, tend_rate, legendre_basis, wave_slot):
    lats, lons = out_grad.shape[1:]
    slot_dev, degs = legendre_basis.shape[1:]
    x, zq = lax.axis_index("x"), lax.axis_index("zq")
    wave, lev = lax.axis_index("wave"), lax.axis_index("lev")

    to, source = (
        wave ^ jnp.where(wave % 2 == 0, *(jnp.array(row, jnp.int32) for row in table))
        for table in (TO, FROM)
    )

    def swapped(blocks):
        return [blocks[0]] + [
            lax.ppermute(blocks[k], "wave", [(w, w ^ TO[w % 2][k]) for w in range(8)])
            for k in range(1, 8)
        ]

    def own(table):
        return jnp.where(wave % 2 == 0, *(jnp.array(row, jnp.int32) for row in table))

    basis_at, four_at, last_at = own(BASIS_AT), own(FOUR_AT), own(LAST_AT)
    beside = tuple(
        [four[2 * basis.index(j) + lev] for j in range(8) for lev in range(2)]
        for basis, four in zip(BASIS_AT, FOUR_AT)
    )

    basis, token = basis_blocks(lev.astype(jnp.int32)[None], basis_at, legendre_basis)
    grads = gradient(to, tend_rate, out_grad, grid_state, token)
    basis = exchange(basis, BASIS_AT, ("x", "zq"))
    grads = swapped(grads)
    table = wave_table(wave_slot.reshape(8, slot_dev)[to], source, lons, 64)
    blocks = swapped(fourier_rows(table, grads))
    fourier = exchange(turn(source, four_at, basis, blocks), FOUR_AT, ("x", "zq", "lev"))

    first = wave * slot_dev + 8 * lev + 2 * x + zq
    slots = jnp.take(wave_slot, first + 16 * jnp.arange(slot_dev // 16, dtype=jnp.int32))
    parts = spectral_parts(slots, own(beside), last_at, fourier, basis)
    parts = exchange(parts, LAST_AT, ("x", "zp", "zq", "lev"))
    return finish(last_at, parts).reshape(degs // 16, 2, 32, slot_dev)


def solution(mesh):
    fine = Mesh(mesh.devices.reshape(4, 2, 2, *mesh.devices.shape[1:]), AXES)
    lat = ("x", "zp", "zq")
    in_specs = (P("lev", lat, "wave"), P("lev", lat, "wave"), P("lev"), P(lat, "wave", None), P())
    out_specs = P(lat, None, "lev", "wave")
    return jax.shard_map(local, mesh=fine, in_specs=in_specs, out_specs=out_specs, check_vma=False)
```

```python
import math

import jax
import jax.numpy as jnp
from jax import lax
from jax.experimental import pallas as pl
from jax.experimental.pallas import tpu as pltpu
from jax.sharding import Mesh, PartitionSpec as P

TO = ((0, 1, 2, 6, 4, 3, 7, 5), (0, 1, 6, 2, 4, 7, 3, 5))
FROM = ((0, 1, 2, 6, 4, 7, 3, 5), (0, 1, 6, 2, 4, 3, 7, 5))


AXES = ("x", "zp", "zq", "wave", "lev")
FAR_PAIR = tuple((dx, dz) for dz in range(2) for dx in (2, 1, 3, 0))
FAR_ALL = tuple((dx, dz) for dz in (0, 2, 1, 3) for dx in (2, 1, 3, 0))


def far_permute(block, dx, dz):
    def at(x, z, wave, lev):
        return ((x * 4 + z) * 8 + wave) * 2 + lev

    pairs = [
        (at(x, z, wave, lev), at((x + (1 - wave % 2 * 2) * dx) % 4, z ^ dz, wave, 1 - lev))
        for x in range(4)
        for z in range(4)
        for wave in range(8)
        for lev in range(2)
    ]
    return lax.ppermute(block, AXES, pairs)


def params(mib):
    return pltpu.CompilerParams(vmem_limit_bytes=mib * 1024 * 1024)


def cost(flops, moved, trans=0):
    return pl.CostEstimate(flops=flops, bytes_accessed=moved, transcendentals=trans)


def basis_kernel(lev_ref, basis_hbm, out_hbm, token_ref, in_buf, out_buf, in_sems, out_sems):
    steps, lats, _, degs = in_buf.shape
    lev = lev_ref[0]
    half = lats // 32 * 16
    reads = [
        [
            pltpu.make_async_copy(
                basis_hbm.at[part, 2 * b + lev], in_buf.at[b, part], in_sems.at[b, i]
            )
            for i, part in enumerate((pl.ds(0, half), pl.ds(half, lats - half)))
        ]
        for b in range(steps)
    ]
    for read in sum(reads, []):
        read.start()
    row = lax.broadcasted_iota(jnp.int32, (128, 128), 0)
    col = lax.broadcasted_iota(jnp.int32, (128, 128), 1)
    swap = (col == row % 16 * 8 + row // 16).astype(jnp.bfloat16)
    token_ref[...] = jnp.zeros_like(token_ref)
    writes = []
    for b in range(steps):
        for read in reads[b]:
            read.wait()
        for g in range(lats // 16):
            block = in_buf[b, 16 * g : 16 * g + 16].astype(jnp.float32).reshape(128, degs)
            turned = jnp.dot(swap, block.astype(jnp.bfloat16), preferred_element_type=jnp.float32)
            out_buf[b, :, 16 * g : 16 * g + 16, :] = turned.astype(jnp.bfloat16).reshape(
                8, 16, degs
            )
        for i in range(2):
            part = pl.ds(4 * i, 4)
            write = pltpu.make_async_copy(
                out_buf.at[b, part], out_hbm.at[part, b], out_sems.at[b, i]
            )
            write.start()
            writes.append(write)
    for write in writes:
        write.wait()


def basis_blocks(lev, basis):
    lats, slots, degs = basis.shape
    steps = slots // 16
    hbm = pl.BlockSpec(memory_space=pltpu.HBM)
    return pl.pallas_call(
        basis_kernel,
        in_specs=[pl.BlockSpec(memory_space=pltpu.SMEM), hbm],
        out_specs=[hbm, pl.BlockSpec(memory_space=pltpu.VMEM)],
        out_shape=[
            jax.ShapeDtypeStruct((8, steps, lats, degs), jnp.bfloat16),
            jax.ShapeDtypeStruct((8, 128), jnp.float32),
        ],
        scratch_shapes=[
            pltpu.VMEM((steps, lats, 8, degs), jnp.bfloat16),
            pltpu.VMEM((steps, 8, lats, degs), jnp.bfloat16),
            pltpu.SemaphoreType.DMA((steps, 2)),
            pltpu.SemaphoreType.DMA((steps, 2)),
        ],
        compiler_params=params(60),
        cost_estimate=cost(0, 2 * lats * slots * degs),
        name="basis_blocks",
    )(lev, basis.reshape(lats, slots // 8, 8, degs))


def grad_kernel(wave_ref, rate_ref, grad_any, state_any, _, *refs):
    outs, (grad_buf, state_buf, sems) = refs[:8], refs[8:]
    lons = grad_buf.shape[-1]
    copies = []
    for k in range(8):
        to = wave_ref[k]
        copies.append(
            (
                pltpu.make_async_copy(grad_any.at[:, to], grad_buf.at[k], sems.at[0, k]),
                pltpu.make_async_copy(state_any.at[:, to], state_buf.at[k], sems.at[1, k]),
            )
        )
    for pair in copies:
        pair[0].start()
        pair[1].start()
    for k in range(8):
        copies[k][0].wait()
        copies[k][1].wait()
        for c in range(4):
            slope = 1.0 - jnp.tanh(state_buf[k, c].astype(jnp.float32)) ** 2
            rate = rate_ref[8 * c + wave_ref[k]]
            value = grad_buf[k, c].astype(jnp.float32) * (1.0 + rate * slope)
            outs[k][c // 2, :, pl.ds((c % 2) * lons, lons)] = value.astype(jnp.bfloat16)


def gradient(to, rate, grad, state, after):
    chans, lats, lons = grad.shape
    four = (4, chans // 4, lats, lons)
    smem, anywhere = pl.BlockSpec(memory_space=pltpu.SMEM), pl.BlockSpec(memory_space=pl.ANY)
    buffer = pltpu.VMEM((8, 4, lats, lons), jnp.bfloat16)
    return pl.pallas_call(
        grad_kernel,
        in_specs=[smem, smem, anywhere, anywhere, pl.BlockSpec(memory_space=pltpu.VMEM)],
        out_shape=[jax.ShapeDtypeStruct((2, lats, 2 * lons), jnp.bfloat16)] * 8,
        scratch_shapes=[buffer, buffer, pltpu.SemaphoreType.DMA((2, 8))],
        compiler_params=params(60),
        cost_estimate=cost(6 * grad.size, 6 * grad.size, grad.size),
        name="gradient",
    )(to, rate, grad.reshape(four), state.reshape(four), after)


def table_kernel(coarse_cos, coarse_sin, fine_cos, fine_sin, out_ref):
    fine = fine_cos.shape[0]
    for j in range(coarse_cos.shape[0]):
        cos, sin = coarse_cos[j : j + 1, :], coarse_sin[j : j + 1, :]
        out_ref[0, j * fine : (j + 1) * fine, :] = (
            cos * fine_cos[...] - sin * fine_sin[...]
        ).astype(jnp.bfloat16)


def wave_table(slots, blocks, lons, fine):
    lon_total = 8 * lons
    quarter = jnp.array([0, lon_total // 4], jnp.int32)[None, :, None]
    phase = jnp.broadcast_to(quarter, (8, 2, slots.shape[1])).reshape(1, -1)
    slot = jnp.broadcast_to(slots[:, None, :], (8, 2, slots.shape[1])).reshape(1, -1)

    def trig(lon, shift):
        index = (slot * lon[:, None] + shift) % lon_total
        angle = index.astype(jnp.float32) * (2.0 * math.pi / lon_total)
        return jnp.cos(angle), jnp.sin(angle)

    starts = blocks[:, None] * lons + fine * jnp.arange(lons // fine, dtype=jnp.int32)[None, :]
    coarse_cos, coarse_sin = trig(starts.reshape(-1), 0)
    fine_cos, fine_sin = trig(jnp.arange(fine, dtype=jnp.int32), phase)
    scale = 1.0 / math.sqrt(lon_total)
    columns = slot.shape[1]
    part = lambda a: pl.BlockSpec((a.shape[0], 256), lambda j: (0, j))
    return pl.pallas_call(
        table_kernel,
        grid=(columns // 256,),
        in_specs=[part(a) for a in (coarse_cos, coarse_sin, fine_cos, fine_sin)],
        out_specs=pl.BlockSpec((1, lon_total, 256), lambda j: (j, 0, 0)),
        out_shape=jax.ShapeDtypeStruct((columns // 256, lon_total, 256), jnp.bfloat16),
        compiler_params=params(12),
        cost_estimate=cost(3 * columns * lon_total, 2 * columns * lon_total),
        name="wave_table",
    )(coarse_cos * scale, coarse_sin * scale, fine_cos, fine_sin)


def fourier_kernel(table_ref, *refs):
    grads, outs, rows = refs[:8], refs[8:16], refs[16]
    lats, lons = grads[0].shape[1], grads[0].shape[2] // 2
    for k in range(8):
        for c in range(4):
            rows[pl.ds(c * lats, lats), pl.ds(k * lons, lons)] = grads[k][
                c // 2, :, pl.ds((c % 2) * lons, lons)
            ]
    width, slots = 4 * lats, outs[0].shape[0]
    for step in range(16 * slots // 256):
        value = jnp.dot(rows[...], table_ref[step], preferred_element_type=jnp.float32).T
        first, stop = 256 * step, 256 * step + 256
        for kp in range(first // slots, -(-stop // slots)):
            low, high = max(first, kp * slots), min(stop, (kp + 1) * slots)
            outs[kp // 2][low - kp * slots : high - kp * slots, pl.ds(kp % 2 * width, width)] = (
                value[low - first : high - first].astype(jnp.bfloat16)
            )


def fourier_rows(table, grads):
    _, lats, lons2 = grads[0].shape
    steps, lon_total, _ = table.shape
    slots = steps * 256 // 16
    return pl.pallas_call(
        fourier_kernel,
        in_specs=[pl.BlockSpec(memory_space=pltpu.VMEM)] * 9,
        out_shape=[jax.ShapeDtypeStruct((slots, 8 * lats), jnp.bfloat16)] * 8,
        scratch_shapes=[pltpu.VMEM((4 * lats, lon_total), jnp.bfloat16)],
        compiler_params=params(24),
        cost_estimate=cost(2 * steps * 256 * lon_total * 4 * lats, 2 * table.size),
        name="fourier_rows",
    )(table, *grads)


def turn_kernel(wave_ref, to_ref, lev_ref, _, *refs):
    blocks, near_ref, far_refs, (rows, buf) = refs[:8], refs[8], refs[9:17], refs[17:]
    slots, width = blocks[0].shape
    lev = lev_ref[0]
    for t in range(width // 128):
        lanes = slice(128 * t, 128 * t + 128)
        for k in range(8):
            start = pl.multiple_of(wave_ref[k] * slots, 8)
            rows[t, pl.ds(start, slots), :] = blocks[k][:, lanes].astype(jnp.float32)
        for s in range(slots):
            b, half, r = s // 16, s // 8 % 2, s % 8
            buf[half, r, b, :, lanes] = rows[t, pl.ds(s, 8, stride=slots), :].astype(jnp.bfloat16)
    for r in range(8):
        near_ref[r] = buf[lev, r]
        far_refs[r][...] = buf[1 - lev, to_ref[r]]


def turn(waves, to, lev, after, blocks):
    slots, width = blocks[0].shape
    vmem, smem = pl.BlockSpec(memory_space=pltpu.VMEM), pl.BlockSpec(memory_space=pltpu.SMEM)
    far = jax.ShapeDtypeStruct((slots // 16, 8, width), jnp.bfloat16)
    near = jax.ShapeDtypeStruct((8, *far.shape), jnp.bfloat16)
    near, *far = pl.pallas_call(
        turn_kernel,
        in_specs=[smem, smem, smem, pl.BlockSpec(memory_space=pl.ANY)] + [vmem] * 8,
        out_shape=[near] + [far] * 8,
        scratch_shapes=[
            pltpu.VMEM((width // 128, 8 * slots, 128), jnp.float32),
            pltpu.VMEM((2, *near.shape), jnp.bfloat16),
        ],
        compiler_params=params(12),
        cost_estimate=cost(0, 32 * blocks[0].size),
        name="turn",
    )(waves, to, lev, after, *blocks)
    return near, far


def spectral_kernel(slot_ref, from_ref, to_ref, basis_any, near_ref, *refs):
    far_refs, near_out, far_outs = refs[:8], refs[8], refs[9:25]
    far_ref, far_out, basis, left, total, sems = refs[25:]
    steps, _, lats, degs = basis.shape
    deg_dev = degs // 16
    copies = [
        pltpu.make_async_copy(basis_any.at[:, b], basis.at[b], sems.at[b]) for b in range(steps)
    ]
    for copy in copies:
        copy.start()
    for j in range(8):
        far_ref[from_ref[j]] = far_refs[j][...]

    def summed(b):
        for q in range(8):
            for half, source in enumerate((near_ref, far_ref)):
                block = source[q, b].astype(jnp.float32)
                for seg in range(8):
                    left[pl.ds(64 * half + 8 * seg, 8), pl.ds(q * lats, lats)] = block[
                        :, seg * lats : (seg + 1) * lats
                    ]
        copies[b].wait()
        value = jnp.dot(
            left[...].astype(jnp.bfloat16),
            basis[b].reshape(8 * lats, degs),
            preferred_element_type=jnp.float32,
        )
        degree = lax.broadcasted_iota(jnp.int32, value.shape, 1)
        return jnp.where(degree >= slot_ref[b], value, 0.0)

    outs = (near_out, far_out)
    for k in range(2):
        even, odd = summed(2 * k), summed(2 * k + 1)
        for half in range(2):
            rows = slice(64 * half, 64 * half + 64)
            both = jnp.concatenate([even[rows], odd[rows]], 0).T
            for a in range(16):
                outs[half][a, pl.ds(k * deg_dev, deg_dev)] = both[
                    a * deg_dev : (a + 1) * deg_dev
                ].astype(jnp.bfloat16)
    total[...] = summed(4).T
    fold = deg_dev // 2
    even = total[pl.ds(0, degs // 2, stride=2), :]
    odd = total[pl.ds(1, degs // 2, stride=2), :]
    low = lax.broadcasted_iota(jnp.int32, even.shape, 1) < 64
    pair = (
        jnp.where(low, even, pltpu.roll(odd, 64, 1)),
        jnp.where(low, pltpu.roll(even, 64, 1), odd),
    )
    rows = 5 * fold
    for half in range(2):
        for a in range(16):
            outs[half][a, pl.ds(2 * deg_dev, fold)] = pair[half][
                a * fold : (a + 1) * fold
            ].astype(jnp.bfloat16)
            outs[half][a, pl.ds(rows, near_out.shape[1] - rows)] = jnp.zeros(
                (near_out.shape[1] - rows, 128), jnp.bfloat16
            )
    for j in range(16):
        far_outs[j][...] = far_out[to_ref[j]]


def spectral_parts(slots, source, to, basis, near, far):
    _, steps, lats, degs = basis.shape
    vmem, smem = pl.BlockSpec(memory_space=pltpu.VMEM), pl.BlockSpec(memory_space=pltpu.SMEM)
    message = jax.ShapeDtypeStruct((104, 128), jnp.bfloat16)
    messages = jax.ShapeDtypeStruct((16, *message.shape), jnp.bfloat16)
    near, *far = pl.pallas_call(
        spectral_kernel,
        in_specs=[smem, smem, smem, pl.BlockSpec(memory_space=pl.ANY)] + [vmem] * 9,
        out_shape=[messages] + [message] * 16,
        scratch_shapes=[
            pltpu.VMEM(near.shape, jnp.bfloat16),
            pltpu.VMEM(messages.shape, jnp.bfloat16),
            pltpu.VMEM((steps, 8, lats, degs), jnp.bfloat16),
            pltpu.VMEM((128, 8 * lats), jnp.float32),
            pltpu.VMEM((degs, 128), jnp.float32),
            pltpu.SemaphoreType.DMA((steps,)),
        ],
        compiler_params=params(16),
        cost_estimate=cost(5 * 2 * 128 * 8 * lats * degs, 2 * basis.size + 4 * near.size),
        name="spectral_parts",
    )(slots, source, to, basis, near, *far)
    return near, far


def finish_kernel(lev_ref, from_ref, near_ref, *refs):
    far_refs, out_ref, rows = refs[:16], refs[16], refs[17]
    depth = near_ref.shape[1]
    mine = lev_ref[0] * 8
    for x in range(4):
        for zq in range(2):
            first = near_ref[4 * x + zq].astype(jnp.float32)
            second = near_ref[4 * x + 2 + zq].astype(jnp.float32)
            start = pl.multiple_of((mine + 2 * x + zq) * depth, 8)
            rows[pl.ds(start, depth), :] = first + second
    for j, (dx, dz) in enumerate(FAR_ALL):
        if dz < 2:
            first = far_refs[j][...].astype(jnp.float32)
            second = far_refs[FAR_ALL.index((dx, dz ^ 2))][...].astype(jnp.float32)
            start = pl.multiple_of((8 - mine + from_ref[j]) * depth, 8)
            rows[pl.ds(start, depth), :] = first + second
    low = lax.broadcasted_iota(jnp.int32, (16, 128), 1) < 64
    for n in range(0, 40, 2):
        parts = []
        for k in range(2):
            one = rows[pl.ds(40 * k + n, 16, stride=depth), :]
            two = rows[pl.ds(40 * k + n + 1, 16, stride=depth), :]
            parts.append(jnp.where(low, one, pltpu.roll(two, 64, 1)))
            parts.append(jnp.where(low, pltpu.roll(one, 64, 1), two))
        parts.append(rows[pl.ds(80 + n // 2, 16, stride=depth), :])
        out_ref[pl.ds(64 * n, 128), :] = jnp.concatenate(parts, 0).T


def finish(lev, source, near, far):
    vmem, smem = pl.BlockSpec(memory_space=pltpu.VMEM), pl.BlockSpec(memory_space=pltpu.SMEM)
    return pl.pallas_call(
        finish_kernel,
        in_specs=[smem, smem] + [vmem] * 17,
        out_shape=jax.ShapeDtypeStruct((40 * 64, 80), jnp.float32),
        scratch_shapes=[pltpu.VMEM((16 * near.shape[1], 128), jnp.float32)],
        compiler_params=params(12),
        cost_estimate=cost(2 * near.size, 4 * near.size + 4 * 40 * 64 * 128),
        name="finish",
    )(lev, source, near, *far)


def local(out_grad, grid_state, tend_rate, legendre_basis, wave_slot):
    lats, lons = out_grad.shape[1:]
    slot_dev, degs = legendre_basis.shape[1:]
    x, zq = lax.axis_index("x"), lax.axis_index("zq")
    wave, lev = lax.axis_index("wave"), lax.axis_index("lev")

    to, source = (
        wave ^ jnp.where(wave % 2 == 0, *(jnp.array(row, jnp.int32) for row in table))
        for table in (TO, FROM)
    )

    def swapped(blocks):
        return [blocks[0]] + [
            lax.ppermute(blocks[k], "wave", [(w, w ^ TO[w % 2][k]) for w in range(8)])
            for k in range(1, 8)
        ]

    lev = lev.astype(jnp.int32)[None]
    basis, token = basis_blocks(lev, legendre_basis)
    grads = gradient(to, tend_rate, out_grad, grid_state, token)
    basis = lax.all_to_all(basis, ("x", "zq"), 0, 0, tiled=True)
    grads = swapped(grads)
    table = wave_table(wave_slot.reshape(8, slot_dev)[to], source, lons, 64)
    blocks = swapped(fourier_rows(table, grads))

    way = 1 - wave % 2 * 2
    pair_to, pair_from = (
        jnp.stack([(x + sign * way * dx) % 4 * 2 + (zq ^ dz) for dx, dz in FAR_PAIR])
        for sign in (1, -1)
    )
    near, far = turn(source, pair_to, lev, basis, blocks)
    near = lax.all_to_all(near, ("x", "zq"), 0, 0, tiled=True)
    far = [far_permute(block, *offset) for offset, block in zip(FAR_PAIR, far)]

    z = 2 * lax.axis_index("zp") + zq
    all_to = jnp.stack([(x + way * dx) % 4 * 4 + (z ^ dz) for dx, dz in FAR_ALL])
    all_from = jnp.stack([(x - way * dx) % 4 * 2 + ((z ^ dz) & 1) for dx, dz in FAR_ALL])
    first = wave * slot_dev + 8 * lev[0] + 2 * x + zq
    slots = jnp.take(wave_slot, first + 16 * jnp.arange(slot_dev // 16, dtype=jnp.int32))
    near, far = spectral_parts(slots, pair_from, all_to, basis, near, far)
    near = lax.all_to_all(near, ("x", "zp", "zq"), 0, 0, tiled=True)
    far = [far_permute(block, *offset) for offset, block in zip(FAR_ALL, far)]
    return finish(lev, all_from, near, far).reshape(degs // 16, 2, 32, slot_dev)


def solution(mesh):
    fine = Mesh(mesh.devices.reshape(4, 2, 2, *mesh.devices.shape[1:]), AXES)
    lat = ("x", "zp", "zq")
    in_specs = (P("lev", lat, "wave"), P("lev", lat, "wave"), P("lev"), P(lat, "wave", None), P())
    out_specs = P(lat, None, "lev", "wave")
    return jax.shard_map(local, mesh=fine, in_specs=in_specs, out_specs=out_specs, check_vma=False)
```

```python
import math

import jax
import jax.numpy as jnp
from jax import lax
from jax.experimental import pallas as pl
from jax.experimental.pallas import tpu as pltpu
from jax.sharding import Mesh, PartitionSpec as P

TO = ((0, 1, 2, 6, 4, 3, 7, 5), (0, 1, 6, 2, 4, 7, 3, 5))
FROM = ((0, 1, 2, 6, 4, 7, 3, 5), (0, 1, 6, 2, 4, 3, 7, 5))


def params(mib):
    return pltpu.CompilerParams(vmem_limit_bytes=mib * 1024 * 1024)


def cost(flops, moved, trans=0):
    return pl.CostEstimate(flops=flops, bytes_accessed=moved, transcendentals=trans)


def basis_kernel(lev_ref, basis_hbm, out_hbm, token_ref, in_buf, out_buf, in_sems, out_sems):
    steps, lats, _, degs = in_buf.shape
    lev = lev_ref[0]
    reads = [
        pltpu.make_async_copy(basis_hbm.at[:, 2 * b + lev], in_buf.at[b], in_sems.at[b])
        for b in range(steps)
    ]
    for read in reads:
        read.start()
    row = lax.broadcasted_iota(jnp.int32, (128, 128), 0)
    col = lax.broadcasted_iota(jnp.int32, (128, 128), 1)
    swap = (col == row % 16 * 8 + row // 16).astype(jnp.bfloat16)
    token_ref[...] = jnp.zeros_like(token_ref)
    writes = []
    for b in range(steps):
        reads[b].wait()
        for g in range(lats // 16):
            block = in_buf[b, 16 * g : 16 * g + 16].astype(jnp.float32).reshape(128, degs)
            turned = jnp.dot(swap, block.astype(jnp.bfloat16), preferred_element_type=jnp.float32)
            out_buf[b, :, 16 * g : 16 * g + 16, :] = turned.astype(jnp.bfloat16).reshape(
                8, 16, degs
            )
        writes.append(pltpu.make_async_copy(out_buf.at[b], out_hbm.at[:, b], out_sems.at[b]))
        writes[b].start()
    for write in writes:
        write.wait()


def basis_blocks(lev, basis):
    lats, slots, degs = basis.shape
    steps = slots // 16
    hbm = pl.BlockSpec(memory_space=pltpu.HBM)
    return pl.pallas_call(
        basis_kernel,
        in_specs=[pl.BlockSpec(memory_space=pltpu.SMEM), hbm],
        out_specs=[hbm, pl.BlockSpec(memory_space=pltpu.VMEM)],
        out_shape=[
            jax.ShapeDtypeStruct((8, steps, lats, degs), jnp.bfloat16),
            jax.ShapeDtypeStruct((8, 128), jnp.float32),
        ],
        scratch_shapes=[
            pltpu.VMEM((steps, lats, 8, degs), jnp.bfloat16),
            pltpu.VMEM((steps, 8, lats, degs), jnp.bfloat16),
            pltpu.SemaphoreType.DMA((steps,)),
            pltpu.SemaphoreType.DMA((steps,)),
        ],
        compiler_params=params(60),
        cost_estimate=cost(0, 2 * lats * slots * degs),
        name="basis_blocks",
    )(lev, basis.reshape(lats, slots // 8, 8, degs))


def grad_kernel(wave_ref, rate_ref, grad_ref, state_ref, _, *outs):
    lons = grad_ref.shape[-1]
    for k in range(8):
        to = wave_ref[k]
        for c in range(4):
            slope = 1.0 - jnp.tanh(state_ref[c, to].astype(jnp.float32)) ** 2
            value = grad_ref[c, to].astype(jnp.float32) * (1.0 + rate_ref[8 * c + to] * slope)
            outs[k][c // 2, :, pl.ds((c % 2) * lons, lons)] = value.astype(jnp.bfloat16)


def gradient(to, rate, grad, state, after):
    chans, lats, lons = grad.shape
    four = (4, chans // 4, lats, lons)
    smem, vmem = pl.BlockSpec(memory_space=pltpu.SMEM), pl.BlockSpec(memory_space=pltpu.VMEM)
    return pl.pallas_call(
        grad_kernel,
        in_specs=[smem, smem, vmem, vmem, vmem],
        out_shape=[jax.ShapeDtypeStruct((2, lats, 2 * lons), jnp.bfloat16)] * 8,
        compiler_params=params(16),
        cost_estimate=cost(6 * grad.size, 6 * grad.size, grad.size),
        name="gradient",
    )(to, rate, grad.reshape(four), state.reshape(four), after)


def table_kernel(coarse_cos, coarse_sin, fine_cos, fine_sin, out_ref):
    fine = fine_cos.shape[0]
    for j in range(coarse_cos.shape[0]):
        cos, sin = coarse_cos[j : j + 1, :], coarse_sin[j : j + 1, :]
        out_ref[0, j * fine : (j + 1) * fine, :] = (
            cos * fine_cos[...] - sin * fine_sin[...]
        ).astype(jnp.bfloat16)


def wave_table(slots, blocks, lons, fine):
    lon_total = 8 * lons
    quarter = jnp.array([0, lon_total // 4], jnp.int32)[None, :, None]
    phase = jnp.broadcast_to(quarter, (8, 2, slots.shape[1])).reshape(1, -1)
    slot = jnp.broadcast_to(slots[:, None, :], (8, 2, slots.shape[1])).reshape(1, -1)

    def trig(lon, shift):
        index = (slot * lon[:, None] + shift) % lon_total
        angle = index.astype(jnp.float32) * (2.0 * math.pi / lon_total)
        return jnp.cos(angle), jnp.sin(angle)

    starts = blocks[:, None] * lons + fine * jnp.arange(lons // fine, dtype=jnp.int32)[None, :]
    coarse_cos, coarse_sin = trig(starts.reshape(-1), 0)
    fine_cos, fine_sin = trig(jnp.arange(fine, dtype=jnp.int32), phase)
    scale = 1.0 / math.sqrt(lon_total)
    columns = slot.shape[1]
    part = lambda a: pl.BlockSpec((a.shape[0], 256), lambda j: (0, j))
    return pl.pallas_call(
        table_kernel,
        grid=(columns // 256,),
        in_specs=[part(a) for a in (coarse_cos, coarse_sin, fine_cos, fine_sin)],
        out_specs=pl.BlockSpec((1, lon_total, 256), lambda j: (j, 0, 0)),
        out_shape=jax.ShapeDtypeStruct((columns // 256, lon_total, 256), jnp.bfloat16),
        compiler_params=params(12),
        cost_estimate=cost(3 * columns * lon_total, 2 * columns * lon_total),
        name="wave_table",
    )(coarse_cos * scale, coarse_sin * scale, fine_cos, fine_sin)


def fourier_kernel(table_ref, *refs):
    grads, outs, rows = refs[:8], refs[8:16], refs[16]
    lats, lons = grads[0].shape[1], grads[0].shape[2] // 2
    for k in range(8):
        for c in range(4):
            rows[pl.ds(c * lats, lats), pl.ds(k * lons, lons)] = grads[k][
                c // 2, :, pl.ds((c % 2) * lons, lons)
            ]
    width, slots = 4 * lats, outs[0].shape[0]
    for step in range(16 * slots // 256):
        value = jnp.dot(rows[...], table_ref[step], preferred_element_type=jnp.float32).T
        first, stop = 256 * step, 256 * step + 256
        for kp in range(first // slots, -(-stop // slots)):
            low, high = max(first, kp * slots), min(stop, (kp + 1) * slots)
            outs[kp // 2][low - kp * slots : high - kp * slots, pl.ds(kp % 2 * width, width)] = (
                value[low - first : high - first].astype(jnp.bfloat16)
            )


def fourier_rows(table, grads):
    _, lats, lons2 = grads[0].shape
    steps, lon_total, _ = table.shape
    slots = steps * 256 // 16
    return pl.pallas_call(
        fourier_kernel,
        in_specs=[pl.BlockSpec(memory_space=pltpu.VMEM)] * 9,
        out_shape=[jax.ShapeDtypeStruct((slots, 8 * lats), jnp.bfloat16)] * 8,
        scratch_shapes=[pltpu.VMEM((4 * lats, lon_total), jnp.bfloat16)],
        compiler_params=params(24),
        cost_estimate=cost(2 * steps * 256 * lon_total * 4 * lats, 2 * table.size),
        name="fourier_rows",
    )(table, *grads)


def turn_kernel(wave_ref, *refs):
    blocks, (out_ref, rows) = refs[:8], refs[8:]
    slots, width = blocks[0].shape
    for t in range(width // 128):
        lanes = slice(128 * t, 128 * t + 128)
        for k in range(8):
            start = pl.multiple_of(wave_ref[k] * slots, 8)
            rows[t, pl.ds(start, slots), :] = blocks[k][:, lanes].astype(jnp.float32)
        for s in range(slots):
            b, lev, r = s // 16, s // 8 % 2, s % 8
            out_ref[2 * r + lev, b, :, lanes] = rows[t, pl.ds(s, 8, stride=slots), :].astype(
                jnp.bfloat16
            )


def turn(waves, blocks):
    slots, width = blocks[0].shape
    vmem = pl.BlockSpec(memory_space=pltpu.VMEM)
    return pl.pallas_call(
        turn_kernel,
        in_specs=[pl.BlockSpec(memory_space=pltpu.SMEM)] + [vmem] * 8,
        out_shape=jax.ShapeDtypeStruct((16, slots // 16, 8, width), jnp.bfloat16),
        scratch_shapes=[pltpu.VMEM((width // 128, 8 * slots, 128), jnp.float32)],
        compiler_params=params(12),
        cost_estimate=cost(0, 32 * blocks[0].size),
        name="turn",
    )(waves, *blocks)


def spectral_kernel(slot_ref, four_ref, head_ref, basis_any, out_ref, basis, left, total, sems):
    steps, _, lats, degs = basis.shape
    deg_dev = degs // 16
    head = head_ref.shape[1]
    copies = [
        pltpu.make_async_copy(basis_any.at[:, b], basis.at[b], sems.at[b])
        for b in range(head, steps)
    ]
    for copy in copies:
        copy.start()

    def summed(b):
        for q in range(8):
            for lev in range(2):
                block = four_ref[2 * q + lev, b].astype(jnp.float32)
                for seg in range(8):
                    left[pl.ds(64 * lev + 8 * seg, 8), pl.ds(q * lats, lats)] = block[
                        :, seg * lats : (seg + 1) * lats
                    ]
        if b >= head:
            copies[b - head].wait()
            blocks = basis[b]
        else:
            blocks = head_ref[:, b]
        value = jnp.dot(
            left[...].astype(jnp.bfloat16),
            blocks.reshape(8 * lats, degs),
            preferred_element_type=jnp.float32,
        )
        degree = lax.broadcasted_iota(jnp.int32, value.shape, 1)
        return jnp.where(degree >= slot_ref[b], value, 0.0)

    for k in range(2):
        even, odd = summed(2 * k), summed(2 * k + 1)
        for lev in range(2):
            rows = slice(64 * lev, 64 * lev + 64)
            both = jnp.concatenate([even[rows], odd[rows]], 0).T
            for a in range(16):
                out_ref[2 * a + lev, pl.ds(k * deg_dev, deg_dev)] = both[
                    a * deg_dev : (a + 1) * deg_dev
                ].astype(jnp.bfloat16)
    total[...] = summed(4).T
    half = deg_dev // 2
    even = total[pl.ds(0, degs // 2, stride=2), :]
    odd = total[pl.ds(1, degs // 2, stride=2), :]
    low = lax.broadcasted_iota(jnp.int32, even.shape, 1) < 64
    pair = (
        jnp.where(low, even, pltpu.roll(odd, 64, 1)),
        jnp.where(low, pltpu.roll(even, 64, 1), odd),
    )
    for a in range(16):
        for lev in range(2):
            out_ref[2 * a + lev, pl.ds(2 * deg_dev, half)] = pair[lev][
                a * half : (a + 1) * half
            ].astype(jnp.bfloat16)
    rows = 5 * half
    for a in range(32):
        out_ref[a, pl.ds(rows, out_ref.shape[1] - rows)] = jnp.zeros(
            (out_ref.shape[1] - rows, 128), jnp.bfloat16
        )


def spectral_parts(slots, fourier, head, basis):
    _, steps, lats, degs = basis.shape
    vmem, smem = pl.BlockSpec(memory_space=pltpu.VMEM), pl.BlockSpec(memory_space=pltpu.SMEM)
    return pl.pallas_call(
        spectral_kernel,
        in_specs=[smem, vmem, vmem, pl.BlockSpec(memory_space=pl.ANY)],
        out_shape=jax.ShapeDtypeStruct((32, 104, 128), jnp.bfloat16),
        scratch_shapes=[
            pltpu.VMEM((steps, 8, lats, degs), jnp.bfloat16),
            pltpu.VMEM((128, 8 * lats), jnp.float32),
            pltpu.VMEM((degs, 128), jnp.float32),
            pltpu.SemaphoreType.DMA((steps,)),
        ],
        compiler_params=params(16),
        cost_estimate=cost(5 * 2 * 128 * 8 * lats * degs, 2 * basis.size + 2 * fourier.size),
        name="spectral_parts",
    )(slots, fourier, head, basis)


def finish_kernel(in_ref, out_ref, rows):
    depth = in_ref.shape[1]
    for x in range(4):
        for zq in range(2):
            for lev in range(2):
                first = in_ref[8 * x + 2 * zq + lev].astype(jnp.float32)
                second = in_ref[8 * x + 4 + 2 * zq + lev].astype(jnp.float32)
                rows[pl.ds((8 * lev + 2 * x + zq) * depth, depth), :] = first + second
    low = lax.broadcasted_iota(jnp.int32, (16, 128), 1) < 64
    for n in range(0, 40, 2):
        parts = []
        for k in range(2):
            one = rows[pl.ds(40 * k + n, 16, stride=depth), :]
            two = rows[pl.ds(40 * k + n + 1, 16, stride=depth), :]
            parts.append(jnp.where(low, one, pltpu.roll(two, 64, 1)))
            parts.append(jnp.where(low, pltpu.roll(one, 64, 1), two))
        parts.append(rows[pl.ds(80 + n // 2, 16, stride=depth), :])
        out_ref[pl.ds(64 * n, 128), :] = jnp.concatenate(parts, 0).T


def finish(received):
    return pl.pallas_call(
        finish_kernel,
        out_shape=jax.ShapeDtypeStruct((40 * 64, 80), jnp.float32),
        scratch_shapes=[pltpu.VMEM((16 * received.shape[1], 128), jnp.float32)],
        compiler_params=params(12),
        cost_estimate=cost(received.size, 2 * received.size + 4 * 40 * 64 * 128),
        name="finish",
    )(received)


def local(out_grad, grid_state, tend_rate, legendre_basis, wave_slot):
    lats, lons = out_grad.shape[1:]
    slot_dev, degs = legendre_basis.shape[1:]
    x, zq = lax.axis_index("x"), lax.axis_index("zq")
    wave, lev = lax.axis_index("wave"), lax.axis_index("lev")

    to, source = (
        wave ^ jnp.where(wave % 2 == 0, *(jnp.array(row, jnp.int32) for row in table))
        for table in (TO, FROM)
    )

    def swapped(blocks):
        return [blocks[0]] + [
            lax.ppermute(blocks[k], "wave", [(w, w ^ TO[w % 2][k]) for w in range(8)])
            for k in range(1, 8)
        ]

    basis, token = basis_blocks(lev.astype(jnp.int32)[None], legendre_basis)
    grads = gradient(to, tend_rate, out_grad, grid_state, token)
    basis = lax.all_to_all(basis, ("x", "zq"), 0, 0, tiled=True)
    grads = swapped(grads)
    table = wave_table(wave_slot.reshape(8, slot_dev)[to], source, lons, 64)
    blocks = swapped(fourier_rows(table, grads))
    fourier, basis = lax.optimization_barrier((turn(source, blocks), basis))
    fourier = lax.all_to_all(fourier, ("x", "zq", "lev"), 0, 0, tiled=True)

    first = wave * slot_dev + 8 * lev + 2 * x + zq
    slots = jnp.take(wave_slot, first + 16 * jnp.arange(slot_dev // 16, dtype=jnp.int32))
    parts = spectral_parts(slots, fourier, basis[:, :2], basis)
    parts = lax.all_to_all(parts, ("x", "zp", "zq", "lev"), 0, 0, tiled=True)
    return finish(parts).reshape(degs // 16, 2, 32, slot_dev)


def solution(mesh):
    fine = Mesh(
        mesh.devices.reshape(4, 2, 2, *mesh.devices.shape[1:]), ("x", "zp", "zq", "wave", "lev")
    )
    lat = ("x", "zp", "zq")
    in_specs = (P("lev", lat, "wave"), P("lev", lat, "wave"), P("lev"), P(lat, "wave", None), P())
    out_specs = P(lat, None, "lev", "wave")
    return jax.shard_map(local, mesh=fine, in_specs=in_specs, out_specs=out_specs, check_vma=False)
```

```python
import math

import jax
import jax.numpy as jnp
from jax import lax
from jax.experimental import pallas as pl
from jax.experimental.pallas import tpu as pltpu
from jax.sharding import Mesh, PartitionSpec as P

TO = ((0, 1, 2, 6, 4, 3, 7, 5), (0, 1, 6, 2, 4, 7, 3, 5))
FROM = ((0, 1, 2, 6, 4, 7, 3, 5), (0, 1, 6, 2, 4, 3, 7, 5))


def params(mib):
    return pltpu.CompilerParams(vmem_limit_bytes=mib * 1024 * 1024)


def cost(flops, moved, trans=0):
    return pl.CostEstimate(flops=flops, bytes_accessed=moved, transcendentals=trans)


def basis_kernel(lev_ref, basis_hbm, out_hbm, token_ref, in_buf, out_buf, in_sems, out_sems):
    steps, lats, _, degs = in_buf.shape
    lev = lev_ref[0]
    reads = [
        pltpu.make_async_copy(basis_hbm.at[:, 2 * b + lev], in_buf.at[b], in_sems.at[b])
        for b in range(steps)
    ]
    for read in reads:
        read.start()
    row = lax.broadcasted_iota(jnp.int32, (128, 128), 0)
    col = lax.broadcasted_iota(jnp.int32, (128, 128), 1)
    swap = (col == row % 16 * 8 + row // 16).astype(jnp.bfloat16)
    token_ref[...] = jnp.zeros_like(token_ref)
    writes = []
    for b in range(steps):
        reads[b].wait()
        lanes = 384
        for g in range(lats // 16):
            part = slice(16 * g, 16 * g + 16)
            block = in_buf[b, part, :, :lanes].astype(jnp.float32).reshape(128, lanes)
            turned = jnp.dot(swap, block.astype(jnp.bfloat16), preferred_element_type=jnp.float32)
            out_buf[b, :, part, :lanes] = turned.astype(jnp.bfloat16).reshape(8, 16, lanes)
            other = jnp.swapaxes(in_buf[b, part, :, lanes:].astype(jnp.float32), 0, 1)
            out_buf[b, :, part, lanes:] = other.astype(jnp.bfloat16)
        writes.append(pltpu.make_async_copy(out_buf.at[b], out_hbm.at[:, b], out_sems.at[b]))
        writes[b].start()
    for write in writes:
        write.wait()


def basis_blocks(lev, basis):
    lats, slots, degs = basis.shape
    steps = slots // 16
    hbm = pl.BlockSpec(memory_space=pltpu.HBM)
    return pl.pallas_call(
        basis_kernel,
        in_specs=[pl.BlockSpec(memory_space=pltpu.SMEM), hbm],
        out_specs=[hbm, pl.BlockSpec(memory_space=pltpu.VMEM)],
        out_shape=[
            jax.ShapeDtypeStruct((8, steps, lats, degs), jnp.bfloat16),
            jax.ShapeDtypeStruct((8, 128), jnp.float32),
        ],
        scratch_shapes=[
            pltpu.VMEM((steps, lats, 8, degs), jnp.bfloat16),
            pltpu.VMEM((steps, 8, lats, degs), jnp.bfloat16),
            pltpu.SemaphoreType.DMA((steps,)),
            pltpu.SemaphoreType.DMA((steps,)),
        ],
        compiler_params=params(60),
        cost_estimate=cost(0, 2 * lats * slots * degs),
        name="basis_blocks",
    )(lev, basis.reshape(lats, slots // 8, 8, degs))


def grad_kernel(wave_ref, rate_ref, grad_ref, state_ref, _, *outs):
    lons = grad_ref.shape[-1]
    for k in range(8):
        to = wave_ref[k]
        for c in range(4):
            slope = 1.0 - jnp.tanh(state_ref[c, to].astype(jnp.float32)) ** 2
            value = grad_ref[c, to].astype(jnp.float32) * (1.0 + rate_ref[8 * c + to] * slope)
            outs[k][c // 2, :, pl.ds((c % 2) * lons, lons)] = value.astype(jnp.bfloat16)


def gradient(to, rate, grad, state, after):
    chans, lats, lons = grad.shape
    four = (4, chans // 4, lats, lons)
    smem, vmem = pl.BlockSpec(memory_space=pltpu.SMEM), pl.BlockSpec(memory_space=pltpu.VMEM)
    return pl.pallas_call(
        grad_kernel,
        in_specs=[smem, smem, vmem, vmem, vmem],
        out_shape=[jax.ShapeDtypeStruct((2, lats, 2 * lons), jnp.bfloat16)] * 8,
        compiler_params=params(16),
        cost_estimate=cost(6 * grad.size, 6 * grad.size, grad.size),
        name="gradient",
    )(to, rate, grad.reshape(four), state.reshape(four), after)


def table_kernel(coarse_cos, coarse_sin, fine_cos, fine_sin, out_ref):
    fine = fine_cos.shape[0]
    for j in range(coarse_cos.shape[0]):
        cos, sin = coarse_cos[j : j + 1, :], coarse_sin[j : j + 1, :]
        out_ref[0, j * fine : (j + 1) * fine, :] = (
            cos * fine_cos[...] - sin * fine_sin[...]
        ).astype(jnp.bfloat16)


def wave_table(slots, blocks, lons, fine):
    lon_total = 8 * lons
    quarter = jnp.array([0, lon_total // 4], jnp.int32)[None, :, None]
    phase = jnp.broadcast_to(quarter, (8, 2, slots.shape[1])).reshape(1, -1)
    slot = jnp.broadcast_to(slots[:, None, :], (8, 2, slots.shape[1])).reshape(1, -1)

    def trig(lon, shift):
        index = (slot * lon[:, None] + shift) % lon_total
        angle = index.astype(jnp.float32) * (2.0 * math.pi / lon_total)
        return jnp.cos(angle), jnp.sin(angle)

    starts = blocks[:, None] * lons + fine * jnp.arange(lons // fine, dtype=jnp.int32)[None, :]
    coarse_cos, coarse_sin = trig(starts.reshape(-1), 0)
    fine_cos, fine_sin = trig(jnp.arange(fine, dtype=jnp.int32), phase)
    scale = 1.0 / math.sqrt(lon_total)
    columns = slot.shape[1]
    part = lambda a: pl.BlockSpec((a.shape[0], 256), lambda j: (0, j))
    return pl.pallas_call(
        table_kernel,
        grid=(columns // 256,),
        in_specs=[part(a) for a in (coarse_cos, coarse_sin, fine_cos, fine_sin)],
        out_specs=pl.BlockSpec((1, lon_total, 256), lambda j: (j, 0, 0)),
        out_shape=jax.ShapeDtypeStruct((columns // 256, lon_total, 256), jnp.bfloat16),
        compiler_params=params(12),
        cost_estimate=cost(3 * columns * lon_total, 2 * columns * lon_total),
        name="wave_table",
    )(coarse_cos * scale, coarse_sin * scale, fine_cos, fine_sin)


def fourier_kernel(table_ref, *refs):
    grads, outs, rows = refs[:8], refs[8:16], refs[16]
    lats, lons = grads[0].shape[1], grads[0].shape[2] // 2
    for k in range(8):
        for c in range(4):
            rows[pl.ds(c * lats, lats), pl.ds(k * lons, lons)] = grads[k][
                c // 2, :, pl.ds((c % 2) * lons, lons)
            ]
    width, slots = 4 * lats, outs[0].shape[0]
    for step in range(16 * slots // 256):
        value = jnp.dot(rows[...], table_ref[step], preferred_element_type=jnp.float32).T
        first, stop = 256 * step, 256 * step + 256
        for kp in range(first // slots, -(-stop // slots)):
            low, high = max(first, kp * slots), min(stop, (kp + 1) * slots)
            outs[kp // 2][low - kp * slots : high - kp * slots, pl.ds(kp % 2 * width, width)] = (
                value[low - first : high - first].astype(jnp.bfloat16)
            )


def fourier_rows(table, grads):
    _, lats, lons2 = grads[0].shape
    steps, lon_total, _ = table.shape
    slots = steps * 256 // 16
    return pl.pallas_call(
        fourier_kernel,
        in_specs=[pl.BlockSpec(memory_space=pltpu.VMEM)] * 9,
        out_shape=[jax.ShapeDtypeStruct((slots, 8 * lats), jnp.bfloat16)] * 8,
        scratch_shapes=[pltpu.VMEM((4 * lats, lon_total), jnp.bfloat16)],
        compiler_params=params(24),
        cost_estimate=cost(2 * steps * 256 * lon_total * 4 * lats, 2 * table.size),
        name="fourier_rows",
    )(table, *grads)


def turn_kernel(wave_ref, *refs):
    blocks, (out_ref, rows) = refs[:8], refs[8:]
    slots, width = blocks[0].shape
    for t in range(width // 128):
        lanes = slice(128 * t, 128 * t + 128)
        for k in range(8):
            start = pl.multiple_of(wave_ref[k] * slots, 8)
            rows[t, pl.ds(start, slots), :] = blocks[k][:, lanes].astype(jnp.float32)
        for s in range(slots):
            b, lev, r = s // 16, s // 8 % 2, s % 8
            out_ref[2 * r + lev, b, :, lanes] = rows[t, pl.ds(s, 8, stride=slots), :].astype(
                jnp.bfloat16
            )


def turn(waves, blocks):
    slots, width = blocks[0].shape
    vmem = pl.BlockSpec(memory_space=pltpu.VMEM)
    return pl.pallas_call(
        turn_kernel,
        in_specs=[pl.BlockSpec(memory_space=pltpu.SMEM)] + [vmem] * 8,
        out_shape=jax.ShapeDtypeStruct((16, slots // 16, 8, width), jnp.bfloat16),
        scratch_shapes=[pltpu.VMEM((width // 128, 8 * slots, 128), jnp.float32)],
        compiler_params=params(12),
        cost_estimate=cost(0, 32 * blocks[0].size),
        name="turn",
    )(waves, *blocks)


def spectral_kernel(slot_ref, four_ref, head_ref, basis_any, out_ref, basis, left, total, sems):
    steps, _, lats, degs = basis.shape
    deg_dev = degs // 16
    head = head_ref.shape[1]
    halves = (pl.ds(0, 4), pl.ds(4, 4))
    copies = [
        [
            pltpu.make_async_copy(basis_any.at[part, b], basis.at[b, part], sems.at[b, i])
            for i, part in enumerate(halves)
        ]
        for b in range(head, steps)
    ]
    for copy in sum(copies, []):
        copy.start()

    def summed(b):
        for q in range(8):
            for lev in range(2):
                block = four_ref[2 * q + lev, b].astype(jnp.float32)
                for seg in range(8):
                    left[pl.ds(64 * lev + 8 * seg, 8), pl.ds(q * lats, lats)] = block[
                        :, seg * lats : (seg + 1) * lats
                    ]
        if b >= head:
            for copy in copies[b - head]:
                copy.wait()
            blocks = basis[b]
        else:
            blocks = head_ref[:, b]
        value = jnp.dot(
            left[...].astype(jnp.bfloat16),
            blocks.reshape(8 * lats, degs),
            preferred_element_type=jnp.float32,
        )
        degree = lax.broadcasted_iota(jnp.int32, value.shape, 1)
        return jnp.where(degree >= slot_ref[b], value, 0.0)

    for k in range(2):
        even, odd = summed(2 * k), summed(2 * k + 1)
        for lev in range(2):
            rows = slice(64 * lev, 64 * lev + 64)
            both = jnp.concatenate([even[rows], odd[rows]], 0).T
            for a in range(16):
                out_ref[2 * a + lev, pl.ds(k * deg_dev, deg_dev)] = both[
                    a * deg_dev : (a + 1) * deg_dev
                ].astype(jnp.bfloat16)
    total[...] = summed(4).T
    half = deg_dev // 2
    even = total[pl.ds(0, degs // 2, stride=2), :]
    odd = total[pl.ds(1, degs // 2, stride=2), :]
    low = lax.broadcasted_iota(jnp.int32, even.shape, 1) < 64
    pair = (
        jnp.where(low, even, pltpu.roll(odd, 64, 1)),
        jnp.where(low, pltpu.roll(even, 64, 1), odd),
    )
    for a in range(16):
        for lev in range(2):
            out_ref[2 * a + lev, pl.ds(2 * deg_dev, half)] = pair[lev][
                a * half : (a + 1) * half
            ].astype(jnp.bfloat16)
    rows = 5 * half
    for a in range(32):
        out_ref[a, pl.ds(rows, out_ref.shape[1] - rows)] = jnp.zeros(
            (out_ref.shape[1] - rows, 128), jnp.bfloat16
        )


def spectral_parts(slots, fourier, head, basis):
    _, steps, lats, degs = basis.shape
    vmem, smem = pl.BlockSpec(memory_space=pltpu.VMEM), pl.BlockSpec(memory_space=pltpu.SMEM)
    return pl.pallas_call(
        spectral_kernel,
        in_specs=[smem, vmem, vmem, pl.BlockSpec(memory_space=pl.ANY)],
        out_shape=jax.ShapeDtypeStruct((32, 104, 128), jnp.bfloat16),
        scratch_shapes=[
            pltpu.VMEM((steps, 8, lats, degs), jnp.bfloat16),
            pltpu.VMEM((128, 8 * lats), jnp.float32),
            pltpu.VMEM((degs, 128), jnp.float32),
            pltpu.SemaphoreType.DMA((steps, 2)),
        ],
        compiler_params=params(16),
        cost_estimate=cost(5 * 2 * 128 * 8 * lats * degs, 2 * basis.size + 2 * fourier.size),
        name="spectral_parts",
    )(slots, fourier, head, basis)


def finish_kernel(in_ref, out_hbm, rows, out_ref, sems):
    depth = in_ref.shape[1]
    for x in range(4):
        for zq in range(2):
            for lev in range(2):
                first = in_ref[8 * x + 2 * zq + lev].astype(jnp.float32)
                second = in_ref[8 * x + 4 + 2 * zq + lev].astype(jnp.float32)
                rows[pl.ds((8 * lev + 2 * x + zq) * depth, depth), :] = first + second
    low = lax.broadcasted_iota(jnp.int32, (16, 128), 1) < 64
    copies = []
    for n in range(0, 40, 2):
        parts = []
        for k in range(2):
            one = rows[pl.ds(40 * k + n, 16, stride=depth), :]
            two = rows[pl.ds(40 * k + n + 1, 16, stride=depth), :]
            parts.append(jnp.where(low, one, pltpu.roll(two, 64, 1)))
            parts.append(jnp.where(low, pltpu.roll(one, 64, 1), two))
        parts.append(rows[pl.ds(80 + n // 2, 16, stride=depth), :])
        out_ref[pl.ds(64 * n, 128), :] = jnp.concatenate(parts, 0).T
        if n % 10 == 8:
            piece = pl.ds(64 * (n - 8), 640)
            copies.append(
                pltpu.make_async_copy(out_ref.at[piece], out_hbm.at[piece], sems.at[n // 10])
            )
            copies[-1].start()
    for copy in copies:
        copy.wait()


def finish(received):
    return pl.pallas_call(
        finish_kernel,
        in_specs=[pl.BlockSpec(memory_space=pltpu.VMEM)],
        out_specs=pl.BlockSpec(memory_space=pltpu.HBM),
        out_shape=jax.ShapeDtypeStruct((40 * 64, 80), jnp.float32),
        scratch_shapes=[
            pltpu.VMEM((16 * received.shape[1], 128), jnp.float32),
            pltpu.VMEM((40 * 64, 80), jnp.float32),
            pltpu.SemaphoreType.DMA((4,)),
        ],
        compiler_params=params(12),
        cost_estimate=cost(received.size, 2 * received.size + 4 * 40 * 64 * 128),
        name="finish",
    )(received)


def local(out_grad, grid_state, tend_rate, legendre_basis, wave_slot):
    lats, lons = out_grad.shape[1:]
    slot_dev, degs = legendre_basis.shape[1:]
    x, zq = lax.axis_index("x"), lax.axis_index("zq")
    wave, lev = lax.axis_index("wave"), lax.axis_index("lev")

    to, source = (
        wave ^ jnp.where(wave % 2 == 0, *(jnp.array(row, jnp.int32) for row in table))
        for table in (TO, FROM)
    )

    def swapped(blocks):
        return [blocks[0]] + [
            lax.ppermute(blocks[k], "wave", [(w, w ^ TO[w % 2][k]) for w in range(8)])
            for k in range(1, 8)
        ]

    basis, token = basis_blocks(lev.astype(jnp.int32)[None], legendre_basis)
    grads = gradient(to, tend_rate, out_grad, grid_state, token)
    basis = lax.all_to_all(basis, ("x", "zq"), 0, 0, tiled=True)
    grads = swapped(grads)
    table = wave_table(wave_slot.reshape(8, slot_dev)[to], source, lons, 64)
    blocks = swapped(fourier_rows(table, grads))
    fourier, basis = lax.optimization_barrier((turn(source, blocks), basis))
    fourier = lax.all_to_all(fourier, ("x", "zq", "lev"), 0, 0, tiled=True)

    first = wave * slot_dev + 8 * lev + 2 * x + zq
    slots = jnp.take(wave_slot, first + 16 * jnp.arange(slot_dev // 16, dtype=jnp.int32))
    parts = spectral_parts(slots, fourier, basis[:, :2], basis)
    parts = lax.all_to_all(parts, ("x", "zp", "zq", "lev"), 0, 0, tiled=True)
    return finish(parts).reshape(degs // 16, 2, 32, slot_dev)


def solution(mesh):
    fine = Mesh(
        mesh.devices.reshape(4, 2, 2, *mesh.devices.shape[1:]), ("x", "zp", "zq", "wave", "lev")
    )
    lat = ("x", "zp", "zq")
    in_specs = (P("lev", lat, "wave"), P("lev", lat, "wave"), P("lev"), P(lat, "wave", None), P())
    out_specs = P(lat, None, "lev", "wave")
    return jax.shard_map(local, mesh=fine, in_specs=in_specs, out_specs=out_specs, check_vma=False)
```

```python
import math

import jax
import jax.numpy as jnp
from jax import lax
from jax.experimental import pallas as pl
from jax.experimental.pallas import tpu as pltpu
from jax.sharding import Mesh, PartitionSpec as P

TO = ((0, 1, 2, 6, 4, 3, 7, 5), (0, 1, 6, 2, 4, 7, 3, 5))
FROM = ((0, 1, 2, 6, 4, 7, 3, 5), (0, 1, 6, 2, 4, 3, 7, 5))


def params(mib):
    return pltpu.CompilerParams(vmem_limit_bytes=mib * 1024 * 1024)


def cost(flops, moved, trans=0):
    return pl.CostEstimate(flops=flops, bytes_accessed=moved, transcendentals=trans)


def basis_kernel(lev_ref, basis_hbm, out_hbm, token_ref, in_buf, out_buf, in_sems, out_sems):
    steps, lats, _, degs = in_buf.shape
    lev = lev_ref[0]
    reads = [
        pltpu.make_async_copy(basis_hbm.at[:, 2 * b + lev], in_buf.at[b], in_sems.at[b])
        for b in range(steps)
    ]
    for read in reads:
        read.start()
    row = lax.broadcasted_iota(jnp.int32, (128, 128), 0)
    col = lax.broadcasted_iota(jnp.int32, (128, 128), 1)
    swap = (col == row % 16 * 8 + row // 16).astype(jnp.bfloat16)
    token_ref[...] = jnp.zeros_like(token_ref)
    writes = []
    for b in range(steps):
        reads[b].wait()
        lanes = 384
        for g in range(lats // 16):
            part = slice(16 * g, 16 * g + 16)
            block = in_buf[b, part, :, :lanes].astype(jnp.float32).reshape(128, lanes)
            turned = jnp.dot(swap, block.astype(jnp.bfloat16), preferred_element_type=jnp.float32)
            out_buf[b, :, part, :lanes] = turned.astype(jnp.bfloat16).reshape(8, 16, lanes)
            other = jnp.swapaxes(in_buf[b, part, :, lanes:].astype(jnp.float32), 0, 1)
            out_buf[b, :, part, lanes:] = other.astype(jnp.bfloat16)
        writes.append(pltpu.make_async_copy(out_buf.at[b], out_hbm.at[:, b], out_sems.at[b]))
        writes[b].start()
    for write in writes:
        write.wait()


def basis_blocks(lev, basis):
    lats, slots, degs = basis.shape
    steps = slots // 16
    hbm = pl.BlockSpec(memory_space=pltpu.HBM)
    return pl.pallas_call(
        basis_kernel,
        in_specs=[pl.BlockSpec(memory_space=pltpu.SMEM), hbm],
        out_specs=[hbm, pl.BlockSpec(memory_space=pltpu.VMEM)],
        out_shape=[
            jax.ShapeDtypeStruct((8, steps, lats, degs), jnp.bfloat16),
            jax.ShapeDtypeStruct((8, 128), jnp.float32),
        ],
        scratch_shapes=[
            pltpu.VMEM((steps, lats, 8, degs), jnp.bfloat16),
            pltpu.VMEM((steps, 8, lats, degs), jnp.bfloat16),
            pltpu.SemaphoreType.DMA((steps,)),
            pltpu.SemaphoreType.DMA((steps,)),
        ],
        compiler_params=params(60),
        cost_estimate=cost(0, 2 * lats * slots * degs),
        name="basis_blocks",
    )(lev, basis.reshape(lats, slots // 8, 8, degs))


def grad_kernel(wave_ref, rate_ref, grad_ref, state_ref, _, *outs):
    lons = grad_ref.shape[-1]
    for k in range(8):
        to = wave_ref[k]
        for c in range(4):
            slope = 1.0 - jnp.tanh(state_ref[c, to].astype(jnp.float32)) ** 2
            value = grad_ref[c, to].astype(jnp.float32) * (1.0 + rate_ref[8 * c + to] * slope)
            outs[k][c // 2, :, pl.ds((c % 2) * lons, lons)] = value.astype(jnp.bfloat16)


def gradient(to, rate, grad, state, after):
    chans, lats, lons = grad.shape
    four = (4, chans // 4, lats, lons)
    smem, vmem = pl.BlockSpec(memory_space=pltpu.SMEM), pl.BlockSpec(memory_space=pltpu.VMEM)
    return pl.pallas_call(
        grad_kernel,
        in_specs=[smem, smem, vmem, vmem, vmem],
        out_shape=[jax.ShapeDtypeStruct((2, lats, 2 * lons), jnp.bfloat16)] * 8,
        compiler_params=params(16),
        cost_estimate=cost(6 * grad.size, 6 * grad.size, grad.size),
        name="gradient",
    )(to, rate, grad.reshape(four), state.reshape(four), after)


def table_kernel(coarse_cos, coarse_sin, fine_cos, fine_sin, out_ref):
    fine = fine_cos.shape[0]
    for j in range(coarse_cos.shape[0]):
        cos, sin = coarse_cos[j : j + 1, :], coarse_sin[j : j + 1, :]
        out_ref[0, j * fine : (j + 1) * fine, :] = (
            cos * fine_cos[...] - sin * fine_sin[...]
        ).astype(jnp.bfloat16)


def wave_table(slots, blocks, lons, fine):
    lon_total = 8 * lons
    quarter = jnp.array([0, lon_total // 4], jnp.int32)[None, :, None]
    phase = jnp.broadcast_to(quarter, (8, 2, slots.shape[1])).reshape(1, -1)
    slot = jnp.broadcast_to(slots[:, None, :], (8, 2, slots.shape[1])).reshape(1, -1)

    def trig(lon, shift):
        index = (slot * lon[:, None] + shift) % lon_total
        angle = index.astype(jnp.float32) * (2.0 * math.pi / lon_total)
        return jnp.cos(angle), jnp.sin(angle)

    starts = blocks[:, None] * lons + fine * jnp.arange(lons // fine, dtype=jnp.int32)[None, :]
    coarse_cos, coarse_sin = trig(starts.reshape(-1), 0)
    fine_cos, fine_sin = trig(jnp.arange(fine, dtype=jnp.int32), phase)
    scale = 1.0 / math.sqrt(lon_total)
    columns = slot.shape[1]
    part = lambda a: pl.BlockSpec((a.shape[0], 256), lambda j: (0, j))
    return pl.pallas_call(
        table_kernel,
        grid=(columns // 256,),
        in_specs=[part(a) for a in (coarse_cos, coarse_sin, fine_cos, fine_sin)],
        out_specs=pl.BlockSpec((1, lon_total, 256), lambda j: (j, 0, 0)),
        out_shape=jax.ShapeDtypeStruct((columns // 256, lon_total, 256), jnp.bfloat16),
        compiler_params=params(12),
        cost_estimate=cost(3 * columns * lon_total, 2 * columns * lon_total),
        name="wave_table",
    )(coarse_cos * scale, coarse_sin * scale, fine_cos, fine_sin)


def fourier_kernel(table_ref, *refs):
    grads, outs, rows = refs[:8], refs[8:16], refs[16]
    lats, lons = grads[0].shape[1], grads[0].shape[2] // 2
    for k in range(8):
        for c in range(4):
            rows[pl.ds(c * lats, lats), pl.ds(k * lons, lons)] = grads[k][
                c // 2, :, pl.ds((c % 2) * lons, lons)
            ]
    width, slots = 4 * lats, outs[0].shape[0]
    for step in range(16 * slots // 256):
        value = jnp.dot(rows[...], table_ref[step], preferred_element_type=jnp.float32).T
        first, stop = 256 * step, 256 * step + 256
        for kp in range(first // slots, -(-stop // slots)):
            low, high = max(first, kp * slots), min(stop, (kp + 1) * slots)
            outs[kp // 2][low - kp * slots : high - kp * slots, pl.ds(kp % 2 * width, width)] = (
                value[low - first : high - first].astype(jnp.bfloat16)
            )


def fourier_rows(table, grads):
    _, lats, lons2 = grads[0].shape
    steps, lon_total, _ = table.shape
    slots = steps * 256 // 16
    return pl.pallas_call(
        fourier_kernel,
        in_specs=[pl.BlockSpec(memory_space=pltpu.VMEM)] * 9,
        out_shape=[jax.ShapeDtypeStruct((slots, 8 * lats), jnp.bfloat16)] * 8,
        scratch_shapes=[pltpu.VMEM((4 * lats, lon_total), jnp.bfloat16)],
        compiler_params=params(24),
        cost_estimate=cost(2 * steps * 256 * lon_total * 4 * lats, 2 * table.size),
        name="fourier_rows",
    )(table, *grads)


def turn_kernel(wave_ref, *refs):
    blocks, (out_ref, rows) = refs[:8], refs[8:]
    slots, width = blocks[0].shape
    for t in range(width // 128):
        lanes = slice(128 * t, 128 * t + 128)
        for k in range(8):
            start = pl.multiple_of(wave_ref[k] * slots, 8)
            rows[t, pl.ds(start, slots), :] = blocks[k][:, lanes].astype(jnp.float32)
        for s in range(slots):
            b, lev, r = s // 16, s // 8 % 2, s % 8
            out_ref[2 * r + lev, b, :, lanes] = rows[t, pl.ds(s, 8, stride=slots), :].astype(
                jnp.bfloat16
            )


def turn(waves, blocks):
    slots, width = blocks[0].shape
    vmem = pl.BlockSpec(memory_space=pltpu.VMEM)
    return pl.pallas_call(
        turn_kernel,
        in_specs=[pl.BlockSpec(memory_space=pltpu.SMEM)] + [vmem] * 8,
        out_shape=jax.ShapeDtypeStruct((16, slots // 16, 8, width), jnp.bfloat16),
        scratch_shapes=[pltpu.VMEM((width // 128, 8 * slots, 128), jnp.float32)],
        compiler_params=params(12),
        cost_estimate=cost(0, 32 * blocks[0].size),
        name="turn",
    )(waves, *blocks)


def spectral_kernel(four_ref, head_ref, basis_any, out_ref, basis, left, total, sems):
    steps, _, lats, degs = basis.shape
    deg_dev = degs // 16
    head = head_ref.shape[1]
    halves = (pl.ds(0, 4), pl.ds(4, 4))
    copies = [
        [
            pltpu.make_async_copy(basis_any.at[part, b], basis.at[b, part], sems.at[b, i])
            for i, part in enumerate(halves)
        ]
        for b in range(head, steps)
    ]
    for copy in sum(copies, []):
        copy.start()

    def summed(b):
        for q in range(8):
            for lev in range(2):
                block = four_ref[2 * q + lev, b].astype(jnp.float32)
                for seg in range(8):
                    left[pl.ds(64 * lev + 8 * seg, 8), pl.ds(q * lats, lats)] = block[
                        :, seg * lats : (seg + 1) * lats
                    ]
        if b >= head:
            for copy in copies[b - head]:
                copy.wait()
            blocks = basis[b]
        else:
            blocks = head_ref[:, b]
        return jnp.dot(
            left[...].astype(jnp.bfloat16),
            blocks.reshape(8 * lats, degs),
            preferred_element_type=jnp.float32,
        )

    for k in range(2):
        even, odd = summed(2 * k), summed(2 * k + 1)
        for lev in range(2):
            rows = slice(64 * lev, 64 * lev + 64)
            both = jnp.concatenate([even[rows], odd[rows]], 0).T
            for a in range(16):
                out_ref[2 * a + lev, pl.ds(k * deg_dev, deg_dev)] = both[
                    a * deg_dev : (a + 1) * deg_dev
                ].astype(jnp.bfloat16)
    total[...] = summed(4).T
    half = deg_dev // 2
    even = total[pl.ds(0, degs // 2, stride=2), :]
    odd = total[pl.ds(1, degs // 2, stride=2), :]
    low = lax.broadcasted_iota(jnp.int32, even.shape, 1) < 64
    pair = (
        jnp.where(low, even, pltpu.roll(odd, 64, 1)),
        jnp.where(low, pltpu.roll(even, 64, 1), odd),
    )
    for a in range(16):
        for lev in range(2):
            out_ref[2 * a + lev, pl.ds(2 * deg_dev, half)] = pair[lev][
                a * half : (a + 1) * half
            ].astype(jnp.bfloat16)
    rows = 5 * half
    for a in range(32):
        out_ref[a, pl.ds(rows, out_ref.shape[1] - rows)] = jnp.zeros(
            (out_ref.shape[1] - rows, 128), jnp.bfloat16
        )


def spectral_parts(fourier, head, basis):
    _, steps, lats, degs = basis.shape
    vmem = pl.BlockSpec(memory_space=pltpu.VMEM)
    return pl.pallas_call(
        spectral_kernel,
        in_specs=[vmem, vmem, pl.BlockSpec(memory_space=pl.ANY)],
        out_shape=jax.ShapeDtypeStruct((32, 104, 128), jnp.bfloat16),
        scratch_shapes=[
            pltpu.VMEM((steps, 8, lats, degs), jnp.bfloat16),
            pltpu.VMEM((128, 8 * lats), jnp.float32),
            pltpu.VMEM((degs, 128), jnp.float32),
            pltpu.SemaphoreType.DMA((steps, 2)),
        ],
        compiler_params=params(16),
        cost_estimate=cost(5 * 2 * 128 * 8 * lats * degs, 2 * basis.size + 2 * fourier.size),
        name="spectral_parts",
    )(fourier, head, basis)


def finish_kernel(start_ref, slot_ref, in_ref, out_hbm, rows, out_ref, sems):
    depth = in_ref.shape[1]
    for x in range(4):
        for zq in range(2):
            for lev in range(2):
                first = in_ref[8 * x + 2 * zq + lev].astype(jnp.float32)
                second = in_ref[8 * x + 4 + 2 * zq + lev].astype(jnp.float32)
                rows[pl.ds((8 * lev + 2 * x + zq) * depth, depth), :] = first + second
    low = lax.broadcasted_iota(jnp.int32, (16, 128), 1) < 64
    slots = out_ref.shape[1]
    margin = lax.broadcasted_iota(jnp.int32, (128, slots), 0) // 64 + start_ref[0] - slot_ref[...]
    copies = []
    for n in range(0, 40, 2):
        parts = []
        for k in range(2):
            one = rows[pl.ds(40 * k + n, 16, stride=depth), :]
            two = rows[pl.ds(40 * k + n + 1, 16, stride=depth), :]
            parts.append(jnp.where(low, one, pltpu.roll(two, 64, 1)))
            parts.append(jnp.where(low, pltpu.roll(one, 64, 1), two))
        parts.append(rows[pl.ds(80 + n // 2, 16, stride=depth), :])
        value = jnp.concatenate(parts, 0).T
        out_ref[pl.ds(64 * n, 128), :] = jnp.where(margin + n >= 0, value, 0.0)
        if n % 10 == 8:
            piece = pl.ds(64 * (n - 8), 640)
            copies.append(
                pltpu.make_async_copy(out_ref.at[piece], out_hbm.at[piece], sems.at[n // 10])
            )
            copies[-1].start()
    for copy in copies:
        copy.wait()


def finish(start, slots, received):
    return pl.pallas_call(
        finish_kernel,
        in_specs=[pl.BlockSpec(memory_space=pltpu.SMEM)]
        + [pl.BlockSpec(memory_space=pltpu.VMEM)] * 2,
        out_specs=pl.BlockSpec(memory_space=pltpu.HBM),
        out_shape=jax.ShapeDtypeStruct((40 * 64, 80), jnp.float32),
        scratch_shapes=[
            pltpu.VMEM((16 * received.shape[1], 128), jnp.float32),
            pltpu.VMEM((40 * 64, 80), jnp.float32),
            pltpu.SemaphoreType.DMA((4,)),
        ],
        compiler_params=params(12),
        cost_estimate=cost(received.size, 2 * received.size + 4 * 40 * 64 * 128),
        name="finish",
    )(start, slots, received)


def local(out_grad, grid_state, tend_rate, legendre_basis, wave_slot):
    lats, lons = out_grad.shape[1:]
    slot_dev, degs = legendre_basis.shape[1:]
    x, zq = lax.axis_index("x"), lax.axis_index("zq")
    wave, lev = lax.axis_index("wave"), lax.axis_index("lev")

    to, source = (
        wave ^ jnp.where(wave % 2 == 0, *(jnp.array(row, jnp.int32) for row in table))
        for table in (TO, FROM)
    )

    def swapped(blocks):
        return [blocks[0]] + [
            lax.ppermute(blocks[k], "wave", [(w, w ^ TO[w % 2][k]) for w in range(8)])
            for k in range(1, 8)
        ]

    basis, token = basis_blocks(lev.astype(jnp.int32)[None], legendre_basis)
    grads = gradient(to, tend_rate, out_grad, grid_state, token)
    basis = lax.all_to_all(basis, ("x", "zq"), 0, 0, tiled=True)
    grads = swapped(grads)
    table = wave_table(wave_slot.reshape(8, slot_dev)[to], source, lons, 64)
    blocks = swapped(fourier_rows(table, grads))
    fourier, basis = lax.optimization_barrier((turn(source, blocks), basis))
    fourier = lax.all_to_all(fourier, ("x", "zq", "lev"), 0, 0, tiled=True)

    parts = spectral_parts(fourier, basis[:, :2], basis)
    parts = lax.all_to_all(parts, ("x", "zp", "zq", "lev"), 0, 0, tiled=True)
    deg_dev = degs // 16
    start = (4 * x + 2 * lax.axis_index("zp") + zq).astype(jnp.int32)[None] * deg_dev
    slots = lax.dynamic_slice_in_dim(wave_slot, wave * slot_dev, slot_dev)[None]
    return finish(start, slots, parts).reshape(deg_dev, 2, 32, slot_dev)


def solution(mesh):
    fine = Mesh(
        mesh.devices.reshape(4, 2, 2, *mesh.devices.shape[1:]), ("x", "zp", "zq", "wave", "lev")
    )
    lat = ("x", "zp", "zq")
    in_specs = (P("lev", lat, "wave"), P("lev", lat, "wave"), P("lev"), P(lat, "wave", None), P())
    out_specs = P(lat, None, "lev", "wave")
    return jax.shard_map(local, mesh=fine, in_specs=in_specs, out_specs=out_specs, check_vma=False)
```

```python
import math

import jax
import jax.numpy as jnp
from jax import lax
from jax.experimental import pallas as pl
from jax.experimental.pallas import tpu as pltpu
from jax.sharding import Mesh, PartitionSpec as P

TO = ((0, 1, 2, 6, 4, 3, 7, 5), (0, 1, 6, 2, 4, 7, 3, 5))
FROM = ((0, 1, 2, 6, 4, 7, 3, 5), (0, 1, 6, 2, 4, 3, 7, 5))


def params(mib):
    return pltpu.CompilerParams(vmem_limit_bytes=mib * 1024 * 1024)


def cost(flops, moved, trans=0):
    return pl.CostEstimate(flops=flops, bytes_accessed=moved, transcendentals=trans)


def basis_kernel(lev_ref, basis_hbm, out_hbm, token_ref, in_buf, out_buf, in_sems, out_sems):
    steps, lats, _, degs = in_buf.shape
    lev = lev_ref[0]
    reads = [
        pltpu.make_async_copy(basis_hbm.at[:, 2 * b + lev], in_buf.at[b], in_sems.at[b])
        for b in range(steps)
    ]
    for read in reads:
        read.start()
    row = lax.broadcasted_iota(jnp.int32, (128, 128), 0)
    col = lax.broadcasted_iota(jnp.int32, (128, 128), 1)
    swap = (col == row % 16 * 8 + row // 16).astype(jnp.bfloat16)
    token_ref[...] = jnp.zeros_like(token_ref)
    writes = []
    for b in range(steps):
        reads[b].wait()
        lanes = 384
        for g in range(lats // 16):
            part = slice(16 * g, 16 * g + 16)
            block = in_buf[b, part, :, :lanes].astype(jnp.float32).reshape(128, lanes)
            turned = jnp.dot(swap, block.astype(jnp.bfloat16), preferred_element_type=jnp.float32)
            out_buf[b, :, part, :lanes] = turned.astype(jnp.bfloat16).reshape(8, 16, lanes)
            other = jnp.swapaxes(in_buf[b, part, :, lanes:].astype(jnp.float32), 0, 1)
            out_buf[b, :, part, lanes:] = other.astype(jnp.bfloat16)
        writes.append(pltpu.make_async_copy(out_buf.at[b], out_hbm.at[:, b], out_sems.at[b]))
        writes[b].start()
    for write in writes:
        write.wait()


def basis_blocks(lev, basis):
    lats, slots, degs = basis.shape
    steps = slots // 16
    hbm = pl.BlockSpec(memory_space=pltpu.HBM)
    return pl.pallas_call(
        basis_kernel,
        in_specs=[pl.BlockSpec(memory_space=pltpu.SMEM), hbm],
        out_specs=[hbm, pl.BlockSpec(memory_space=pltpu.VMEM)],
        out_shape=[
            jax.ShapeDtypeStruct((8, steps, lats, degs), jnp.bfloat16),
            jax.ShapeDtypeStruct((8, 128), jnp.float32),
        ],
        scratch_shapes=[
            pltpu.VMEM((steps, lats, 8, degs), jnp.bfloat16),
            pltpu.VMEM((steps, 8, lats, degs), jnp.bfloat16),
            pltpu.SemaphoreType.DMA((steps,)),
            pltpu.SemaphoreType.DMA((steps,)),
        ],
        compiler_params=params(60),
        cost_estimate=cost(0, 2 * lats * slots * degs),
        name="basis_blocks",
    )(lev, basis.reshape(lats, slots // 8, 8, degs))


def grad_kernel(wave_ref, rate_ref, grad_ref, state_ref, _, *outs):
    lons = grad_ref.shape[-1]
    for k in range(8):
        to = wave_ref[k]
        for c in range(4):
            slope = 1.0 - jnp.tanh(state_ref[c, to].astype(jnp.float32)) ** 2
            value = grad_ref[c, to].astype(jnp.float32) * (1.0 + rate_ref[8 * c + to] * slope)
            outs[k][c // 2, :, pl.ds((c % 2) * lons, lons)] = value.astype(jnp.bfloat16)


def gradient(to, rate, grad, state, after):
    chans, lats, lons = grad.shape
    four = (4, chans // 4, lats, lons)
    smem, vmem = pl.BlockSpec(memory_space=pltpu.SMEM), pl.BlockSpec(memory_space=pltpu.VMEM)
    return pl.pallas_call(
        grad_kernel,
        in_specs=[smem, smem, vmem, vmem, vmem],
        out_shape=[jax.ShapeDtypeStruct((2, lats, 2 * lons), jnp.bfloat16)] * 8,
        compiler_params=params(16),
        cost_estimate=cost(6 * grad.size, 6 * grad.size, grad.size),
        name="gradient",
    )(to, rate, grad.reshape(four), state.reshape(four), after)


def table_kernel(coarse_cos, coarse_sin, fine_cos, fine_sin, out_ref):
    fine = fine_cos.shape[0]
    for j in range(coarse_cos.shape[0]):
        cos, sin = coarse_cos[j : j + 1, :], coarse_sin[j : j + 1, :]
        out_ref[0, j * fine : (j + 1) * fine, :] = (
            cos * fine_cos[...] - sin * fine_sin[...]
        ).astype(jnp.bfloat16)


def wave_table(slots, blocks, lons, fine):
    lon_total = 8 * lons
    quarter = jnp.array([0, lon_total // 4], jnp.int32)[None, :, None]
    phase = jnp.broadcast_to(quarter, (8, 2, slots.shape[1])).reshape(1, -1)
    slot = jnp.broadcast_to(slots[:, None, :], (8, 2, slots.shape[1])).reshape(1, -1)

    def trig(lon, shift):
        index = (slot * lon[:, None] + shift) % lon_total
        angle = index.astype(jnp.float32) * (2.0 * math.pi / lon_total)
        return jnp.cos(angle), jnp.sin(angle)

    starts = blocks[:, None] * lons + fine * jnp.arange(lons // fine, dtype=jnp.int32)[None, :]
    coarse_cos, coarse_sin = trig(starts.reshape(-1), 0)
    fine_cos, fine_sin = trig(jnp.arange(fine, dtype=jnp.int32), phase)
    scale = 1.0 / math.sqrt(lon_total)
    columns = slot.shape[1]
    part = lambda a: pl.BlockSpec((a.shape[0], 256), lambda j: (0, j))
    return pl.pallas_call(
        table_kernel,
        grid=(columns // 256,),
        in_specs=[part(a) for a in (coarse_cos, coarse_sin, fine_cos, fine_sin)],
        out_specs=pl.BlockSpec((1, lon_total, 256), lambda j: (j, 0, 0)),
        out_shape=jax.ShapeDtypeStruct((columns // 256, lon_total, 256), jnp.bfloat16),
        compiler_params=params(12),
        cost_estimate=cost(3 * columns * lon_total, 2 * columns * lon_total),
        name="wave_table",
    )(coarse_cos * scale, coarse_sin * scale, fine_cos, fine_sin)


def fourier_kernel(table_ref, *refs):
    grads, outs, rows = refs[:8], refs[8:16], refs[16]
    lats, lons = grads[0].shape[1], grads[0].shape[2] // 2
    for k in range(8):
        for c in range(4):
            rows[pl.ds(c * lats, lats), pl.ds(k * lons, lons)] = grads[k][
                c // 2, :, pl.ds((c % 2) * lons, lons)
            ]
    width, slots = 4 * lats, outs[0].shape[0]
    for step in range(16 * slots // 256):
        value = jnp.dot(rows[...], table_ref[step], preferred_element_type=jnp.float32).T
        first, stop = 256 * step, 256 * step + 256
        for kp in range(first // slots, -(-stop // slots)):
            low, high = max(first, kp * slots), min(stop, (kp + 1) * slots)
            outs[kp // 2][low - kp * slots : high - kp * slots, pl.ds(kp % 2 * width, width)] = (
                value[low - first : high - first].astype(jnp.bfloat16)
            )


def fourier_rows(table, grads):
    _, lats, lons2 = grads[0].shape
    steps, lon_total, _ = table.shape
    slots = steps * 256 // 16
    return pl.pallas_call(
        fourier_kernel,
        in_specs=[pl.BlockSpec(memory_space=pltpu.VMEM)] * 9,
        out_shape=[jax.ShapeDtypeStruct((slots, 8 * lats), jnp.bfloat16)] * 8,
        scratch_shapes=[pltpu.VMEM((4 * lats, lon_total), jnp.bfloat16)],
        compiler_params=params(24),
        cost_estimate=cost(2 * steps * 256 * lon_total * 4 * lats, 2 * table.size),
        name="fourier_rows",
    )(table, *grads)


def turn_kernel(wave_ref, *refs):
    blocks, (out_ref, rows) = refs[:8], refs[8:]
    slots, width = blocks[0].shape
    for t in range(width // 128):
        lanes = slice(128 * t, 128 * t + 128)
        for k in range(8):
            start = pl.multiple_of(wave_ref[k] * slots, 8)
            rows[t, pl.ds(start, slots), :] = blocks[k][:, lanes].astype(jnp.float32)
        for s in range(slots):
            b, lev, r = s // 16, s // 8 % 2, s % 8
            out_ref[2 * r + lev, b, :, lanes] = rows[t, pl.ds(s, 8, stride=slots), :].astype(
                jnp.bfloat16
            )


def turn(waves, blocks):
    slots, width = blocks[0].shape
    vmem = pl.BlockSpec(memory_space=pltpu.VMEM)
    return pl.pallas_call(
        turn_kernel,
        in_specs=[pl.BlockSpec(memory_space=pltpu.SMEM)] + [vmem] * 8,
        out_shape=jax.ShapeDtypeStruct((16, slots // 16, 8, width), jnp.bfloat16),
        scratch_shapes=[pltpu.VMEM((width // 128, 9 * slots, 128), jnp.float32)],
        compiler_params=params(12),
        cost_estimate=cost(0, 32 * blocks[0].size),
        name="turn",
    )(waves, *blocks)


def spectral_kernel(slot_ref, four_ref, head_ref, basis_any, out_ref, basis, left, total, sems):
    steps, _, lats, degs = basis.shape
    deg_dev = degs // 16
    head = head_ref.shape[1]
    halves = (pl.ds(0, 4), pl.ds(4, 4))
    copies = [
        [
            pltpu.make_async_copy(basis_any.at[part, b], basis.at[b, part], sems.at[b, i])
            for i, part in enumerate(halves)
        ]
        for b in range(head, steps)
    ]
    for copy in sum(copies, []):
        copy.start()

    def summed(b):
        for q in range(8):
            for lev in range(2):
                block = four_ref[2 * q + lev, b].astype(jnp.float32)
                for seg in range(8):
                    left[pl.ds(64 * lev + 8 * seg, 8), pl.ds(q * lats, lats)] = block[
                        :, seg * lats : (seg + 1) * lats
                    ]
        if b >= head:
            for copy in copies[b - head]:
                copy.wait()
            blocks = basis[b]
        else:
            blocks = head_ref[:, b]
        value = jnp.dot(
            left[...].astype(jnp.bfloat16),
            blocks.reshape(8 * lats, degs),
            preferred_element_type=jnp.float32,
        )
        degree = lax.broadcasted_iota(jnp.int32, value.shape, 1)
        return jnp.where(degree >= slot_ref[b], value, 0.0)

    for k in range(2):
        even, odd = summed(2 * k), summed(2 * k + 1)
        for lev in range(2):
            rows = slice(64 * lev, 64 * lev + 64)
            both = jnp.concatenate([even[rows], odd[rows]], 0).T
            for a in range(16):
                out_ref[2 * a + lev, pl.ds(k * deg_dev, deg_dev)] = both[
                    a * deg_dev : (a + 1) * deg_dev
                ].astype(jnp.bfloat16)
    total[pl.ds(0, degs), :] = summed(4).T
    half = deg_dev // 2
    even = total[pl.ds(0, degs // 2, stride=2), :]
    odd = total[pl.ds(1, degs // 2, stride=2), :]
    low = lax.broadcasted_iota(jnp.int32, even.shape, 1) < 64
    pair = (
        jnp.where(low, even, pltpu.roll(odd, 64, 1)),
        jnp.where(low, pltpu.roll(even, 64, 1), odd),
    )
    for a in range(16):
        for lev in range(2):
            out_ref[2 * a + lev, pl.ds(2 * deg_dev, half)] = pair[lev][
                a * half : (a + 1) * half
            ].astype(jnp.bfloat16)
    rows = 5 * half
    for a in range(32):
        out_ref[a, pl.ds(rows, out_ref.shape[1] - rows)] = jnp.zeros(
            (out_ref.shape[1] - rows, 128), jnp.bfloat16
        )


def spectral_parts(slots, fourier, head, basis):
    _, steps, lats, degs = basis.shape
    vmem, smem = pl.BlockSpec(memory_space=pltpu.VMEM), pl.BlockSpec(memory_space=pltpu.SMEM)
    return pl.pallas_call(
        spectral_kernel,
        in_specs=[smem, vmem, vmem, pl.BlockSpec(memory_space=pl.ANY)],
        out_shape=jax.ShapeDtypeStruct((32, 104, 128), jnp.bfloat16),
        scratch_shapes=[
            pltpu.VMEM((steps, 8, lats, degs), jnp.bfloat16),
            pltpu.VMEM((128, 8 * lats), jnp.float32),
            pltpu.VMEM((degs + 8, 128), jnp.float32),
            pltpu.SemaphoreType.DMA((steps, 2)),
        ],
        compiler_params=params(16),
        cost_estimate=cost(5 * 2 * 128 * 8 * lats * degs, 2 * basis.size + 2 * fourier.size),
        name="spectral_parts",
    )(slots, fourier, head, basis)


def finish_kernel(in_ref, out_hbm, rows, out_ref, sems):
    depth = in_ref.shape[1]
    for x in range(4):
        for zq in range(2):
            for lev in range(2):
                first = in_ref[8 * x + 2 * zq + lev].astype(jnp.float32)
                second = in_ref[8 * x + 4 + 2 * zq + lev].astype(jnp.float32)
                rows[pl.ds((8 * lev + 2 * x + zq) * depth, depth), :] = first + second
    low = lax.broadcasted_iota(jnp.int32, (16, 128), 1) < 64
    copies = []
    for n in range(0, 40, 2):
        parts = []
        for k in range(2):
            one = rows[pl.ds(40 * k + n, 16, stride=depth), :]
            two = rows[pl.ds(40 * k + n + 1, 16, stride=depth), :]
            parts.append(jnp.where(low, one, pltpu.roll(two, 64, 1)))
            parts.append(jnp.where(low, pltpu.roll(one, 64, 1), two))
        parts.append(rows[pl.ds(80 + n // 2, 16, stride=depth), :])
        out_ref[pl.ds(64 * n, 128), :] = jnp.concatenate(parts, 0).T
        if n % 10 == 8:
            piece = pl.ds(64 * (n - 8), 640)
            copies.append(
                pltpu.make_async_copy(out_ref.at[piece], out_hbm.at[piece], sems.at[n // 10])
            )
            copies[-1].start()
    for copy in copies:
        copy.wait()


def finish(received):
    return pl.pallas_call(
        finish_kernel,
        in_specs=[pl.BlockSpec(memory_space=pltpu.VMEM)],
        out_specs=pl.BlockSpec(memory_space=pltpu.HBM),
        out_shape=jax.ShapeDtypeStruct((40 * 64, 80), jnp.float32),
        scratch_shapes=[
            pltpu.VMEM((17 * received.shape[1], 128), jnp.float32),
            pltpu.VMEM((40 * 64, 80), jnp.float32),
            pltpu.SemaphoreType.DMA((4,)),
        ],
        compiler_params=params(12),
        cost_estimate=cost(received.size, 2 * received.size + 4 * 40 * 64 * 128),
        name="finish",
    )(received)


def local(out_grad, grid_state, tend_rate, legendre_basis, wave_slot):
    lats, lons = out_grad.shape[1:]
    slot_dev, degs = legendre_basis.shape[1:]
    x, zq = lax.axis_index("x"), lax.axis_index("zq")
    wave, lev = lax.axis_index("wave"), lax.axis_index("lev")

    to, source = (
        wave ^ jnp.where(wave % 2 == 0, *(jnp.array(row, jnp.int32) for row in table))
        for table in (TO, FROM)
    )

    def swapped(blocks):
        return [blocks[0]] + [
            lax.ppermute(blocks[k], "wave", [(w, w ^ TO[w % 2][k]) for w in range(8)])
            for k in range(1, 8)
        ]

    basis, token = basis_blocks(lev.astype(jnp.int32)[None], legendre_basis)
    grads = gradient(to, tend_rate, out_grad, grid_state, token)
    basis = lax.all_to_all(basis, ("x", "zq"), 0, 0, tiled=True)
    grads = swapped(grads)
    table = wave_table(wave_slot.reshape(8, slot_dev)[to], source, lons, 64)
    blocks = swapped(fourier_rows(table, grads))
    fourier, basis = lax.optimization_barrier((turn(source, blocks), basis))
    fourier = lax.all_to_all(fourier, ("x", "zq", "lev"), 0, 0, tiled=True)

    first = wave * slot_dev + 8 * lev + 2 * x + zq
    slots = jnp.take(wave_slot, first + 16 * jnp.arange(slot_dev // 16, dtype=jnp.int32))
    parts = spectral_parts(slots, fourier, basis[:, :3], basis)
    parts = lax.all_to_all(parts, ("x", "zp", "zq", "lev"), 0, 0, tiled=True)
    return finish(parts).reshape(degs // 16, 2, 32, slot_dev)


def solution(mesh):
    fine = Mesh(
        mesh.devices.reshape(4, 2, 2, *mesh.devices.shape[1:]), ("x", "zp", "zq", "wave", "lev")
    )
    lat = ("x", "zp", "zq")
    in_specs = (P("lev", lat, "wave"), P("lev", lat, "wave"), P("lev"), P(lat, "wave", None), P())
    out_specs = P(lat, None, "lev", "wave")
    return jax.shard_map(local, mesh=fine, in_specs=in_specs, out_specs=out_specs, check_vma=False)
```

```python
import math

import jax
import jax.numpy as jnp
from jax import lax
from jax.experimental import pallas as pl
from jax.experimental.pallas import tpu as pltpu
from jax.sharding import Mesh, PartitionSpec as P

TO = ((0, 1, 2, 6, 4, 3, 7, 5), (0, 1, 6, 2, 4, 7, 3, 5))
FROM = ((0, 1, 2, 6, 4, 7, 3, 5), (0, 1, 6, 2, 4, 3, 7, 5))


def params(mib):
    return pltpu.CompilerParams(vmem_limit_bytes=mib * 1024 * 1024)


def cost(flops, moved, trans=0):
    return pl.CostEstimate(flops=flops, bytes_accessed=moved, transcendentals=trans)


def basis_kernel(lev_ref, basis_hbm, out_hbm, token_ref, in_buf, out_buf, in_sems, out_sems):
    steps, lats, _, degs = in_buf.shape
    lev = lev_ref[0]
    reads = [
        pltpu.make_async_copy(basis_hbm.at[:, 2 * b + lev], in_buf.at[b], in_sems.at[b])
        for b in range(steps)
    ]
    for read in reads:
        read.start()
    row = lax.broadcasted_iota(jnp.int32, (128, 128), 0)
    col = lax.broadcasted_iota(jnp.int32, (128, 128), 1)
    swap = (col == row % 16 * 8 + row // 16).astype(jnp.bfloat16)
    token_ref[...] = jnp.zeros_like(token_ref)
    writes = []
    for b in range(steps):
        reads[b].wait()
        lanes = 384
        for g in range(lats // 16):
            part = slice(16 * g, 16 * g + 16)
            block = in_buf[b, part, :, :lanes].astype(jnp.float32).reshape(128, lanes)
            turned = jnp.dot(swap, block.astype(jnp.bfloat16), preferred_element_type=jnp.float32)
            out_buf[b, :, part, :lanes] = turned.astype(jnp.bfloat16).reshape(8, 16, lanes)
            other = jnp.swapaxes(in_buf[b, part, :, lanes:].astype(jnp.float32), 0, 1)
            out_buf[b, :, part, lanes:] = other.astype(jnp.bfloat16)
        writes.append(pltpu.make_async_copy(out_buf.at[b], out_hbm.at[:, b], out_sems.at[b]))
        writes[b].start()
    for write in writes:
        write.wait()


def basis_blocks(lev, basis):
    lats, slots, degs = basis.shape
    steps = slots // 16
    hbm = pl.BlockSpec(memory_space=pltpu.HBM)
    return pl.pallas_call(
        basis_kernel,
        in_specs=[pl.BlockSpec(memory_space=pltpu.SMEM), hbm],
        out_specs=[hbm, pl.BlockSpec(memory_space=pltpu.VMEM)],
        out_shape=[
            jax.ShapeDtypeStruct((8, steps, lats, degs), jnp.bfloat16),
            jax.ShapeDtypeStruct((8, 128), jnp.float32),
        ],
        scratch_shapes=[
            pltpu.VMEM((steps, lats, 8, degs), jnp.bfloat16),
            pltpu.VMEM((steps, 8, lats, degs), jnp.bfloat16),
            pltpu.SemaphoreType.DMA((steps,)),
            pltpu.SemaphoreType.DMA((steps,)),
        ],
        compiler_params=params(63),
        cost_estimate=cost(0, 2 * lats * slots * degs),
        name="basis_blocks",
    )(lev, basis.reshape(lats, slots // 8, 8, degs))


def grad_kernel(wave_ref, rate_ref, grad_ref, state_ref, _, *outs):
    lons = grad_ref.shape[-1]
    for k in range(8):
        to = wave_ref[k]
        for c in range(4):
            slope = 1.0 - jnp.tanh(state_ref[c, to].astype(jnp.float32)) ** 2
            value = grad_ref[c, to].astype(jnp.float32) * (1.0 + rate_ref[8 * c + to] * slope)
            outs[k][c // 2, :, pl.ds((c % 2) * lons, lons)] = value.astype(jnp.bfloat16)


def gradient(to, rate, grad, state, after):
    chans, lats, lons = grad.shape
    four = (4, chans // 4, lats, lons)
    smem, vmem = pl.BlockSpec(memory_space=pltpu.SMEM), pl.BlockSpec(memory_space=pltpu.VMEM)
    return pl.pallas_call(
        grad_kernel,
        in_specs=[smem, smem, vmem, vmem, vmem],
        out_shape=[jax.ShapeDtypeStruct((2, lats, 2 * lons), jnp.bfloat16)] * 8,
        compiler_params=params(16),
        cost_estimate=cost(6 * grad.size, 6 * grad.size, grad.size),
        name="gradient",
    )(to, rate, grad.reshape(four), state.reshape(four), after)


def table_kernel(coarse_cos, coarse_sin, fine_cos, fine_sin, out_ref):
    fine = fine_cos.shape[0]
    for j in range(coarse_cos.shape[0]):
        cos, sin = coarse_cos[j : j + 1, :], coarse_sin[j : j + 1, :]
        out_ref[0, j * fine : (j + 1) * fine, :] = (
            cos * fine_cos[...] - sin * fine_sin[...]
        ).astype(jnp.bfloat16)


def wave_table(slots, blocks, lons, fine):
    lon_total = 8 * lons
    quarter = jnp.array([0, lon_total // 4], jnp.int32)[None, :, None]
    phase = jnp.broadcast_to(quarter, (8, 2, slots.shape[1])).reshape(1, -1)
    slot = jnp.broadcast_to(slots[:, None, :], (8, 2, slots.shape[1])).reshape(1, -1)

    def trig(lon, shift):
        index = (slot * lon[:, None] + shift) % lon_total
        angle = index.astype(jnp.float32) * (2.0 * math.pi / lon_total)
        return jnp.cos(angle), jnp.sin(angle)

    starts = blocks[:, None] * lons + fine * jnp.arange(lons // fine, dtype=jnp.int32)[None, :]
    coarse_cos, coarse_sin = trig(starts.reshape(-1), 0)
    fine_cos, fine_sin = trig(jnp.arange(fine, dtype=jnp.int32), phase)
    scale = 1.0 / math.sqrt(lon_total)
    columns = slot.shape[1]
    part = lambda a: pl.BlockSpec((a.shape[0], 256), lambda j: (0, j))
    return pl.pallas_call(
        table_kernel,
        grid=(columns // 256,),
        in_specs=[part(a) for a in (coarse_cos, coarse_sin, fine_cos, fine_sin)],
        out_specs=pl.BlockSpec((1, lon_total, 256), lambda j: (j, 0, 0)),
        out_shape=jax.ShapeDtypeStruct((columns // 256, lon_total, 256), jnp.bfloat16),
        compiler_params=params(12),
        cost_estimate=cost(3 * columns * lon_total, 2 * columns * lon_total),
        name="wave_table",
    )(coarse_cos * scale, coarse_sin * scale, fine_cos, fine_sin)


def fourier_kernel(table_ref, *refs):
    grads, outs, rows = refs[:8], refs[8:16], refs[16]
    lats, lons = grads[0].shape[1], grads[0].shape[2] // 2
    for k in range(8):
        for c in range(4):
            rows[pl.ds(c * lats, lats), pl.ds(k * lons, lons)] = grads[k][
                c // 2, :, pl.ds((c % 2) * lons, lons)
            ]
    width, slots = 4 * lats, outs[0].shape[0]
    for step in range(16 * slots // 256):
        value = jnp.dot(rows[...], table_ref[step], preferred_element_type=jnp.float32).T
        first, stop = 256 * step, 256 * step + 256
        for kp in range(first // slots, -(-stop // slots)):
            low, high = max(first, kp * slots), min(stop, (kp + 1) * slots)
            outs[kp // 2][low - kp * slots : high - kp * slots, pl.ds(kp % 2 * width, width)] = (
                value[low - first : high - first].astype(jnp.bfloat16)
            )


def fourier_rows(table, grads):
    _, lats, lons2 = grads[0].shape
    steps, lon_total, _ = table.shape
    slots = steps * 256 // 16
    return pl.pallas_call(
        fourier_kernel,
        in_specs=[pl.BlockSpec(memory_space=pltpu.VMEM)] * 9,
        out_shape=[jax.ShapeDtypeStruct((slots, 8 * lats), jnp.bfloat16)] * 8,
        scratch_shapes=[pltpu.VMEM((4 * lats, lon_total), jnp.bfloat16)],
        compiler_params=params(24),
        cost_estimate=cost(2 * steps * 256 * lon_total * 4 * lats, 2 * table.size),
        name="fourier_rows",
    )(table, *grads)


def turn_kernel(wave_ref, *refs):
    blocks, (out_ref, rows) = refs[:8], refs[8:]
    slots, width = blocks[0].shape
    for t in range(width // 128):
        lanes = slice(128 * t, 128 * t + 128)
        for k in range(8):
            start = pl.multiple_of(wave_ref[k] * slots, 8)
            rows[t, pl.ds(start, slots), :] = blocks[k][:, lanes].astype(jnp.float32)
        for s in range(slots):
            b, lev, r = s // 16, s // 8 % 2, s % 8
            out_ref[2 * r + lev, b, :, lanes] = rows[t, pl.ds(s, 8, stride=slots), :].astype(
                jnp.bfloat16
            )


def turn(waves, blocks):
    slots, width = blocks[0].shape
    vmem = pl.BlockSpec(memory_space=pltpu.VMEM)
    return pl.pallas_call(
        turn_kernel,
        in_specs=[pl.BlockSpec(memory_space=pltpu.SMEM)] + [vmem] * 8,
        out_shape=jax.ShapeDtypeStruct((16, slots // 16, 8, width), jnp.bfloat16),
        scratch_shapes=[pltpu.VMEM((width // 128, 9 * slots, 128), jnp.float32)],
        compiler_params=params(12),
        cost_estimate=cost(0, 32 * blocks[0].size),
        name="turn",
    )(waves, *blocks)


def spectral_kernel(slot_ref, four_ref, head_ref, basis_any, out_ref, basis, left, total, sems):
    steps, _, lats, degs = basis.shape
    deg_dev = degs // 16
    head = head_ref.shape[1]
    halves = (pl.ds(0, 4), pl.ds(4, 4))
    copies = [
        [
            pltpu.make_async_copy(basis_any.at[part, b], basis.at[b, part], sems.at[b, i])
            for i, part in enumerate(halves)
        ]
        for b in range(head, steps)
    ]
    for copy in sum(copies, []):
        copy.start()

    def summed(b):
        for q in range(8):
            for lev in range(2):
                block = four_ref[2 * q + lev, b].astype(jnp.float32)
                for seg in range(8):
                    left[pl.ds(64 * lev + 8 * seg, 8), pl.ds(q * lats, lats)] = block[
                        :, seg * lats : (seg + 1) * lats
                    ]
        if b >= head:
            for copy in copies[b - head]:
                copy.wait()
            blocks = basis[b]
        else:
            blocks = head_ref[:, b]
        value = jnp.dot(
            left[...].astype(jnp.bfloat16),
            blocks.reshape(8 * lats, degs),
            preferred_element_type=jnp.float32,
        )
        degree = lax.broadcasted_iota(jnp.int32, value.shape, 1)
        return jnp.where(degree >= slot_ref[b], value, 0.0)

    for k in range(2):
        even, odd = summed(2 * k), summed(2 * k + 1)
        for lev in range(2):
            rows = slice(64 * lev, 64 * lev + 64)
            both = jnp.concatenate([even[rows], odd[rows]], 0).T
            for a in range(16):
                out_ref[2 * a + lev, pl.ds(k * deg_dev, deg_dev)] = both[
                    a * deg_dev : (a + 1) * deg_dev
                ].astype(jnp.bfloat16)
    total[pl.ds(0, degs), :] = summed(4).T
    half = deg_dev // 2
    even = total[pl.ds(0, degs // 2, stride=2), :]
    odd = total[pl.ds(1, degs // 2, stride=2), :]
    low = lax.broadcasted_iota(jnp.int32, even.shape, 1) < 64
    pair = (
        jnp.where(low, even, pltpu.roll(odd, 64, 1)),
        jnp.where(low, pltpu.roll(even, 64, 1), odd),
    )
    for a in range(16):
        for lev in range(2):
            out_ref[2 * a + lev, pl.ds(2 * deg_dev, half)] = pair[lev][
                a * half : (a + 1) * half
            ].astype(jnp.bfloat16)
    rows = 5 * half
    for a in range(32):
        out_ref[a, pl.ds(rows, out_ref.shape[1] - rows)] = jnp.zeros(
            (out_ref.shape[1] - rows, 128), jnp.bfloat16
        )


def spectral_parts(slots, fourier, head, basis):
    _, steps, lats, degs = basis.shape
    vmem, smem = pl.BlockSpec(memory_space=pltpu.VMEM), pl.BlockSpec(memory_space=pltpu.SMEM)
    return pl.pallas_call(
        spectral_kernel,
        in_specs=[smem, vmem, vmem, pl.BlockSpec(memory_space=pl.ANY)],
        out_shape=jax.ShapeDtypeStruct((32, 104, 128), jnp.bfloat16),
        scratch_shapes=[
            pltpu.VMEM((steps, 8, lats, degs), jnp.bfloat16),
            pltpu.VMEM((128, 8 * lats), jnp.float32),
            pltpu.VMEM((degs + 8, 128), jnp.float32),
            pltpu.SemaphoreType.DMA((steps, 2)),
        ],
        compiler_params=params(16),
        cost_estimate=cost(5 * 2 * 128 * 8 * lats * degs, 2 * basis.size + 2 * fourier.size),
        name="spectral_parts",
    )(slots, fourier, head, basis)


def finish_kernel(in_ref, out_hbm, rows, out_ref, sems):
    depth = in_ref.shape[1]
    for x in range(4):
        for zq in range(2):
            for lev in range(2):
                first = in_ref[8 * x + 2 * zq + lev].astype(jnp.float32)
                second = in_ref[8 * x + 4 + 2 * zq + lev].astype(jnp.float32)
                rows[pl.ds((8 * lev + 2 * x + zq) * depth, depth), :] = first + second
    low = lax.broadcasted_iota(jnp.int32, (16, 128), 1) < 64
    copies = []
    for n in range(0, 40, 2):
        parts = []
        for k in range(2):
            one = rows[pl.ds(40 * k + n, 16, stride=depth), :]
            two = rows[pl.ds(40 * k + n + 1, 16, stride=depth), :]
            parts.append(jnp.where(low, one, pltpu.roll(two, 64, 1)))
            parts.append(jnp.where(low, pltpu.roll(one, 64, 1), two))
        parts.append(rows[pl.ds(80 + n // 2, 16, stride=depth), :])
        out_ref[pl.ds(64 * n, 128), :] = jnp.concatenate(parts, 0).T
        if n % 10 == 8:
            piece = pl.ds(64 * (n - 8), 640)
            copies.append(
                pltpu.make_async_copy(out_ref.at[piece], out_hbm.at[piece], sems.at[n // 10])
            )
            copies[-1].start()
    for copy in copies:
        copy.wait()


def finish(received):
    return pl.pallas_call(
        finish_kernel,
        in_specs=[pl.BlockSpec(memory_space=pltpu.VMEM)],
        out_specs=pl.BlockSpec(memory_space=pltpu.HBM),
        out_shape=jax.ShapeDtypeStruct((40 * 64, 80), jnp.float32),
        scratch_shapes=[
            pltpu.VMEM((17 * received.shape[1], 128), jnp.float32),
            pltpu.VMEM((40 * 64, 80), jnp.float32),
            pltpu.SemaphoreType.DMA((4,)),
        ],
        compiler_params=params(12),
        cost_estimate=cost(received.size, 2 * received.size + 4 * 40 * 64 * 128),
        name="finish",
    )(received)


def local(out_grad, grid_state, tend_rate, legendre_basis, wave_slot):
    lats, lons = out_grad.shape[1:]
    slot_dev, degs = legendre_basis.shape[1:]
    x, zq = lax.axis_index("x"), lax.axis_index("zq")
    wave, lev = lax.axis_index("wave"), lax.axis_index("lev")

    to, source = (
        wave ^ jnp.where(wave % 2 == 0, *(jnp.array(row, jnp.int32) for row in table))
        for table in (TO, FROM)
    )

    def swapped(blocks):
        return [blocks[0]] + [
            lax.ppermute(blocks[k], "wave", [(w, w ^ TO[w % 2][k]) for w in range(8)])
            for k in range(1, 8)
        ]

    basis, token = basis_blocks(lev.astype(jnp.int32)[None], legendre_basis)
    grads = gradient(to, tend_rate, out_grad, grid_state, token)
    basis = lax.all_to_all(basis, ("x", "zq"), 0, 0, tiled=True)
    grads = swapped(grads)
    slots, grads[1] = lax.optimization_barrier((wave_slot.reshape(8, slot_dev)[to], grads[1]))
    table = wave_table(slots, source, lons, 64)
    blocks = swapped(fourier_rows(table, grads))
    fourier, basis = lax.optimization_barrier((turn(source, blocks), basis))
    fourier = lax.all_to_all(fourier, ("x", "zq", "lev"), 0, 0, tiled=True)

    first = wave * slot_dev + 8 * lev + 2 * x + zq
    slots = jnp.take(wave_slot, first + 16 * jnp.arange(slot_dev // 16, dtype=jnp.int32))
    parts = spectral_parts(slots, fourier, basis[:, :3], basis)
    parts = lax.all_to_all(parts, ("x", "zp", "zq", "lev"), 0, 0, tiled=True)
    return finish(parts).reshape(degs // 16, 2, 32, slot_dev)


def solution(mesh):
    fine = Mesh(
        mesh.devices.reshape(4, 2, 2, *mesh.devices.shape[1:]), ("x", "zp", "zq", "wave", "lev")
    )
    lat = ("x", "zp", "zq")
    in_specs = (P("lev", lat, "wave"), P("lev", lat, "wave"), P("lev"), P(lat, "wave", None), P())
    out_specs = P(lat, None, "lev", "wave")
    return jax.shard_map(local, mesh=fine, in_specs=in_specs, out_specs=out_specs, check_vma=False)
```

```python
import math

import jax
import jax.numpy as jnp
from jax import lax
from jax.experimental import pallas as pl
from jax.experimental.pallas import tpu as pltpu
from jax.sharding import Mesh, PartitionSpec as P

TO = ((0, 1, 2, 6, 4, 3, 7, 5), (0, 1, 6, 2, 4, 7, 3, 5))
FROM = ((0, 1, 2, 6, 4, 7, 3, 5), (0, 1, 6, 2, 4, 3, 7, 5))


def params(mib):
    return pltpu.CompilerParams(vmem_limit_bytes=mib * 1024 * 1024)


def cost(flops, moved, trans=0):
    return pl.CostEstimate(flops=flops, bytes_accessed=moved, transcendentals=trans)


def basis_kernel(lev_ref, basis_hbm, out_hbm, token_ref, in_buf, out_buf, in_sems, out_sems):
    pieces, lats, steps, _, degs = in_buf.shape
    lev = lev_ref[0]
    reads = [
        pltpu.make_async_copy(
            basis_hbm.at[pl.ds(lats * g, lats), :, lev], in_buf.at[g], in_sems.at[g]
        )
        for g in range(pieces)
    ]
    for read in reads:
        read.start()
    row = lax.broadcasted_iota(jnp.int32, (128, 128), 0)
    col = lax.broadcasted_iota(jnp.int32, (128, 128), 1)
    swap = (col == row % 16 * 8 + row // 16).astype(jnp.bfloat16)
    token_ref[...] = jnp.zeros_like(token_ref)
    writes = []
    for g in range(pieces):
        reads[g].wait()
        for b in range(steps):
            block = in_buf[g, :, b].astype(jnp.float32).reshape(128, degs)
            turned = jnp.dot(swap, block.astype(jnp.bfloat16), preferred_element_type=jnp.float32)
            out_buf[g, :, b] = turned.astype(jnp.bfloat16).reshape(8, lats, degs)
        writes.append(
            pltpu.make_async_copy(
                out_buf.at[g], out_hbm.at[:, :, pl.ds(lats * g, lats)], out_sems.at[g]
            )
        )
        writes[g].start()
    for write in writes:
        write.wait()


def basis_blocks(lev, basis):
    lats, slots, degs = basis.shape
    steps = slots // 16
    hbm = pl.BlockSpec(memory_space=pltpu.HBM)
    return pl.pallas_call(
        basis_kernel,
        in_specs=[pl.BlockSpec(memory_space=pltpu.SMEM), hbm],
        out_specs=[hbm, pl.BlockSpec(memory_space=pltpu.VMEM)],
        out_shape=[
            jax.ShapeDtypeStruct((8, steps, lats, degs), jnp.bfloat16),
            jax.ShapeDtypeStruct((8, 128), jnp.float32),
        ],
        scratch_shapes=[
            pltpu.VMEM((lats // 16, 16, steps, 8, degs), jnp.bfloat16),
            pltpu.VMEM((lats // 16, 8, steps, 16, degs), jnp.bfloat16),
            pltpu.SemaphoreType.DMA((lats // 16,)),
            pltpu.SemaphoreType.DMA((lats // 16,)),
        ],
        compiler_params=params(63),
        cost_estimate=cost(0, 2 * lats * slots * degs),
        name="basis_blocks",
    )(lev, basis.reshape(lats, steps, 2, 8, degs))


def grad_kernel(wave_ref, rate_ref, grad_ref, state_ref, _, *outs):
    lons = grad_ref.shape[-1]
    for k in range(8):
        to = wave_ref[k]
        for c in range(4):
            slope = 1.0 - jnp.tanh(state_ref[c, to].astype(jnp.float32)) ** 2
            value = grad_ref[c, to].astype(jnp.float32) * (1.0 + rate_ref[8 * c + to] * slope)
            outs[k][c // 2, :, pl.ds((c % 2) * lons, lons)] = value.astype(jnp.bfloat16)


def gradient(to, rate, grad, state, after):
    chans, lats, lons = grad.shape
    four = (4, chans // 4, lats, lons)
    smem, vmem = pl.BlockSpec(memory_space=pltpu.SMEM), pl.BlockSpec(memory_space=pltpu.VMEM)
    return pl.pallas_call(
        grad_kernel,
        in_specs=[smem, smem, vmem, vmem, vmem],
        out_shape=[jax.ShapeDtypeStruct((2, lats, 2 * lons), jnp.bfloat16)] * 8,
        compiler_params=params(16),
        cost_estimate=cost(6 * grad.size, 6 * grad.size, grad.size),
        name="gradient",
    )(to, rate, grad.reshape(four), state.reshape(four), after)


def table_kernel(coarse_cos, coarse_sin, fine_cos, fine_sin, out_ref):
    fine = fine_cos.shape[0]
    for j in range(coarse_cos.shape[0]):
        cos, sin = coarse_cos[j : j + 1, :], coarse_sin[j : j + 1, :]
        out_ref[0, j * fine : (j + 1) * fine, :] = (
            cos * fine_cos[...] - sin * fine_sin[...]
        ).astype(jnp.bfloat16)


def wave_table(slots, blocks, lons, fine):
    lon_total = 8 * lons
    quarter = jnp.array([0, lon_total // 4], jnp.int32)[None, :, None]
    phase = jnp.broadcast_to(quarter, (8, 2, slots.shape[1])).reshape(1, -1)
    slot = jnp.broadcast_to(slots[:, None, :], (8, 2, slots.shape[1])).reshape(1, -1)

    def trig(lon, shift):
        index = (slot * lon[:, None] + shift) % lon_total
        angle = index.astype(jnp.float32) * (2.0 * math.pi / lon_total)
        return jnp.cos(angle), jnp.sin(angle)

    starts = blocks[:, None] * lons + fine * jnp.arange(lons // fine, dtype=jnp.int32)[None, :]
    coarse_cos, coarse_sin = trig(starts.reshape(-1), 0)
    fine_cos, fine_sin = trig(jnp.arange(fine, dtype=jnp.int32), phase)
    scale = 1.0 / math.sqrt(lon_total)
    columns = slot.shape[1]
    part = lambda a: pl.BlockSpec((a.shape[0], 256), lambda j: (0, j))
    return pl.pallas_call(
        table_kernel,
        grid=(columns // 256,),
        in_specs=[part(a) for a in (coarse_cos, coarse_sin, fine_cos, fine_sin)],
        out_specs=pl.BlockSpec((1, lon_total, 256), lambda j: (j, 0, 0)),
        out_shape=jax.ShapeDtypeStruct((columns // 256, lon_total, 256), jnp.bfloat16),
        compiler_params=params(12),
        cost_estimate=cost(3 * columns * lon_total, 2 * columns * lon_total),
        name="wave_table",
    )(coarse_cos * scale, coarse_sin * scale, fine_cos, fine_sin)


def fourier_kernel(table_ref, *refs):
    grads, outs, rows = refs[:8], refs[8:16], refs[16]
    lats, lons = grads[0].shape[1], grads[0].shape[2] // 2
    for k in range(8):
        for c in range(4):
            rows[pl.ds(c * lats, lats), pl.ds(k * lons, lons)] = grads[k][
                c // 2, :, pl.ds((c % 2) * lons, lons)
            ]
    width, slots = 4 * lats, outs[0].shape[0]
    for step in range(16 * slots // 256):
        value = jnp.dot(rows[...], table_ref[step], preferred_element_type=jnp.float32).T
        first, stop = 256 * step, 256 * step + 256
        for kp in range(first // slots, -(-stop // slots)):
            low, high = max(first, kp * slots), min(stop, (kp + 1) * slots)
            outs[kp // 2][low - kp * slots : high - kp * slots, pl.ds(kp % 2 * width, width)] = (
                value[low - first : high - first].astype(jnp.bfloat16)
            )


def fourier_rows(table, grads):
    _, lats, lons2 = grads[0].shape
    steps, lon_total, _ = table.shape
    slots = steps * 256 // 16
    return pl.pallas_call(
        fourier_kernel,
        in_specs=[pl.BlockSpec(memory_space=pltpu.VMEM)] * 9,
        out_shape=[jax.ShapeDtypeStruct((slots, 8 * lats), jnp.bfloat16)] * 8,
        scratch_shapes=[pltpu.VMEM((4 * lats, lon_total), jnp.bfloat16)],
        compiler_params=params(24),
        cost_estimate=cost(2 * steps * 256 * lon_total * 4 * lats, 2 * table.size),
        name="fourier_rows",
    )(table, *grads)


def turn_kernel(wave_ref, *refs):
    blocks, (out_ref, rows) = refs[:8], refs[8:]
    slots, width = blocks[0].shape
    for t in range(width // 128):
        lanes = slice(128 * t, 128 * t + 128)
        for k in range(8):
            start = pl.multiple_of(wave_ref[k] * slots, 8)
            rows[t, pl.ds(start, slots), :] = blocks[k][:, lanes].astype(jnp.float32)
        for s in range(slots):
            b, lev, r = s // 16, s // 8 % 2, s % 8
            out_ref[2 * r + lev, b, :, lanes] = rows[t, pl.ds(s, 8, stride=slots), :].astype(
                jnp.bfloat16
            )


def turn(waves, blocks):
    slots, width = blocks[0].shape
    vmem = pl.BlockSpec(memory_space=pltpu.VMEM)
    return pl.pallas_call(
        turn_kernel,
        in_specs=[pl.BlockSpec(memory_space=pltpu.SMEM)] + [vmem] * 8,
        out_shape=jax.ShapeDtypeStruct((16, slots // 16, 8, width), jnp.bfloat16),
        scratch_shapes=[pltpu.VMEM((width // 128, 9 * slots, 128), jnp.float32)],
        compiler_params=params(12),
        cost_estimate=cost(0, 32 * blocks[0].size),
        name="turn",
    )(waves, *blocks)


def spectral_kernel(slot_ref, four_ref, head_ref, basis_any, out_ref, basis, left, total, sems):
    steps, _, lats, degs = basis.shape
    deg_dev = degs // 16
    head = head_ref.shape[1]
    halves = (pl.ds(0, 4), pl.ds(4, 4))
    copies = [
        [
            pltpu.make_async_copy(basis_any.at[part, b], basis.at[b, part], sems.at[b, i])
            for i, part in enumerate(halves)
        ]
        for b in range(head, steps)
    ]
    for copy in sum(copies, []):
        copy.start()

    def summed(b):
        for q in range(8):
            for lev in range(2):
                block = four_ref[2 * q + lev, b].astype(jnp.float32)
                for seg in range(8):
                    left[pl.ds(64 * lev + 8 * seg, 8), pl.ds(q * lats, lats)] = block[
                        :, seg * lats : (seg + 1) * lats
                    ]
        if b >= head:
            for copy in copies[b - head]:
                copy.wait()
            blocks = basis[b]
        else:
            blocks = head_ref[:, b]
        value = jnp.dot(
            left[...].astype(jnp.bfloat16),
            blocks.reshape(8 * lats, degs),
            preferred_element_type=jnp.float32,
        )
        degree = lax.broadcasted_iota(jnp.int32, value.shape, 1)
        return jnp.where(degree >= slot_ref[b], value, 0.0)

    for k in range(2):
        even, odd = summed(2 * k), summed(2 * k + 1)
        for lev in range(2):
            rows = slice(64 * lev, 64 * lev + 64)
            both = jnp.concatenate([even[rows], odd[rows]], 0).T
            for a in range(16):
                out_ref[2 * a + lev, pl.ds(k * deg_dev, deg_dev)] = both[
                    a * deg_dev : (a + 1) * deg_dev
                ].astype(jnp.bfloat16)
    total[pl.ds(0, degs), :] = summed(4).T
    half = deg_dev // 2
    even = total[pl.ds(0, degs // 2, stride=2), :]
    odd = total[pl.ds(1, degs // 2, stride=2), :]
    low = lax.broadcasted_iota(jnp.int32, even.shape, 1) < 64
    pair = (
        jnp.where(low, even, pltpu.roll(odd, 64, 1)),
        jnp.where(low, pltpu.roll(even, 64, 1), odd),
    )
    for a in range(16):
        for lev in range(2):
            out_ref[2 * a + lev, pl.ds(2 * deg_dev, half)] = pair[lev][
                a * half : (a + 1) * half
            ].astype(jnp.bfloat16)
    rows = 5 * half
    for a in range(32):
        out_ref[a, pl.ds(rows, out_ref.shape[1] - rows)] = jnp.zeros(
            (out_ref.shape[1] - rows, 128), jnp.bfloat16
        )


def spectral_parts(slots, fourier, head, basis):
    _, steps, lats, degs = basis.shape
    vmem, smem = pl.BlockSpec(memory_space=pltpu.VMEM), pl.BlockSpec(memory_space=pltpu.SMEM)
    return pl.pallas_call(
        spectral_kernel,
        in_specs=[smem, vmem, vmem, pl.BlockSpec(memory_space=pl.ANY)],
        out_shape=jax.ShapeDtypeStruct((32, 104, 128), jnp.bfloat16),
        scratch_shapes=[
            pltpu.VMEM((steps, 8, lats, degs), jnp.bfloat16),
            pltpu.VMEM((128, 8 * lats), jnp.float32),
            pltpu.VMEM((degs + 8, 128), jnp.float32),
            pltpu.SemaphoreType.DMA((steps, 2)),
        ],
        compiler_params=params(16),
        cost_estimate=cost(5 * 2 * 128 * 8 * lats * degs, 2 * basis.size + 2 * fourier.size),
        name="spectral_parts",
    )(slots, fourier, head, basis)


def finish_kernel(in_ref, out_hbm, rows, out_ref, sems):
    depth = in_ref.shape[1]
    for x in range(4):
        for zq in range(2):
            for lev in range(2):
                first = in_ref[8 * x + 2 * zq + lev].astype(jnp.float32)
                second = in_ref[8 * x + 4 + 2 * zq + lev].astype(jnp.float32)
                rows[pl.ds((8 * lev + 2 * x + zq) * depth, depth), :] = first + second
    low = lax.broadcasted_iota(jnp.int32, (16, 128), 1) < 64
    copies = []
    for n in range(0, 40, 2):
        parts = []
        for k in range(2):
            one = rows[pl.ds(40 * k + n, 16, stride=depth), :]
            two = rows[pl.ds(40 * k + n + 1, 16, stride=depth), :]
            parts.append(jnp.where(low, one, pltpu.roll(two, 64, 1)))
            parts.append(jnp.where(low, pltpu.roll(one, 64, 1), two))
        parts.append(rows[pl.ds(80 + n // 2, 16, stride=depth), :])
        out_ref[pl.ds(64 * n, 128), :] = jnp.concatenate(parts, 0).T
        if n % 10 == 8:
            piece = pl.ds(64 * (n - 8), 640)
            copies.append(
                pltpu.make_async_copy(out_ref.at[piece], out_hbm.at[piece], sems.at[n // 10])
            )
            copies[-1].start()
    for copy in copies:
        copy.wait()


def finish(received):
    return pl.pallas_call(
        finish_kernel,
        in_specs=[pl.BlockSpec(memory_space=pltpu.VMEM)],
        out_specs=pl.BlockSpec(memory_space=pltpu.HBM),
        out_shape=jax.ShapeDtypeStruct((40 * 64, 80), jnp.float32),
        scratch_shapes=[
            pltpu.VMEM((17 * received.shape[1], 128), jnp.float32),
            pltpu.VMEM((40 * 64, 80), jnp.float32),
            pltpu.SemaphoreType.DMA((4,)),
        ],
        compiler_params=params(12),
        cost_estimate=cost(received.size, 2 * received.size + 4 * 40 * 64 * 128),
        name="finish",
    )(received)


def local(out_grad, grid_state, tend_rate, legendre_basis, wave_slot):
    lats, lons = out_grad.shape[1:]
    slot_dev, degs = legendre_basis.shape[1:]
    x, zq = lax.axis_index("x"), lax.axis_index("zq")
    wave, lev = lax.axis_index("wave"), lax.axis_index("lev")

    to, source = (
        wave ^ jnp.where(wave % 2 == 0, *(jnp.array(row, jnp.int32) for row in table))
        for table in (TO, FROM)
    )

    def swapped(blocks):
        return [blocks[0]] + [
            lax.ppermute(blocks[k], "wave", [(w, w ^ TO[w % 2][k]) for w in range(8)])
            for k in range(1, 8)
        ]

    basis, token = basis_blocks(lev.astype(jnp.int32)[None], legendre_basis)
    grads = gradient(to, tend_rate, out_grad, grid_state, token)
    basis = lax.all_to_all(basis, ("x", "zq"), 0, 0, tiled=True)
    grads = swapped(grads)
    slots, grads[1] = lax.optimization_barrier((wave_slot.reshape(8, slot_dev)[to], grads[1]))
    table = wave_table(slots, source, lons, 64)
    blocks = swapped(fourier_rows(table, grads))
    fourier, basis = lax.optimization_barrier((turn(source, blocks), basis))
    fourier = lax.all_to_all(fourier, ("x", "zq", "lev"), 0, 0, tiled=True)

    first = wave * slot_dev + 8 * lev + 2 * x + zq
    slots = jnp.take(wave_slot, first + 16 * jnp.arange(slot_dev // 16, dtype=jnp.int32))
    parts = spectral_parts(slots, fourier, basis[:, :3], basis)
    parts = lax.all_to_all(parts, ("x", "zp", "zq", "lev"), 0, 0, tiled=True)
    return finish(parts).reshape(degs // 16, 2, 32, slot_dev)


def solution(mesh):
    fine = Mesh(
        mesh.devices.reshape(4, 2, 2, *mesh.devices.shape[1:]), ("x", "zp", "zq", "wave", "lev")
    )
    lat = ("x", "zp", "zq")
    in_specs = (P("lev", lat, "wave"), P("lev", lat, "wave"), P("lev"), P(lat, "wave", None), P())
    out_specs = P(lat, None, "lev", "wave")
    return jax.shard_map(local, mesh=fine, in_specs=in_specs, out_specs=out_specs, check_vma=False)
```

```python
import math

import jax
import jax.numpy as jnp
from jax import lax
from jax.experimental import pallas as pl
from jax.experimental.pallas import tpu as pltpu
from jax.sharding import Mesh, PartitionSpec as P

TO = ((0, 1, 2, 6, 4, 3, 7, 5), (0, 1, 6, 2, 4, 7, 3, 5))
FROM = ((0, 1, 2, 6, 4, 7, 3, 5), (0, 1, 6, 2, 4, 3, 7, 5))


def params(mib):
    return pltpu.CompilerParams(vmem_limit_bytes=mib * 1024 * 1024)


def cost(flops, moved, trans=0):
    return pl.CostEstimate(flops=flops, bytes_accessed=moved, transcendentals=trans)


def basis_kernel(lev_ref, basis_hbm, out_hbm, token_ref, in_buf, out_buf, in_sems, out_sems):
    steps, lats, _, degs = in_buf.shape
    lev = lev_ref[0]
    reads = [
        pltpu.make_async_copy(basis_hbm.at[:, 2 * b + lev], in_buf.at[b], in_sems.at[b])
        for b in range(steps)
    ]
    for read in reads:
        read.start()
    row = lax.broadcasted_iota(jnp.int32, (128, 128), 0)
    col = lax.broadcasted_iota(jnp.int32, (128, 128), 1)
    swap = (col == row % 16 * 8 + row // 16).astype(jnp.bfloat16)
    token_ref[...] = jnp.zeros_like(token_ref)
    writes = []
    for b in range(steps):
        reads[b].wait()
        lanes = 384
        for g in range(lats // 16):
            part = slice(16 * g, 16 * g + 16)
            block = in_buf[b, part, :, :lanes].astype(jnp.float32).reshape(128, lanes)
            turned = jnp.dot(swap, block.astype(jnp.bfloat16), preferred_element_type=jnp.float32)
            out_buf[b, :, part, :lanes] = turned.astype(jnp.bfloat16).reshape(8, 16, lanes)
            other = jnp.swapaxes(in_buf[b, part, :, lanes:].astype(jnp.float32), 0, 1)
            out_buf[b, :, part, lanes:] = other.astype(jnp.bfloat16)
        writes.append(pltpu.make_async_copy(out_buf.at[b], out_hbm.at[:, b], out_sems.at[b]))
        writes[b].start()
    for write in writes:
        write.wait()


def basis_blocks(lev, basis):
    lats, slots, degs = basis.shape
    steps = slots // 16
    hbm = pl.BlockSpec(memory_space=pltpu.HBM)
    return pl.pallas_call(
        basis_kernel,
        in_specs=[pl.BlockSpec(memory_space=pltpu.SMEM), hbm],
        out_specs=[hbm, pl.BlockSpec(memory_space=pltpu.VMEM)],
        out_shape=[
            jax.ShapeDtypeStruct((8, steps, lats, degs), jnp.bfloat16),
            jax.ShapeDtypeStruct((8, 128), jnp.float32),
        ],
        scratch_shapes=[
            pltpu.VMEM((steps, lats, 8, degs), jnp.bfloat16),
            pltpu.VMEM((steps, 8, lats, degs), jnp.bfloat16),
            pltpu.SemaphoreType.DMA((steps,)),
            pltpu.SemaphoreType.DMA((steps,)),
        ],
        compiler_params=params(63),
        cost_estimate=cost(0, 2 * lats * slots * degs),
        name="basis_blocks",
    )(lev, basis.reshape(lats, slots // 8, 8, degs))


def grad_kernel(wave_ref, rate_ref, grad_ref, state_ref, _, *outs):
    lons = grad_ref.shape[-1]
    for k in range(8):
        to = wave_ref[k]
        for c in range(4):
            slope = 1.0 - jnp.tanh(state_ref[c, to].astype(jnp.float32)) ** 2
            value = grad_ref[c, to].astype(jnp.float32) * (1.0 + rate_ref[8 * c + to] * slope)
            outs[k][c // 2, :, pl.ds((c % 2) * lons, lons)] = value.astype(jnp.bfloat16)


def gradient(to, rate, grad, state, after):
    chans, lats, lons = grad.shape
    four = (4, chans // 4, lats, lons)
    smem, vmem = pl.BlockSpec(memory_space=pltpu.SMEM), pl.BlockSpec(memory_space=pltpu.VMEM)
    return pl.pallas_call(
        grad_kernel,
        in_specs=[smem, smem, vmem, vmem, vmem],
        out_shape=[jax.ShapeDtypeStruct((2, lats, 2 * lons), jnp.bfloat16)] * 8,
        compiler_params=params(16),
        cost_estimate=cost(6 * grad.size, 6 * grad.size, grad.size),
        name="gradient",
    )(to, rate, grad.reshape(four), state.reshape(four), after)


def table_kernel(coarse_cos, coarse_sin, fine_cos, fine_sin, out_ref):
    fine = fine_cos.shape[0]
    for j in range(coarse_cos.shape[0]):
        cos, sin = coarse_cos[j : j + 1, :], coarse_sin[j : j + 1, :]
        out_ref[0, j * fine : (j + 1) * fine, :] = (
            cos * fine_cos[...] - sin * fine_sin[...]
        ).astype(jnp.bfloat16)


def wave_table(slots, blocks, lons, fine):
    lon_total = 8 * lons
    quarter = jnp.array([0, lon_total // 4], jnp.int32)[None, :, None]
    phase = jnp.broadcast_to(quarter, (8, 2, slots.shape[1])).reshape(1, -1)
    slot = jnp.broadcast_to(slots[:, None, :], (8, 2, slots.shape[1])).reshape(1, -1)

    def trig(lon, shift):
        index = (slot * lon[:, None] + shift) % lon_total
        angle = index.astype(jnp.float32) * (2.0 * math.pi / lon_total)
        return jnp.cos(angle), jnp.sin(angle)

    starts = blocks[:, None] * lons + fine * jnp.arange(lons // fine, dtype=jnp.int32)[None, :]
    coarse_cos, coarse_sin = trig(starts.reshape(-1), 0)
    fine_cos, fine_sin = trig(jnp.arange(fine, dtype=jnp.int32), phase)
    scale = 1.0 / math.sqrt(lon_total)
    columns = slot.shape[1]
    part = lambda a: pl.BlockSpec((a.shape[0], 256), lambda j: (0, j))
    return pl.pallas_call(
        table_kernel,
        grid=(columns // 256,),
        in_specs=[part(a) for a in (coarse_cos, coarse_sin, fine_cos, fine_sin)],
        out_specs=pl.BlockSpec((1, lon_total, 256), lambda j: (j, 0, 0)),
        out_shape=jax.ShapeDtypeStruct((columns // 256, lon_total, 256), jnp.bfloat16),
        compiler_params=params(12),
        cost_estimate=cost(3 * columns * lon_total, 2 * columns * lon_total),
        name="wave_table",
    )(coarse_cos * scale, coarse_sin * scale, fine_cos, fine_sin)


def fourier_kernel(table_ref, *refs):
    grads, outs, rows = refs[:8], refs[8:16], refs[16]
    lats, lons = grads[0].shape[1], grads[0].shape[2] // 2
    for k in range(8):
        for c in range(4):
            rows[pl.ds(c * lats, lats), pl.ds(k * lons, lons)] = grads[k][
                c // 2, :, pl.ds((c % 2) * lons, lons)
            ]
    width, slots = 4 * lats, outs[0].shape[0]
    for step in range(16 * slots // 256):
        value = jnp.dot(rows[...], table_ref[step], preferred_element_type=jnp.float32).T
        first, stop = 256 * step, 256 * step + 256
        for kp in range(first // slots, -(-stop // slots)):
            low, high = max(first, kp * slots), min(stop, (kp + 1) * slots)
            outs[kp // 2][low - kp * slots : high - kp * slots, pl.ds(kp % 2 * width, width)] = (
                value[low - first : high - first].astype(jnp.bfloat16)
            )


def fourier_rows(table, grads):
    _, lats, lons2 = grads[0].shape
    steps, lon_total, _ = table.shape
    slots = steps * 256 // 16
    return pl.pallas_call(
        fourier_kernel,
        in_specs=[pl.BlockSpec(memory_space=pltpu.VMEM)] * 9,
        out_shape=[jax.ShapeDtypeStruct((slots, 8 * lats), jnp.bfloat16)] * 8,
        scratch_shapes=[pltpu.VMEM((4 * lats, lon_total), jnp.bfloat16)],
        compiler_params=params(24),
        cost_estimate=cost(2 * steps * 256 * lon_total * 4 * lats, 2 * table.size),
        name="fourier_rows",
    )(table, *grads)


def turn_kernel(wave_ref, *refs):
    blocks, (out_ref, rows) = refs[:8], refs[8:]
    slots, width = blocks[0].shape
    for t in range(width // 128):
        lanes = slice(128 * t, 128 * t + 128)
        for k in range(8):
            start = pl.multiple_of(wave_ref[k] * slots, 8)
            rows[t, pl.ds(start, slots), :] = blocks[k][:, lanes].astype(jnp.float32)
        for s in range(slots):
            b, lev, r = s // 16, s // 8 % 2, s % 8
            out_ref[2 * r + lev, b, :, lanes] = rows[t, pl.ds(s, 8, stride=slots), :].astype(
                jnp.bfloat16
            )


def turn(waves, blocks):
    slots, width = blocks[0].shape
    vmem = pl.BlockSpec(memory_space=pltpu.VMEM)
    return pl.pallas_call(
        turn_kernel,
        in_specs=[pl.BlockSpec(memory_space=pltpu.SMEM)] + [vmem] * 8,
        out_shape=jax.ShapeDtypeStruct((16, slots // 16, 8, width), jnp.bfloat16),
        scratch_shapes=[pltpu.VMEM((width // 128, 9 * slots, 128), jnp.float32)],
        compiler_params=params(12),
        cost_estimate=cost(0, 32 * blocks[0].size),
        name="turn",
    )(waves, *blocks)


def spectral_kernel(slot_ref, four_ref, head_ref, basis_any, out_ref, basis, left, total, sems):
    steps, _, lats, degs = basis.shape
    deg_dev = degs // 16
    head = head_ref.shape[1]
    halves = (pl.ds(0, 4), pl.ds(4, 4))
    copies = [
        [
            pltpu.make_async_copy(basis_any.at[part, b], basis.at[b, part], sems.at[b, i])
            for i, part in enumerate(halves)
        ]
        for b in range(head, steps)
    ]
    for copy in sum(copies, []):
        copy.start()

    def summed(b):
        for q in range(8):
            for lev in range(2):
                block = four_ref[2 * q + lev, b].astype(jnp.float32)
                for seg in range(0, 8, 2):
                    pair = [block[:, i * lats : (i + 1) * lats] for i in (seg, seg + 1)]
                    left[pl.ds(64 * lev + 8 * seg, 16), pl.ds(q * lats, lats)] = jnp.concatenate(
                        pair, 0
                    ).astype(jnp.bfloat16)
        if b >= head:
            for copy in copies[b - head]:
                copy.wait()
            blocks = basis[b]
        else:
            blocks = head_ref[:, b]
        value = jnp.dot(
            left[...],
            blocks.reshape(8 * lats, degs),
            preferred_element_type=jnp.float32,
        )
        degree = lax.broadcasted_iota(jnp.int32, value.shape, 1)
        return jnp.where(degree >= slot_ref[b], value, 0.0)

    for k in range(2):
        even, odd = summed(2 * k), summed(2 * k + 1)
        for lev in range(2):
            rows = slice(64 * lev, 64 * lev + 64)
            both = jnp.concatenate([even[rows], odd[rows]], 0).T
            for a in range(16):
                out_ref[2 * a + lev, pl.ds(k * deg_dev, deg_dev)] = both[
                    a * deg_dev : (a + 1) * deg_dev
                ].astype(jnp.bfloat16)
    total[pl.ds(0, degs), :] = summed(4).T
    half = deg_dev // 2
    even = total[pl.ds(0, degs // 2, stride=2), :]
    odd = total[pl.ds(1, degs // 2, stride=2), :]
    low = lax.broadcasted_iota(jnp.int32, even.shape, 1) < 64
    pair = (
        jnp.where(low, even, pltpu.roll(odd, 64, 1)),
        jnp.where(low, pltpu.roll(even, 64, 1), odd),
    )
    for a in range(16):
        for lev in range(2):
            out_ref[2 * a + lev, pl.ds(2 * deg_dev, half)] = pair[lev][
                a * half : (a + 1) * half
            ].astype(jnp.bfloat16)
    rows = 5 * half
    for a in range(32):
        out_ref[a, pl.ds(rows, out_ref.shape[1] - rows)] = jnp.zeros(
            (out_ref.shape[1] - rows, 128), jnp.bfloat16
        )


def spectral_parts(slots, fourier, head, basis):
    _, steps, lats, degs = basis.shape
    vmem, smem = pl.BlockSpec(memory_space=pltpu.VMEM), pl.BlockSpec(memory_space=pltpu.SMEM)
    return pl.pallas_call(
        spectral_kernel,
        in_specs=[smem, vmem, vmem, pl.BlockSpec(memory_space=pl.ANY)],
        out_shape=jax.ShapeDtypeStruct((32, 104, 128), jnp.bfloat16),
        scratch_shapes=[
            pltpu.VMEM((steps, 8, lats, degs), jnp.bfloat16),
            pltpu.VMEM((128, 8 * lats), jnp.bfloat16),
            pltpu.VMEM((degs + 8, 128), jnp.float32),
            pltpu.SemaphoreType.DMA((steps, 2)),
        ],
        compiler_params=params(16),
        cost_estimate=cost(5 * 2 * 128 * 8 * lats * degs, 2 * basis.size + 2 * fourier.size),
        name="spectral_parts",
    )(slots, fourier, head, basis)


def finish_kernel(in_ref, out_hbm, rows, out_ref, sems):
    depth = in_ref.shape[1]
    step = depth + 1
    for x in range(4):
        for zq in range(2):
            for lev in range(2):
                first = in_ref[8 * x + 2 * zq + lev].astype(jnp.float32)
                second = in_ref[8 * x + 4 + 2 * zq + lev].astype(jnp.float32)
                rows[pl.ds((8 * lev + 2 * x + zq) * step, depth), :] = first + second
    low = lax.broadcasted_iota(jnp.int32, (16, 128), 1) < 64
    copies = []
    for n in range(0, 40, 2):
        parts = []
        for k in range(2):
            one = rows[pl.ds(40 * k + n, 16, stride=step), :]
            two = rows[pl.ds(40 * k + n + 1, 16, stride=step), :]
            parts.append(jnp.where(low, one, pltpu.roll(two, 64, 1)))
            parts.append(jnp.where(low, pltpu.roll(one, 64, 1), two))
        parts.append(rows[pl.ds(80 + n // 2, 16, stride=step), :])
        out_ref[pl.ds(64 * n, 128), :] = jnp.concatenate(parts, 0).T
        if n % 10 == 8:
            piece = pl.ds(64 * (n - 8), 640)
            copies.append(
                pltpu.make_async_copy(out_ref.at[piece], out_hbm.at[piece], sems.at[n // 10])
            )
            copies[-1].start()
    for copy in copies:
        copy.wait()


def finish(received):
    return pl.pallas_call(
        finish_kernel,
        in_specs=[pl.BlockSpec(memory_space=pltpu.VMEM)],
        out_specs=pl.BlockSpec(memory_space=pltpu.HBM),
        out_shape=jax.ShapeDtypeStruct((40 * 64, 80), jnp.float32),
        scratch_shapes=[
            pltpu.VMEM((17 * received.shape[1] + 24, 128), jnp.float32),
            pltpu.VMEM((40 * 64, 80), jnp.float32),
            pltpu.SemaphoreType.DMA((4,)),
        ],
        compiler_params=params(12),
        cost_estimate=cost(received.size, 2 * received.size + 4 * 40 * 64 * 128),
        name="finish",
    )(received)


def local(out_grad, grid_state, tend_rate, legendre_basis, wave_slot):
    lats, lons = out_grad.shape[1:]
    slot_dev, degs = legendre_basis.shape[1:]
    x, zq = lax.axis_index("x"), lax.axis_index("zq")
    wave, lev = lax.axis_index("wave"), lax.axis_index("lev")

    to, source = (
        wave ^ jnp.where(wave % 2 == 0, *(jnp.array(row, jnp.int32) for row in table))
        for table in (TO, FROM)
    )

    def swapped(blocks):
        return [blocks[0]] + [
            lax.ppermute(blocks[k], "wave", [(w, w ^ TO[w % 2][k]) for w in range(8)])
            for k in range(1, 8)
        ]

    basis, token = basis_blocks(lev.astype(jnp.int32)[None], legendre_basis)
    grads = gradient(to, tend_rate, out_grad, grid_state, token)
    basis = lax.all_to_all(basis, ("x", "zq"), 0, 0, tiled=True)
    grads = swapped(grads)
    slots, grads[1] = lax.optimization_barrier((wave_slot.reshape(8, slot_dev)[to], grads[1]))
    table = wave_table(slots, source, lons, 64)
    blocks = swapped(fourier_rows(table, grads))
    fourier, basis = lax.optimization_barrier((turn(source, blocks), basis))
    fourier = lax.all_to_all(fourier, ("x", "zq", "lev"), 0, 0, tiled=True)

    first = wave * slot_dev + 8 * lev + 2 * x + zq
    slots = jnp.take(wave_slot, first + 16 * jnp.arange(slot_dev // 16, dtype=jnp.int32))
    parts = spectral_parts(slots, fourier, basis[:, :3], basis)
    parts = lax.all_to_all(parts, ("x", "zp", "zq", "lev"), 0, 0, tiled=True)
    return finish(parts).reshape(degs // 16, 2, 32, slot_dev)


def solution(mesh):
    fine = Mesh(
        mesh.devices.reshape(4, 2, 2, *mesh.devices.shape[1:]), ("x", "zp", "zq", "wave", "lev")
    )
    lat = ("x", "zp", "zq")
    in_specs = (P("lev", lat, "wave"), P("lev", lat, "wave"), P("lev"), P(lat, "wave", None), P())
    out_specs = P(lat, None, "lev", "wave")
    return jax.shard_map(local, mesh=fine, in_specs=in_specs, out_specs=out_specs, check_vma=False)
```

```python
import math

import jax
import jax.numpy as jnp
from jax import lax
from jax.experimental import pallas as pl
from jax.experimental.pallas import tpu as pltpu
from jax.sharding import Mesh, PartitionSpec as P

TO = ((0, 1, 2, 6, 4, 3, 7, 5), (0, 1, 6, 2, 4, 7, 3, 5))
FROM = ((0, 1, 2, 6, 4, 7, 3, 5), (0, 1, 6, 2, 4, 3, 7, 5))


def params(mib):
    return pltpu.CompilerParams(vmem_limit_bytes=mib * 1024 * 1024)


def cost(flops, moved, trans=0):
    return pl.CostEstimate(flops=flops, bytes_accessed=moved, transcendentals=trans)


def basis_kernel(lev_ref, basis_hbm, out_hbm, token_ref, in_buf, out_buf, in_sems, out_sems):
    steps, lats, _, degs = in_buf.shape
    lev = lev_ref[0]
    reads = [
        pltpu.make_async_copy(basis_hbm.at[:, 2 * b + lev], in_buf.at[b], in_sems.at[b])
        for b in range(steps)
    ]
    for read in reads:
        read.start()
    row = lax.broadcasted_iota(jnp.int32, (128, 128), 0)
    col = lax.broadcasted_iota(jnp.int32, (128, 128), 1)
    swap = (col == row % 16 * 8 + row // 16).astype(jnp.bfloat16)
    token_ref[...] = jnp.zeros_like(token_ref)
    writes = []
    for b in range(steps):
        reads[b].wait()
        lanes = 384
        for g in range(lats // 16):
            part = slice(16 * g, 16 * g + 16)
            block = in_buf[b, part, :, :lanes].astype(jnp.float32).reshape(128, lanes)
            turned = jnp.dot(swap, block.astype(jnp.bfloat16), preferred_element_type=jnp.float32)
            out_buf[b, :, part, :lanes] = turned.astype(jnp.bfloat16).reshape(8, 16, lanes)
            other = jnp.swapaxes(in_buf[b, part, :, lanes:].astype(jnp.float32), 0, 1)
            out_buf[b, :, part, lanes:] = other.astype(jnp.bfloat16)
        writes.append(pltpu.make_async_copy(out_buf.at[b], out_hbm.at[:, b], out_sems.at[b]))
        writes[b].start()
    for write in writes:
        write.wait()


def basis_blocks(lev, basis):
    lats, slots, degs = basis.shape
    steps = slots // 16
    hbm = pl.BlockSpec(memory_space=pltpu.HBM)
    return pl.pallas_call(
        basis_kernel,
        in_specs=[pl.BlockSpec(memory_space=pltpu.SMEM), hbm],
        out_specs=[hbm, pl.BlockSpec(memory_space=pltpu.VMEM)],
        out_shape=[
            jax.ShapeDtypeStruct((8, steps, lats, degs), jnp.bfloat16),
            jax.ShapeDtypeStruct((8, 128), jnp.float32),
        ],
        scratch_shapes=[
            pltpu.VMEM((steps, lats, 8, degs), jnp.bfloat16),
            pltpu.VMEM((steps, 8, lats, degs), jnp.bfloat16),
            pltpu.SemaphoreType.DMA((steps,)),
            pltpu.SemaphoreType.DMA((steps,)),
        ],
        compiler_params=params(63),
        cost_estimate=cost(0, 2 * lats * slots * degs),
        name="basis_blocks",
    )(lev, basis.reshape(lats, slots // 8, 8, degs))


def grad_kernel(wave_ref, rate_ref, grad_ref, state_ref, _, *outs):
    lons = grad_ref.shape[-1]
    for k in range(8):
        to = wave_ref[k]
        for c in range(4):
            slope = 1.0 - jnp.tanh(state_ref[c, to].astype(jnp.float32)) ** 2
            value = grad_ref[c, to].astype(jnp.float32) * (1.0 + rate_ref[8 * c + to] * slope)
            outs[k][c // 2, :, pl.ds((c % 2) * lons, lons)] = value.astype(jnp.bfloat16)


def gradient(to, rate, grad, state, after):
    chans, lats, lons = grad.shape
    four = (4, chans // 4, lats, lons)
    smem, vmem = pl.BlockSpec(memory_space=pltpu.SMEM), pl.BlockSpec(memory_space=pltpu.VMEM)
    return pl.pallas_call(
        grad_kernel,
        in_specs=[smem, smem, vmem, vmem, vmem],
        out_shape=[jax.ShapeDtypeStruct((2, lats, 2 * lons), jnp.bfloat16)] * 8,
        compiler_params=params(16),
        cost_estimate=cost(6 * grad.size, 6 * grad.size, grad.size),
        name="gradient",
    )(to, rate, grad.reshape(four), state.reshape(four), after)


def table_kernel(coarse_cos, coarse_sin, fine_cos, fine_sin, out_ref):
    fine = fine_cos.shape[0]
    for j in range(coarse_cos.shape[0]):
        cos, sin = coarse_cos[j : j + 1, :], coarse_sin[j : j + 1, :]
        out_ref[0, j * fine : (j + 1) * fine, :] = (
            cos * fine_cos[...] - sin * fine_sin[...]
        ).astype(jnp.bfloat16)


def wave_table(slots, blocks, lons, fine):
    lon_total = 8 * lons
    quarter = jnp.array([0, lon_total // 4], jnp.int32)[None, :, None]
    phase = jnp.broadcast_to(quarter, (8, 2, slots.shape[1])).reshape(1, -1)
    slot = jnp.broadcast_to(slots[:, None, :], (8, 2, slots.shape[1])).reshape(1, -1)

    def trig(lon, shift):
        index = (slot * lon[:, None] + shift) % lon_total
        angle = index.astype(jnp.float32) * (2.0 * math.pi / lon_total)
        return jnp.cos(angle), jnp.sin(angle)

    starts = blocks[:, None] * lons + fine * jnp.arange(lons // fine, dtype=jnp.int32)[None, :]
    coarse_cos, coarse_sin = trig(starts.reshape(-1), 0)
    fine_cos, fine_sin = trig(jnp.arange(fine, dtype=jnp.int32), phase)
    scale = 1.0 / math.sqrt(lon_total)
    columns = slot.shape[1]
    part = lambda a: pl.BlockSpec((a.shape[0], 256), lambda j: (0, j))
    return pl.pallas_call(
        table_kernel,
        grid=(columns // 256,),
        in_specs=[part(a) for a in (coarse_cos, coarse_sin, fine_cos, fine_sin)],
        out_specs=pl.BlockSpec((1, lon_total, 256), lambda j: (j, 0, 0)),
        out_shape=jax.ShapeDtypeStruct((columns // 256, lon_total, 256), jnp.bfloat16),
        compiler_params=params(12),
        cost_estimate=cost(3 * columns * lon_total, 2 * columns * lon_total),
        name="wave_table",
    )(coarse_cos * scale, coarse_sin * scale, fine_cos, fine_sin)


def fourier_kernel(table_ref, *refs):
    grads, outs, rows = refs[:8], refs[8:16], refs[16]
    lats, lons = grads[0].shape[1], grads[0].shape[2] // 2
    for k in range(8):
        for c in range(4):
            rows[pl.ds(c * lats, lats), pl.ds(k * lons, lons)] = grads[k][
                c // 2, :, pl.ds((c % 2) * lons, lons)
            ]
    width, slots = 4 * lats, outs[0].shape[0]
    for step in range(16 * slots // 256):
        value = jnp.dot(rows[...], table_ref[step], preferred_element_type=jnp.float32).T
        first, stop = 256 * step, 256 * step + 256
        for kp in range(first // slots, -(-stop // slots)):
            low, high = max(first, kp * slots), min(stop, (kp + 1) * slots)
            outs[kp // 2][low - kp * slots : high - kp * slots, pl.ds(kp % 2 * width, width)] = (
                value[low - first : high - first].astype(jnp.bfloat16)
            )


def fourier_rows(table, grads):
    _, lats, lons2 = grads[0].shape
    steps, lon_total, _ = table.shape
    slots = steps * 256 // 16
    return pl.pallas_call(
        fourier_kernel,
        in_specs=[pl.BlockSpec(memory_space=pltpu.VMEM)] * 9,
        out_shape=[jax.ShapeDtypeStruct((slots, 8 * lats), jnp.bfloat16)] * 8,
        scratch_shapes=[pltpu.VMEM((4 * lats, lon_total), jnp.bfloat16)],
        compiler_params=params(24),
        cost_estimate=cost(2 * steps * 256 * lon_total * 4 * lats, 2 * table.size),
        name="fourier_rows",
    )(table, *grads)


def turn_kernel(wave_ref, *refs):
    blocks, (out_ref, rows) = refs[:8], refs[8:]
    slots, width = blocks[0].shape
    for t in range(width // 128):
        lanes = slice(128 * t, 128 * t + 128)
        for k in range(8):
            start = pl.multiple_of(wave_ref[k] * slots, 8)
            rows[t, pl.ds(start, slots), :] = blocks[k][:, lanes].astype(jnp.float32)
        for s in range(slots):
            b, lev, r = s // 16, s // 8 % 2, s % 8
            out_ref[2 * r + lev, b, :, lanes] = rows[t, pl.ds(s, 8, stride=slots), :].astype(
                jnp.bfloat16
            )


def turn(waves, blocks):
    slots, width = blocks[0].shape
    vmem = pl.BlockSpec(memory_space=pltpu.VMEM)
    return pl.pallas_call(
        turn_kernel,
        in_specs=[pl.BlockSpec(memory_space=pltpu.SMEM)] + [vmem] * 8,
        out_shape=jax.ShapeDtypeStruct((16, slots // 16, 8, width), jnp.bfloat16),
        scratch_shapes=[pltpu.VMEM((width // 128, 9 * slots, 128), jnp.float32)],
        compiler_params=params(12),
        cost_estimate=cost(0, 32 * blocks[0].size),
        name="turn",
    )(waves, *blocks)


def spectral_kernel(slot_ref, four_ref, head_ref, basis_any, out_ref, basis, left, total, sems):
    steps, _, lats, degs = basis.shape
    deg_dev = degs // 16
    head = head_ref.shape[1]
    halves = (pl.ds(0, 4), pl.ds(4, 4))
    copies = [
        [
            pltpu.make_async_copy(basis_any.at[part, b], basis.at[b, part], sems.at[b, i])
            for i, part in enumerate(halves)
        ]
        for b in range(head, steps)
    ]
    for copy in sum(copies, []):
        copy.start()

    def summed(b):
        for q in range(8):
            for lev in range(2):
                block = four_ref[2 * q + lev, b].astype(jnp.float32)
                for seg in range(8):
                    left[b, pl.ds(64 * lev + 8 * seg, 8), pl.ds(q * lats, lats)] = block[
                        :, seg * lats : (seg + 1) * lats
                    ]
        if b >= head:
            for copy in copies[b - head]:
                copy.wait()
            blocks = basis[b]
        else:
            blocks = head_ref[:, b]
        value = jnp.dot(
            left[b].astype(jnp.bfloat16),
            blocks.reshape(8 * lats, degs),
            preferred_element_type=jnp.float32,
        )
        degree = lax.broadcasted_iota(jnp.int32, value.shape, 1)
        return jnp.where(degree >= slot_ref[b], value, 0.0)

    for k in range(2):
        even, odd = summed(2 * k), summed(2 * k + 1)
        for lev in range(2):
            rows = slice(64 * lev, 64 * lev + 64)
            both = jnp.concatenate([even[rows], odd[rows]], 0).T
            for a in range(16):
                out_ref[2 * a + lev, pl.ds(k * deg_dev, deg_dev)] = both[
                    a * deg_dev : (a + 1) * deg_dev
                ].astype(jnp.bfloat16)
    total[pl.ds(0, degs), :] = summed(4).T
    half = deg_dev // 2
    even = total[pl.ds(0, degs // 2, stride=2), :]
    odd = total[pl.ds(1, degs // 2, stride=2), :]
    low = lax.broadcasted_iota(jnp.int32, even.shape, 1) < 64
    pair = (
        jnp.where(low, even, pltpu.roll(odd, 64, 1)),
        jnp.where(low, pltpu.roll(even, 64, 1), odd),
    )
    for a in range(16):
        for lev in range(2):
            out_ref[2 * a + lev, pl.ds(2 * deg_dev, half)] = pair[lev][
                a * half : (a + 1) * half
            ].astype(jnp.bfloat16)
    rows = 5 * half
    for a in range(32):
        out_ref[a, pl.ds(rows, out_ref.shape[1] - rows)] = jnp.zeros(
            (out_ref.shape[1] - rows, 128), jnp.bfloat16
        )


def spectral_parts(slots, fourier, head, basis):
    _, steps, lats, degs = basis.shape
    vmem, smem = pl.BlockSpec(memory_space=pltpu.VMEM), pl.BlockSpec(memory_space=pltpu.SMEM)
    return pl.pallas_call(
        spectral_kernel,
        in_specs=[smem, vmem, vmem, pl.BlockSpec(memory_space=pl.ANY)],
        out_shape=jax.ShapeDtypeStruct((32, 104, 128), jnp.bfloat16),
        scratch_shapes=[
            pltpu.VMEM((steps, 8, lats, degs), jnp.bfloat16),
            pltpu.VMEM((steps, 128, 8 * lats), jnp.float32),
            pltpu.VMEM((degs + 8, 128), jnp.float32),
            pltpu.SemaphoreType.DMA((steps, 2)),
        ],
        compiler_params=params(16),
        cost_estimate=cost(5 * 2 * 128 * 8 * lats * degs, 2 * basis.size + 2 * fourier.size),
        name="spectral_parts",
    )(slots, fourier, head, basis)


def finish_kernel(in_ref, out_hbm, rows, out_ref, sems):
    depth = in_ref.shape[1]
    for x in range(4):
        for zq in range(2):
            for lev in range(2):
                first = in_ref[8 * x + 2 * zq + lev].astype(jnp.float32)
                second = in_ref[8 * x + 4 + 2 * zq + lev].astype(jnp.float32)
                rows[pl.ds((8 * lev + 2 * x + zq) * depth, depth), :] = first + second
    low = lax.broadcasted_iota(jnp.int32, (16, 128), 1) < 64
    copies = []
    for n in range(0, 40, 2):
        parts = []
        for k in range(2):
            one = rows[pl.ds(40 * k + n, 16, stride=depth), :]
            two = rows[pl.ds(40 * k + n + 1, 16, stride=depth), :]
            parts.append(jnp.where(low, one, pltpu.roll(two, 64, 1)))
            parts.append(jnp.where(low, pltpu.roll(one, 64, 1), two))
        parts.append(rows[pl.ds(80 + n // 2, 16, stride=depth), :])
        out_ref[pl.ds(64 * n, 128), :] = jnp.concatenate(parts, 0).T
        if n % 10 == 8:
            piece = pl.ds(64 * (n - 8), 640)
            copies.append(
                pltpu.make_async_copy(out_ref.at[piece], out_hbm.at[piece], sems.at[n // 10])
            )
            copies[-1].start()
    for copy in copies:
        copy.wait()


def finish(received):
    return pl.pallas_call(
        finish_kernel,
        in_specs=[pl.BlockSpec(memory_space=pltpu.VMEM)],
        out_specs=pl.BlockSpec(memory_space=pltpu.HBM),
        out_shape=jax.ShapeDtypeStruct((40 * 64, 80), jnp.float32),
        scratch_shapes=[
            pltpu.VMEM((17 * received.shape[1], 128), jnp.float32),
            pltpu.VMEM((40 * 64, 80), jnp.float32),
            pltpu.SemaphoreType.DMA((4,)),
        ],
        compiler_params=params(12),
        cost_estimate=cost(received.size, 2 * received.size + 4 * 40 * 64 * 128),
        name="finish",
    )(received)


def local(out_grad, grid_state, tend_rate, legendre_basis, wave_slot):
    lats, lons = out_grad.shape[1:]
    slot_dev, degs = legendre_basis.shape[1:]
    x, zq = lax.axis_index("x"), lax.axis_index("zq")
    wave, lev = lax.axis_index("wave"), lax.axis_index("lev")

    to, source = (
        wave ^ jnp.where(wave % 2 == 0, *(jnp.array(row, jnp.int32) for row in table))
        for table in (TO, FROM)
    )

    def swapped(blocks):
        return [blocks[0]] + [
            lax.ppermute(blocks[k], "wave", [(w, w ^ TO[w % 2][k]) for w in range(8)])
            for k in range(1, 8)
        ]

    basis, token = basis_blocks(lev.astype(jnp.int32)[None], legendre_basis)
    grads = gradient(to, tend_rate, out_grad, grid_state, token)
    basis = lax.all_to_all(basis, ("x", "zq"), 0, 0, tiled=True)
    grads = swapped(grads)
    slots, grads[1] = lax.optimization_barrier((wave_slot.reshape(8, slot_dev)[to], grads[1]))
    table = wave_table(slots, source, lons, 64)
    blocks = swapped(fourier_rows(table, grads))
    fourier, basis = lax.optimization_barrier((turn(source, blocks), basis))
    fourier = lax.all_to_all(fourier, ("x", "zq", "lev"), 0, 0, tiled=True)

    first = wave * slot_dev + 8 * lev + 2 * x + zq
    slots = jnp.take(wave_slot, first + 16 * jnp.arange(slot_dev // 16, dtype=jnp.int32))
    parts = spectral_parts(slots, fourier, basis[:, :3], basis)
    parts = lax.all_to_all(parts, ("x", "zp", "zq", "lev"), 0, 0, tiled=True)
    return finish(parts).reshape(degs // 16, 2, 32, slot_dev)


def solution(mesh):
    fine = Mesh(
        mesh.devices.reshape(4, 2, 2, *mesh.devices.shape[1:]), ("x", "zp", "zq", "wave", "lev")
    )
    lat = ("x", "zp", "zq")
    in_specs = (P("lev", lat, "wave"), P("lev", lat, "wave"), P("lev"), P(lat, "wave", None), P())
    out_specs = P(lat, None, "lev", "wave")
    return jax.shard_map(local, mesh=fine, in_specs=in_specs, out_specs=out_specs, check_vma=False)
```
